256 devices in a mesh: gx: 8 (over y, core), gy: 32 (over x, z).
Axes of the slice: x: 4, y: 4, z: 8, core: 2. Of those that a mesh axis runs over, the one named last changes fastest.
Arguments:
- right_side: float32 [6, 33, 128, 1024], P(None, None, 'gy', 'gx'), may hold values from -12 to 12
- base_flow: float32 [2, 33, 128, 1024], P(None, None, 'gy', 'gx'), may hold values from -4 to 4
- relax: float32 [128, 1024], P('gy', 'gx'), may hold values from 0.4 to 4
Outputs:
- solution_field: float32 [6, 33, 128, 1024], P(None, None, 'gy', 'gx')
- residual: float32 [6, 33, 128, 1024], P(None, None, 'gy', 'gx')
The draws below stay inside these ranges and needn't reach their ends.
All inputs are finite; a program needn't handle non-finite values.
Results may differ from the reference program's by a relative error of at most 0.0044.
Values sent between devices are 32-bit elements; how exact they have to be, the bound alone decides.
No kernel may reach another device: no remote copies, remote signals or barrier semaphores. Data moves between devices by JAX's collectives and lax.ppermute only.
A program may use at most 64 MiB of HBM per device.

```python
import math
import jax
import jax.numpy as jnp
from jax import lax

INST = 33
FIELDS = 6
S = 4
CYCLES = 2
NX = 128
NY = 1024


def draw_right_side(key, part):
    key = jax.random.fold_in(key, 11)
    rows = jnp.arange(NX, dtype=jnp.float32)[:, None] / max(NX - 1, 1)
    cols = jnp.arange(NY, dtype=jnp.float32)[None, :] / max(NY - 1, 1)
    spread = jnp.exp(jnp.log(3.0) * 0.5 * (rows + cols))
    shape = (FIELDS, INST, NX, NY)
    values = jax.random.truncated_normal(key, -4.0, 4.0, shape, jnp.float32)
    return (values * spread).astype(jnp.float32)


def shard_levels(key, extent, pieces, least, high):
    level, own = 1.0, jax.random.fold_in(key, 6)
    for axis_at, parts in pieces:
        steps = jnp.exp(jax.random.uniform(jax.random.fold_in(own, axis_at), (parts,), jnp.float32, least / len(pieces), high / len(pieces)))
        level = level * jnp.repeat(steps, extent[axis_at] // parts).reshape([-1 if axis == axis_at else 1 for axis in range(len(extent))])
    return level


def noise(rng, dims, deviation, limit, shards=(), kind=jnp.bfloat16):
    drawn = deviation * jax.random.normal(rng, dims, jnp.float32)
    if shards:
        drawn = drawn * shard_levels(rng, dims, shards, -0.22, 0.18)
    return jnp.clip(drawn, -limit, limit).astype(kind)


def setup_inputs(seed: int = 0) -> dict:
    key_of = jax.random.split(jax.random.key(seed), 4)
    right_side = draw_right_side(jax.random.fold_in(key_of[3], 71), 0)
    base_flow = noise(key_of[1], (2, INST, NX, NY), 0.7, 4.0, ((2, 32), (3, 8)), jnp.float32)
    relax = jnp.clip(jnp.exp(math.log(4.0) - 2.3025851 * jax.random.uniform(key_of[2], (NX, NY), jnp.float32) ** shard_levels(key_of[2], (NX, NY), ((0, 32), (1, 8)), -0.2, 0.2)), 0.4, 4.0)
    return {"right_side": right_side, "base_flow": base_flow, "relax": relax}


def spectral(count):
    index = jnp.arange(count, dtype=jnp.float32)
    diff = index[:, None] - index[None, :]
    parity = jnp.where(jnp.mod(diff, 2.0) == 0.0, 1.0, -1.0)
    sines = jnp.sin(jnp.pi * diff / count)
    safe = jnp.where(diff == 0.0, 1.0, sines)
    return jnp.where(diff == 0.0, 0.0, 0.5 * parity / safe).astype(jnp.float32)

def apply_op(extended, flow, relax, dmat):
    core = extended[:, :, 1:-1, 1:-1]
    east = extended[:, :, 2:, 1:-1]
    west = extended[:, :, :-2, 1:-1]
    north = extended[:, :, 1:-1, 2:]
    south = extended[:, :, 1:-1, :-2]
    slope_x = 0.5 * (east - west)
    slope_y = 0.5 * (north - south)
    lapl = east + west + north + south - 4.0 * core
    timed = jnp.einsum('st,ftxy->fsxy', dmat, core, precision=lax.Precision.HIGHEST)
    carried = 0.8 * timed + flow[0][None] * slope_x + flow[1][None] * slope_y
    row_u = carried[0] - 0.1 * lapl[0] + slope_x[2] - slope_x[3] - slope_y[4]
    row_v = carried[1] - 0.1 * lapl[1] + slope_y[2] - slope_x[4] - slope_y[5]
    row_p = slope_x[0] + slope_y[1] - 0.2 * lapl[2]
    row_xx = carried[3] + relax * core[3] - 1.0 * slope_x[0]
    row_xy = carried[4] + relax * core[4] - 0.5 * (slope_y[0] + slope_x[1])
    row_yy = carried[5] + relax * core[5] - 1.0 * slope_y[1]
    return jnp.stack([row_u, row_v, row_p, row_xx, row_xy, row_yy]) / 3.0

def substitute(factor, target, count):
    forward = []
    for index_row in range(count):
        total = target[index_row]
        for index_col in range(index_row):
            total = total - factor[index_row, index_col] * forward[index_col]
        forward.append(total / factor[index_row, index_row])
    backward = [None] * count
    for index_row in reversed(range(count)):
        total = forward[index_row]
        for index_col in range(index_row + 1, count):
            total = total - factor[index_col, index_row] * backward[index_col]
        backward[index_row] = total / factor[index_row, index_row]
    return jnp.stack(backward)

def small_solve(gram):
    count = gram.shape[0] - 1
    lead = jnp.arange(count + 1)[:, None]
    cols = jnp.arange(count)[None, :]
    mixer = jnp.where(lead == cols, 2.0, jnp.where(lead == cols + 1, 3.0, 0.0)).astype(jnp.float32)
    high = lax.Precision.HIGHEST
    normal = jnp.dot(mixer.T, jnp.dot(gram, mixer, precision=high), precision=high)
    target = jnp.dot(mixer.T, gram[:, 0], precision=high)
    factor = jnp.linalg.cholesky(normal)
    return substitute(factor, target, count)

def reference(right_side, base_flow, relax):
    dmat = spectral(INST)
    solution_field = jnp.zeros_like(right_side)
    residual = right_side
    widths = ((0, 0), (0, 0), (1, 1), (1, 1))
    for cycle in range(CYCLES):
        basis = [residual]
        for step in range(S):
            basis.append(apply_op(jnp.pad(basis[-1], widths), base_flow, relax, dmat))
        stacked = jnp.stack(basis).reshape(S + 1, -1)
        gram = jnp.einsum('iz,jz->ij', stacked, stacked, precision=lax.Precision.HIGHEST)
        coeffs = small_solve(gram)
        for step in range(S):
            solution_field = solution_field + coeffs[step] * basis[step]
            residual = residual - coeffs[step] * (2.0 * basis[step] + 3.0 * basis[step + 1])
    return (solution_field, residual)
```

```python
import functools

import jax
import jax.numpy as jnp
import numpy as np
from jax import lax
from jax.experimental import pallas as pl
from jax.experimental.pallas import tpu as pltpu
from jax.sharding import PartitionSpec as P

F = 6
T = 33
TP = 40
R = 4
H = 4
E = R + 2 * H
NV = 9
RHO = 4.3
STEP = 2.0 / (3.0 * RHO)
TIMED = (0, 1, 3, 4, 5)
PAIRS = [(i, j) for i in range(NV) for j in range(i, NV)]
PEERS = 256
VM = pl.BlockSpec(memory_space=pltpu.VMEM)


def time_matrices():
    index = np.arange(T, dtype=np.float64)
    diff = index[:, None] - index[None, :]
    sines = np.where(diff == 0.0, 1.0, np.sin(np.pi * diff / T))
    dmat = np.where(diff == 0.0, 0.0, 0.5 * np.where(diff % 2 == 0, 1.0, -1.0) / sines)
    mats = []
    for diagonal in (0.4 * STEP, 0.0):
        full = np.zeros((TP, TP), np.float32)
        full[:T, :T] = 0.8 * STEP * dmat + diagonal * np.eye(T)
        high = full.astype(jnp.bfloat16)
        low = (full - high.astype(np.float32)).astype(jnp.bfloat16)
        top = np.concatenate([high, high], 1)
        bottom = np.concatenate([low, np.zeros_like(low)], 1)
        mats.append(np.concatenate([top, bottom], 0))
    return np.stack(mats)


def lanes(shape=(1, 128)):
    return lax.broadcasted_iota(jnp.int32, shape, len(shape) - 1)


def window(x, place):
    lane = lanes()
    return jnp.where((lane >= place) & (lane < place + 8), pltpu.roll(x, (place + 4) % 128, 1), 0.0)


def raw(ref, f, r):
    return ref[pl.ds(f * T * R + r, T, stride=R), :]


def pack_kernel(rs, flow, relax, main, pack):
    main[0 : F * T * R, :] = rs[...]
    main[F * T * R : 8 * T * R, :] = flow[...]
    main[8 * T * R : 8 * T * R + 8, :] = jnp.concatenate([relax[...], relax[...]], 0)
    for g in range(2):
        total = jnp.zeros((T, 128), jnp.float32)
        for j in range(4):
            f = g * 4 + j
            for r in range(R):
                x = raw(rs, f, r) if f < F else raw(flow, f - F, r)
                total = total + window(x, j * 32 + r * 8)
        pack[g, 0:32, :] = total[0:32]
        last = jnp.zeros((8, 128), jnp.float32)
        sub = lax.broadcasted_iota(jnp.int32, (8, 128), 0)
        last = jnp.where(sub == 0, jnp.broadcast_to(total[32:33], (8, 128)), last)
        if g == 1:
            extra = jnp.zeros((1, 128), jnp.float32)
            for r in range(R):
                extra = extra + window(relax[r : r + 1, :], 2 * 32 + r * 8)
            last = jnp.where(sub == 1, jnp.broadcast_to(extra, (8, 128)), last)
        pack[g, 32:40, :] = last


def put(dst, index, x, scale=None):
    dst[index + (pl.ds(32, 8), slice(None))] = jnp.zeros((8, 128), jnp.float32)
    dst[index + (pl.ds(0, T), slice(None))] = x if scale is None else x * scale


def sides_of(dst, f, own, sides, g, j):
    lane = lanes()
    north, here, south = (
        pltpu.roll(ref[g], (base - 32 * j) % 128, 1) for base, ref in zip((0, 32, 64), sides)
    )
    halo = jnp.where(lane < 32, north, jnp.where(lane < 64, here, jnp.where(lane < 96, south, 0.0)))
    slot = lane % 8
    dst[f, 0] = jnp.where(slot < 4, halo, own)
    dst[f, 1] = jnp.where(slot < 4, own, halo)


def own_windows(slab):
    total = jnp.zeros((TP, 128), jnp.float32)
    for e in range(E):
        total = total + window(slab(e), e * 8)
    return total


def fill(own, north, south, sides, ext, side):
    for f in range(F):
        for r in range(R):
            put(ext, (0, f, r), raw(north, f, r))
            put(ext, (0, f, H + r), raw(own, f, r))
            put(ext, (0, f, H + R + r), raw(south, f, r))
    for f in range(F):
        sides_of(side.at[0], f, own_windows(lambda e: ext[0, f, e]), sides, f // 4, f % 4)


def masks():
    gx, gy = lax.axis_index("gx"), lax.axis_index("gy")
    north = jnp.where(gy > 0, 1.0, 0.0).astype(jnp.float32)
    south = jnp.where(gy < lax.axis_size("gy") - 1, 1.0, 0.0).astype(jnp.float32)
    west = jnp.where(gx > 0, 1.0, 0.0).astype(jnp.float32)
    east = jnp.where(gx < lax.axis_size("gx") - 1, 1.0, 0.0).astype(jnp.float32)
    return north, south, west, east


def combine(core, xm, xp, ym, yp, fu, fv, rl, td):
    ex = [a - b for a, b in zip(xp, xm)]
    ey = [a - b for a, b in zip(yp, ym)]
    half = 0.5 * STEP
    carried = {f: td[f] + fu * ex[f] + fv * ey[f] for f in TIMED}
    around = [xp[f] + xm[f] + (yp[f] + ym[f]) for f in range(3)]
    return [
        carried[0] - (0.1 * STEP) * around[0] + half * (ex[2] - ex[3] - ey[4]),
        carried[1] - (0.1 * STEP) * around[1] + half * (ey[2] - ex[4] - ey[5]),
        half * (ex[0] + ey[1]) - (0.2 * STEP) * around[2] + (0.8 * STEP) * core[2],
        carried[3] + rl * core[3] - half * ex[0],
        carried[4] + rl * core[4] - (0.5 * half) * (ey[0] + ex[1]),
        carried[5] + rl * core[5] - half * ey[1],
    ]


def steps(mats, ext, side, flow, sflow, td, std, merged, basis, first):
    north, south, west, east = masks()
    lane = lanes((8, 128))
    row, slot = lane // 8, lane % 8
    rows_ok = jnp.where(row < H, north, jnp.where(row < H + R, 1.0, jnp.where(row < E, south, 0.0)))
    side_ok = [rows_ok * jnp.where(slot < 4, west, 1.0), rows_ok * jnp.where(slot < 4, 1.0, east)]

    def timed(f, a, b):
        x = jnp.concatenate([a, b], 1)
        high = x.astype(jnp.bfloat16).astype(jnp.float32)
        both = jnp.concatenate([high, x - high], 0).astype(jnp.bfloat16)
        out = jnp.dot(mats[0 if f < 2 else 1], both, preferred_element_type=jnp.float32)
        out = out[:TP] + out[TP:]
        return out[:, :128], out[:, 128:]

    for k in range(H):
        src, dst = k % 2, 1 - k % 2
        low, count = k + 1, E - 2 * (k + 1)
        last = k == H - 1

        def time_pair(i, carry, src=src, low=low):
            r = low + 2 * i
            for n, f in enumerate(TIMED):
                td[n, r], td[n, r + 1] = timed(f, ext[src, f, r], ext[src, f, r + 1])
            return carry

        lax.fori_loop(0, count // 2, time_pair, 0)
        for n, f in enumerate(TIMED):
            if not last:
                std[n, 0], std[n, 1] = timed(f, side[src, f, 0], side[src, f, 1])
        for f in range(F):
            merged[f] = jnp.where(lanes() % 8 == 3, side[src, f, 0], pltpu.roll(side[src, f, 1], 126, 1))

        def main_row(r, carry, src=src, dst=dst, k=k):
            keep = jnp.where(r < H, north, jnp.where(r < H + R, jnp.float32(1.0), south))
            turn = 125 - 8 * r
            for c in range(TP // 8):
                s = pl.ds(8 * c, 8)
                core = [ext[src, f, r, s] for f in range(F)]
                xm = [ext[src, f, r - 1, s] for f in range(F)]
                xp = [ext[src, f, r + 1, s] for f in range(F)]
                edge = [pltpu.roll(merged[f, s], turn, 1) for f in range(F)]
                ym = [jnp.where(lane == 0, edge[f], pltpu.roll(core[f], 1, 1)) for f in range(F)]
                yp = [jnp.where(lane == 127, edge[f], pltpu.roll(core[f], 127, 1)) for f in range(F)]
                rl = jnp.broadcast_to(flow[0, r, pl.ds(T, 1)], (8, 128))
                times = {f: td[n, r, s] for n, f in enumerate(TIMED)}
                out = combine(core, xm, xp, ym, yp, flow[0, r, s], flow[1, r, s], rl, times)
                for f in range(F):
                    new = out[f] + ext[dst, f, r, s] if k else out[f]
                    ext[dst, f, r, s] = new * keep
            return carry

        lax.fori_loop(low, low + count, main_row, 0)
        for p in range(0 if last else 2):
            for c in range(TP // 8):
                s = pl.ds(8 * c, 8)
                core = [side[src, f, p, s] for f in range(F)]
                xm, xp, ym, yp = ([pltpu.roll(a, by, 1) for a in core] for by in (8, 120, 1, 127))
                rl = jnp.broadcast_to(sflow[0, p, pl.ds(T, 1)], (8, 128))
                times = {f: std[n, p, s] for n, f in enumerate(TIMED)}
                out = combine(core, xm, xp, ym, yp, sflow[0, p, s], sflow[1, p, s], rl, times)
                for f in range(F):
                    new = out[f] + side[dst, f, p, s] if k else out[f]
                    side[dst, f, p, s] = new * side_ok[p]
        for f in range(F):
            for r in range(R):
                basis[first + k, f * R + r] = ext[dst, f, H + r]


def first_kernel(own, flow_in, relax, north, south, c0, cn, cs, mats, main, pack, basis, flow, sflow, ext, side, td, std, merged):
    sides = (cn, c0, cs)
    fill(own, north, south, sides, ext, side)
    for f in range(F):
        for r in range(R):
            basis[0, f * R + r] = ext[0, f, H + r]
    half = 0.5 * STEP
    for j in range(2):
        for r in range(R):
            put(flow, (j, r), raw(north, F + j, r), half)
            put(flow, (j, H + r), raw(flow_in, j, r), half)
            put(flow, (j, H + R + r), raw(south, F + j, r), half)
    for r in range(R):
        flow[0, r, pl.ds(T, 1), :] = north[pl.ds(8 * T * R + r, 1), :] * STEP
        flow[0, H + r, pl.ds(T, 1), :] = relax[pl.ds(r, 1), :] * STEP
        flow[0, H + R + r, pl.ds(T, 1), :] = south[pl.ds(8 * T * R + r, 1), :] * STEP
    sub = lax.broadcasted_iota(jnp.int32, (TP, 128), 0)
    scale = jnp.where(sub == T, STEP, half).astype(jnp.float32)
    slot = lanes() % 8
    for j in range(2):
        sides_of(sflow, j, own_windows(lambda e: flow[j, e]), sides, 1, 2 + j)
        for p in range(2):
            halo = (slot < 4) if p == 0 else (slot >= 4)
            sflow[j, p] = sflow[j, p] * jnp.where(halo, scale, 1.0)
    steps(mats, ext, side, flow, sflow, td, std, merged, basis, 1)
    for f in range(F):
        for r in range(R):
            main[pl.ds(f * T * R + r, T, stride=R), :] = basis[H, f * R + r, 0:T]
    for g in range(2):
        total = jnp.zeros((TP, 128), jnp.float32)
        for j in range(4 if g == 0 else 2):
            for r in range(R):
                total = total + window(basis[H, (g * 4 + j) * R + r], j * 32 + r * 8)
        pack[g] = total


def second_kernel(own, north, south, c0, cn, cs, flow, sflow, older, mats, basis, gram, ext, side, td, std, merged, rows):
    fill(own, north, south, (cn, c0, cs), ext, side)
    steps(mats, ext, side, flow, sflow, td, std, merged, basis, 0)

    def slab(i, sums):
        sums = list(sums)
        for c in range(TP // 8):
            s = pl.ds(8 * c, 8)
            vec = [older[k, i, s] for k in range(5)] + [basis[k, i, s] for k in range(4)]
            for e, (a, b) in enumerate(PAIRS):
                sums[e] = sums[e] + vec[a] * vec[b]
        return tuple(sums)

    zero = jnp.zeros((8, 128), jnp.float32)
    sums = lax.fori_loop(0, F * R, slab, (zero,) * len(PAIRS))
    rows[...] = jnp.zeros((48, 128), jnp.float32)
    for e, value in enumerate(sums):
        rows[pl.ds(e, 1), :] = jnp.sum(value, axis=0, keepdims=True)
    total = jnp.sum(rows[...], axis=1, keepdims=True)
    pick = lanes((48, 128)) == lax.broadcasted_iota(jnp.int32, (48, 128), 0)
    line = jnp.sum(jnp.where(pick, total, 0.0), axis=0, keepdims=True)
    gram[...] = jnp.broadcast_to(line, (PEERS, 128))


def plus(a, b):
    return b if a is None else a if b is None else a + b


def minus(a, b):
    return a if b is None else -b if a is None else a - b


def times(a, b):
    return None if a is None or b is None else a * b


def shifted(q):
    out = [None] * NV
    for i in range(NV):
        if i + 1 < NV:
            out[i + 1] = plus(out[i + 1], q[i])
        if i >= 1 and i != 4:
            out[i - 1] = minus(out[i - 1], q[i])
    return out


def cycle(gram, c):
    q = [c]
    for k in range(3):
        new = shifted(q[-1])
        q.append([plus(a, b) for a, b in zip(new, q[-2])] if k else new)
    w = [[plus(times(2.0, a), times(1.5 * RHO, b)) for a, b in zip(v, shifted(v))] for v in q]

    def dot(a, b):
        total = None
        for x, y in zip(a, b):
            total = plus(total, times(x, y))
        return total

    gw = [[dot(gram[i], v) for i in range(NV)] for v in w]
    n = 4
    target = [dot(c, gw[i]) for i in range(n)]
    factor = [[None] * n for _ in range(n)]
    for j in range(n):
        diag = dot(w[j], gw[j])
        for m in range(j):
            diag = diag - factor[j][m] * factor[j][m]
        root = jnp.sqrt(diag)
        factor[j][j] = root
        for i in range(j + 1, n):
            value = dot(w[i], gw[j])
            for m in range(j):
                value = value - factor[i][m] * factor[j][m]
            factor[i][j] = value / root
    y = []
    for i in range(n):
        value = target[i]
        for m in range(i):
            value = value - factor[i][m] * y[m]
        y.append(value / factor[i][i])
    for i in reversed(range(n)):
        value = y[i]
        for m in range(i + 1, n):
            value = value - factor[m][i] * y[m]
        y[i] = value / factor[i][i]
    step, rest = [None] * NV, list(c)
    for i in range(n):
        step = [plus(a, times(y[i], b)) for a, b in zip(step, q[i])]
        rest = [minus(a, times(y[i], b)) for a, b in zip(rest, w[i])]
    return step, rest


def last_kernel(parts, older, newer, solution, residual):
    total = jnp.sum(parts[...].reshape(PEERS // 8, 8, 128), axis=0)
    total = jnp.sum(total, axis=0, keepdims=True)
    gram = [[None] * NV for _ in range(NV)]
    for e, (i, j) in enumerate(PAIRS):
        gram[i][j] = gram[j][i] = jnp.broadcast_to(total[:, e : e + 1], (8, 128))
    step1, rest = cycle(gram, [1.0] + [None] * (NV - 1))
    zero = jnp.zeros((8, 128), jnp.float32)
    rest = [zero if a is None else a for a in rest]
    step2, rest = cycle(gram, rest)
    step = [plus(a, b) for a, b in zip(step1, step2)]
    step = [None if a is None else a[0:1] for a in step]
    rest = [a[0:1] for a in rest]

    def slab(i, carry):
        f, r = i // R, i % R
        sol = res = None
        for k in range(NV):
            x = older[k, i, 0:T] if k < 5 else newer[k - 5, i, 0:T]
            if step[k] is not None:
                sol = plus(sol, step[k] * x)
            res = plus(res, rest[k] * x)
        solution[pl.ds(f * T * R + r, T, stride=R), :] = sol
        residual[pl.ds(f * T * R + r, T, stride=R), :] = res
        return carry

    lax.fori_loop(0, F * R, slab, 0)


def call(kernel, args, outs, scratch=(), final=False):
    args = [pltpu.with_memory_space_constraint(a, pltpu.VMEM) for a in args]
    make = jax.ShapeDtypeStruct if final else pltpu.VMEM
    return pl.pallas_call(
        kernel,
        out_shape=[make(shape, jnp.float32) for shape in outs],
        in_specs=[VM] * len(args),
        out_specs=[VM] * len(outs),
        scratch_shapes=[pltpu.VMEM(shape, jnp.float32) for shape in scratch],
        compiler_params=pltpu.CompilerParams(vmem_limit_bytes=24 << 20),
    )(*args)


def both_ways(x, axis):
    count = lax.axis_size(axis)
    forward = [(i, i + 1) for i in range(count - 1)]
    backward = [(i + 1, i) for i in range(count - 1)]
    return lax.ppermute(x, axis, forward), lax.ppermute(x, axis, backward)


def exchange(main, pack):
    north, south = both_ways(main, "gy")
    left, right = both_ways(pack, "gx")
    slot = lax.broadcasted_iota(jnp.int32, pack.shape, 2) % 8
    here = jnp.where(slot < 4, left, right)
    above, below = both_ways(here, "gy")
    return north, south, here, above, below


WORK = (
    (2, F, E, TP, 128),
    (2, F, 2, TP, 128),
    (len(TIMED), E, TP, 128),
    (len(TIMED), 2, TP, 128),
    (F, TP, 128),
)


def shards(right_side, base_flow, relax):
    rs = right_side.reshape(F * T * R, 128)
    flow = base_flow.reshape(2 * T * R, 128)
    mats = jnp.asarray(time_matrices())
    main, pack = call(pack_kernel, (rs, flow, relax), ((8 * T * R + 8, 128), (2, TP, 128)))
    halo = exchange(main, pack)
    main, pack, older, flows, side_flows = call(
        first_kernel,
        (rs, flow, relax, *halo, mats),
        ((F * T * R, 128), (2, TP, 128), (5, F * R, TP, 128), (2, E, TP, 128), (2, 2, TP, 128)),
        WORK,
    )
    halo = exchange(main, pack)
    newer, gram = call(
        second_kernel,
        (main, *halo, flows, side_flows, older, mats),
        ((4, F * R, TP, 128), (PEERS, 128)),
        WORK + ((48, 128),),
    )
    parts = lax.all_to_all(gram.reshape(PEERS, 1, 128), ("gx", "gy"), 0, 0, tiled=True)
    solution_field, residual = call(
        last_kernel,
        (parts.reshape(PEERS, 128), older, newer),
        ((F * T * R, 128), (F * T * R, 128)),
        final=True,
    )
    return solution_field.reshape(right_side.shape), residual.reshape(right_side.shape)


def solution(mesh):
    placed = (P(None, None, "gy", "gx"), P(None, None, "gy", "gx"), P("gy", "gx"))
    return jax.shard_map(
        shards,
        mesh=mesh,
        in_specs=placed,
        out_specs=(P(None, None, "gy", "gx"), P(None, None, "gy", "gx")),
        check_vma=False,
    )
```

```python
import jax
import jax.numpy as jnp
import numpy as np
from jax import lax
from jax.experimental import pallas as pl
from jax.experimental.pallas import tpu as pltpu
from jax.sharding import PartitionSpec as P

F = 6
T = 33
TP = 40
R = 4
H = 4
E = R + 2 * H
NV = 9
SHIFT = 0.5
SCALE = 0.46
STEP = SCALE / 3.0
MOVE = SCALE * SHIFT
TIMED = (0, 1, 3, 4, 5)
PAIRS = [(i, j) for i in range(NV) for j in range(i, NV)]
PEERS = 256
VM = pl.BlockSpec(memory_space=pltpu.VMEM)


def time_matrices():
    index = np.arange(T, dtype=np.float64)
    diff = index[:, None] - index[None, :]
    sines = np.where(diff == 0.0, 1.0, np.sin(np.pi * diff / T))
    dmat = np.where(diff == 0.0, 0.0, 0.5 * np.where(diff % 2 == 0, 1.0, -1.0) / sines)
    mats = []
    for diagonal in (0.4 * STEP - MOVE, -MOVE):
        full = np.zeros((TP, TP), np.float32)
        full[:T, :T] = 0.8 * STEP * dmat + diagonal * np.eye(T)
        high = full.astype(jnp.bfloat16)
        low = (full - high.astype(np.float32)).astype(jnp.bfloat16)
        top = np.concatenate([high, high], 1)
        bottom = np.concatenate([low, np.zeros_like(low)], 1)
        mats.append(np.concatenate([top, bottom], 0))
    return np.stack(mats)


def lanes(shape=(1, 128)):
    return lax.broadcasted_iota(jnp.int32, shape, len(shape) - 1)


def window(x, place):
    lane = lanes()
    return jnp.where((lane >= place) & (lane < place + 8), pltpu.roll(x, (place + 4) % 128, 1), 0.0)


def raw(ref, f, r):
    return ref[pl.ds(f * T * R + r, T, stride=R), :]


def pack_kernel(rs, flow, relax, mats_in, message, pack, mats, sems):
    rows = F * T * R
    copies = [
        pltpu.make_async_copy(rs, message.at[pl.ds(0, rows)], sems.at[0]),
        pltpu.make_async_copy(flow, message.at[pl.ds(rows, 2 * T * R)], sems.at[1]),
        pltpu.make_async_copy(relax, message.at[pl.ds(8 * T * R, R)], sems.at[2]),
        pltpu.make_async_copy(mats_in, mats, sems.at[3]),
    ]
    for copy in copies:
        copy.start()
    for copy in copies:
        copy.wait()
    for g in range(2):
        total = jnp.zeros((T, 128), jnp.float32)
        for j in range(4):
            for r in range(R):
                total = total + window(raw(message, g * 4 + j, r), j * 32 + r * 8)
        pack[g * TP : g * TP + 32, :] = total[0:32]
        last = jnp.zeros((8, 128), jnp.float32)
        sub = lax.broadcasted_iota(jnp.int32, (8, 128), 0)
        last = jnp.where(sub == 0, jnp.broadcast_to(total[32:33], (8, 128)), last)
        if g == 1:
            extra = jnp.zeros((1, 128), jnp.float32)
            for r in range(R):
                extra = extra + window(message[pl.ds(8 * T * R + r, 1), :], 2 * 32 + r * 8)
            last = jnp.where(sub == 1, jnp.broadcast_to(extra, (8, 128)), last)
        pack[g * TP + 32 : g * TP + 40, :] = last


def put(dst, index, x, scale=None):
    dst[index + (pl.ds(32, 8), slice(None))] = jnp.zeros((8, 128), jnp.float32)
    dst[index + (pl.ds(0, T), slice(None))] = x if scale is None else x * scale


def slabs_of(ref):
    return [ref.at[pl.ds(g * TP, TP)] for g in range(2)]


def sides_of(dst, f, own, sides, g, j, ok):
    lane = lanes()
    north, here, south = (
        pltpu.roll(ref[g][...], (base - 32 * j) % 128, 1) for base, ref in zip((0, 32, 64), sides)
    )
    halo = jnp.where(lane < 32, north, jnp.where(lane < 64, here, south))
    slot = lane % 8
    dst[f, 0] = jnp.where(slot < 4, halo, own) * ok[0]
    dst[f, 1] = jnp.where(slot < 4, own, halo) * ok[1]


def own_windows(slab):
    total = jnp.zeros((TP, 128), jnp.float32)
    for e in range(E):
        total = total + window(slab(e), e * 8)
    return total


def fill(own, north, south, sides, ext, side):
    ok_north, ok_south, _, _ = masks()
    ok = side_masks((1, 128))
    for f in range(F):
        for r in range(R):
            put(ext, (f, r), raw(north, f, r), ok_north)
            put(ext, (f, H + r), raw(own, f, r))
            put(ext, (f, H + R + r), raw(south, f, r), ok_south)
    for f in range(F):
        sides_of(side, f, own_windows(lambda e: ext[f, e]), sides, f // 4, f % 4, ok)


def masks():
    gx, gy = lax.axis_index("gx"), lax.axis_index("gy")
    north = jnp.where(gy > 0, 1.0, 0.0).astype(jnp.float32)
    south = jnp.where(gy < lax.axis_size("gy") - 1, 1.0, 0.0).astype(jnp.float32)
    west = jnp.where(gx > 0, 1.0, 0.0).astype(jnp.float32)
    east = jnp.where(gx < lax.axis_size("gx") - 1, 1.0, 0.0).astype(jnp.float32)
    return north, south, west, east


def side_masks(shape):
    north, south, west, east = masks()
    lane = lanes(shape)
    row, slot = lane // 8, lane % 8
    rows_ok = jnp.where(row < H, north, jnp.where(row < H + R, 1.0, jnp.where(row < E, south, 0.0)))
    return [rows_ok * jnp.where(slot < 4, west, 1.0), rows_ok * jnp.where(slot < 4, 1.0, east)]


def combine(core, xm, xp, ym, yp, fu, fv, rl, td):
    ex = [a - b for a, b in zip(xp, xm)]
    ey = [a - b for a, b in zip(yp, ym)]
    half = 0.5 * STEP
    carried = {f: td[f] + fu * ex[f] + fv * ey[f] for f in TIMED}
    around = [xp[f] + xm[f] + (yp[f] + ym[f]) for f in range(3)]
    return [
        carried[0] - (0.1 * STEP) * around[0] + half * (ex[2] - ex[3] - ey[4]),
        carried[1] - (0.1 * STEP) * around[1] + half * (ey[2] - ex[4] - ey[5]),
        half * (ex[0] + ey[1]) - (0.2 * STEP) * around[2] + (0.8 * STEP - MOVE) * core[2],
        carried[3] + rl * core[3] - half * ex[0],
        carried[4] + rl * core[4] - (0.5 * half) * (ey[0] + ex[1]),
        carried[5] + rl * core[5] - half * ey[1],
    ]


def steps(mats, exts, slabs, flow, sflow, td, std, merged, basis, first):
    north, south, _, _ = masks()
    side_ok = side_masks((8, 128))
    lane = lanes((8, 128))

    def timed(f, a, b):
        x = jnp.concatenate([a, b], 1)
        high = x.astype(jnp.bfloat16).astype(jnp.float32)
        both = jnp.concatenate([high, x - high], 0).astype(jnp.bfloat16)
        out = jnp.dot(mats[0 if f < 2 else 1], both, preferred_element_type=jnp.float32)
        out = out[:TP] + out[TP:]
        return out[:, :128], out[:, 128:]

    for k in range(H):
        src, dst = exts[k % 2], exts[1 - k % 2]
        side, side_new = slabs[k % 2], slabs[1 - k % 2]
        low, count = k + 1, E - 2 * (k + 1)
        last = k == H - 1

        def time_pair(r, src=src):
            for n, f in enumerate(TIMED):
                td[n, r], td[n, r + 1] = timed(f, src[f, r], src[f, r + 1])

        def main_row(r, src=src, dst=dst):
            keep = jnp.where(r < H, north, jnp.where(r < H + R, jnp.float32(1.0), south))
            turn = 125 - 8 * r
            for c in range(TP // 8):
                s = pl.ds(8 * c, 8)
                core = [src[f, r, s] for f in range(F)]
                xm = [src[f, r - 1, s] for f in range(F)]
                xp = [src[f, r + 1, s] for f in range(F)]
                edge = [pltpu.roll(merged[f, s], turn, 1) for f in range(F)]
                ym = [jnp.where(lane == 0, edge[f], pltpu.roll(core[f], 1, 1)) for f in range(F)]
                yp = [jnp.where(lane == 127, edge[f], pltpu.roll(core[f], 127, 1)) for f in range(F)]
                rl = jnp.broadcast_to(flow[0, r, pl.ds(T, 1)], (8, 128))
                times = {f: td[n, r, s] for n, f in enumerate(TIMED)}
                out = combine(core, xm, xp, ym, yp, flow[0, r, s], flow[1, r, s], rl, times)
                for f in range(F):
                    dst[f, r, s] = out[f] * keep

        def pair(i, carry, low=low, time_pair=time_pair, main_row=main_row):
            r = low + 2 * i
            time_pair(jnp.minimum(r + 2, E - 2))
            main_row(r)
            main_row(r + 1)
            return carry

        for f in range(F):
            merged[f] = jnp.where(lanes() % 8 == 3, side[f, 0], pltpu.roll(side[f, 1], 126, 1))
        if not last:
            for n, f in enumerate(TIMED):
                std[n, 0], std[n, 1] = timed(f, side[f, 0], side[f, 1])
        time_pair(low)
        lax.fori_loop(0, count // 2, pair, 0)
        for p in range(0 if last else 2):
            for c in range(TP // 8):
                s = pl.ds(8 * c, 8)
                core = [side[f, p, s] for f in range(F)]
                xm, xp, ym, yp = ([pltpu.roll(a, by, 1) for a in core] for by in (8, 120, 1, 127))
                rl = jnp.broadcast_to(sflow[0, p, pl.ds(T, 1)], (8, 128))
                times = {f: std[n, p, s] for n, f in enumerate(TIMED)}
                out = combine(core, xm, xp, ym, yp, sflow[0, p, s], sflow[1, p, s], rl, times)
                for f in range(F):
                    side_new[f, p, s] = out[f] * side_ok[p]
        for f in range(F):
            for r in range(R):
                basis[first + k, f * R + r] = dst[f, H + r]


def first_kernel(own, north, south, above, here, below, mats, main, pack, basis, flow, sflow, ext0, ext1, side0, side1, td, std, merged):
    sides = [slabs_of(ref) for ref in (above, here, below)]
    fill(own, north, south, sides, ext0, side0)
    for f in range(F):
        for r in range(R):
            basis[0, f * R + r] = ext0[f, H + r]
    half = 0.5 * STEP
    for j in range(2):
        for r in range(R):
            put(flow, (j, r), raw(north, F + j, r), half)
            put(flow, (j, H + r), raw(own, F + j, r), half)
            put(flow, (j, H + R + r), raw(south, F + j, r), half)
    for r in range(R):
        flow[0, r, pl.ds(T, 1), :] = north[pl.ds(8 * T * R + r, 1), :] * STEP
        flow[0, H + r, pl.ds(T, 1), :] = own[pl.ds(8 * T * R + r, 1), :] * STEP
        flow[0, H + R + r, pl.ds(T, 1), :] = south[pl.ds(8 * T * R + r, 1), :] * STEP
    sub = lax.broadcasted_iota(jnp.int32, (TP, 128), 0)
    scale = jnp.where(sub == T, STEP, half).astype(jnp.float32)
    slot = lanes() % 8
    for j in range(2):
        sides_of(sflow, j, own_windows(lambda e: flow[j, e]), sides, 1, 2 + j, (1.0, 1.0))
        for p in range(2):
            halo = (slot < 4) if p == 0 else (slot >= 4)
            sflow[j, p] = sflow[j, p] * jnp.where(halo, scale, 1.0)
    steps(mats, (ext0, ext1), (side0, side1), flow, sflow, td, std, merged, basis, 1)
    for f in range(F):
        for r in range(R):
            main[pl.ds(f * T * R + r, T, stride=R), :] = basis[H, f * R + r, 0:T]
    for g in range(2):
        total = jnp.zeros((TP, 128), jnp.float32)
        for j in range(4 if g == 0 else 2):
            for r in range(R):
                total = total + window(basis[H, (g * 4 + j) * R + r], j * 32 + r * 8)
        pack[g * TP : (g + 1) * TP, :] = total


def second_kernel(own, north, south, above, here, below, flow, sflow, older, mats, basis, gram, ext0, ext1, side0, side1, td, std, merged, rows):
    fill(own, north, south, [slabs_of(ref) for ref in (above, here, below)], ext0, side0)
    steps(mats, (ext0, ext1), (side0, side1), flow, sflow, td, std, merged, basis, 0)

    def slab(i, sums):
        sums = list(sums)
        for c in range(TP // 8):
            s = pl.ds(8 * c, 8)
            vec = [older[k, i, s] for k in range(5)] + [basis[k, i, s] for k in range(4)]
            for e, (a, b) in enumerate(PAIRS):
                sums[e] = sums[e] + vec[a] * vec[b]
        return tuple(sums)

    zero = jnp.zeros((8, 128), jnp.float32)
    sums = lax.fori_loop(0, F * R, slab, (zero,) * len(PAIRS))
    rows[...] = jnp.zeros((48, 128), jnp.float32)
    for e, value in enumerate(sums):
        rows[pl.ds(e, 1), :] = jnp.sum(value, axis=0, keepdims=True)
    total = jnp.sum(rows[...], axis=1, keepdims=True)
    pick = lanes((48, 128)) == lax.broadcasted_iota(jnp.int32, (48, 128), 0)
    line = jnp.sum(jnp.where(pick, total, 0.0), axis=0, keepdims=True)
    gram[...] = jnp.broadcast_to(line, (PEERS, 128))


def plus(a, b):
    return b if a is None else a if b is None else a + b


def minus(a, b):
    return a if b is None else -b if a is None else a - b


def times(a, b):
    return None if a is None or b is None else a * b


def cycle(gram, c):
    q = [c]
    for _ in range(4):
        q.append([None] + q[-1][:-1])
    w = [
        [plus(times(2.0 + 3.0 * SHIFT, a), times(3.0 / SCALE, b)) for a, b in zip(q[k], q[k + 1])]
        for k in range(4)
    ]

    def dot(a, b):
        total = None
        for x, y in zip(a, b):
            total = plus(total, times(x, y))
        return total

    gw = [[dot(gram[i], v) for i in range(NV)] for v in w]
    n = 4
    target = [dot(c, gw[i]) for i in range(n)]
    factor = [[None] * n for _ in range(n)]
    for j in range(n):
        diag = dot(w[j], gw[j])
        for m in range(j):
            diag = diag - factor[j][m] * factor[j][m]
        root = jnp.sqrt(diag)
        factor[j][j] = root
        for i in range(j + 1, n):
            value = dot(w[i], gw[j])
            for m in range(j):
                value = value - factor[i][m] * factor[j][m]
            factor[i][j] = value / root
    y = []
    for i in range(n):
        value = target[i]
        for m in range(i):
            value = value - factor[i][m] * y[m]
        y.append(value / factor[i][i])
    for i in reversed(range(n)):
        value = y[i]
        for m in range(i + 1, n):
            value = value - factor[m][i] * y[m]
        y[i] = value / factor[i][i]
    step, rest = [None] * NV, list(c)
    for i in range(n):
        step = [plus(a, times(y[i], b)) for a, b in zip(step, q[i])]
        rest = [minus(a, times(y[i], b)) for a, b in zip(rest, w[i])]
    return step, rest


def last_kernel(parts, older, newer, solution, residual):
    total = jnp.sum(parts[...].reshape(PEERS // 8, 8, 128), axis=0)
    total = jnp.sum(total, axis=0, keepdims=True)
    gram = [[None] * NV for _ in range(NV)]
    for e, (i, j) in enumerate(PAIRS):
        gram[i][j] = gram[j][i] = jnp.broadcast_to(total[:, e : e + 1], (8, 128))
    step1, rest = cycle(gram, [1.0] + [None] * (NV - 1))
    zero = jnp.zeros((8, 128), jnp.float32)
    rest = [zero if a is None else a for a in rest]
    step2, rest = cycle(gram, rest)
    step = [plus(a, b) for a, b in zip(step1, step2)]
    step = [None if a is None else a[0:1] for a in step]
    rest = [a[0:1] for a in rest]

    def slab(i, carry):
        f, r = i // R, i % R
        sol = res = None
        for k in range(NV):
            x = older[k, i, 0:T] if k < 5 else newer[k - 5, i, 0:T]
            if step[k] is not None:
                sol = plus(sol, step[k] * x)
            res = plus(res, rest[k] * x)
        solution[pl.ds(f * T * R + r, T, stride=R), :] = sol
        residual[pl.ds(f * T * R + r, T, stride=R), :] = res
        return carry

    lax.fori_loop(0, F * R, slab, 0)


def call(kernel, args, outs, scratch=(), first=False, final=False):
    space = pltpu.HBM if first else pltpu.VMEM
    args = [pltpu.with_memory_space_constraint(a, space) for a in args]
    make = jax.ShapeDtypeStruct if final else pltpu.VMEM
    kinds = [jnp.bfloat16 if shape[-1] == 2 * TP else jnp.float32 for shape in outs]
    scratch = [pltpu.VMEM(shape, jnp.float32) for shape in scratch]
    return pl.pallas_call(
        kernel,
        out_shape=[make(shape, kind) for shape, kind in zip(outs, kinds)],
        in_specs=[pl.BlockSpec(memory_space=space)] * len(args),
        out_specs=[VM] * len(outs),
        scratch_shapes=scratch + [pltpu.SemaphoreType.DMA((4,))] * first,
        compiler_params=pltpu.CompilerParams(vmem_limit_bytes=24 << 20),
    )(*args)


def both_ways(x, axis):
    count = lax.axis_size(axis)
    forward = [(i, (i + 1) % count) for i in range(count)]
    backward = [((i + 1) % count, i) for i in range(count)]
    return lax.ppermute(x, axis, forward), lax.ppermute(x, axis, backward)


def exchange(message, pack):
    north, south = both_ways(message, "gy")
    left, right = both_ways(pack, "gx")
    slot = lax.broadcasted_iota(jnp.int32, pack.shape, 1) % 8
    here = jnp.where(slot < 4, left, right)
    above, below = both_ways(here, "gy")
    return message, north, south, above, here, below


WORK = (
    (F, E, TP, 128),
    (F, E, TP, 128),
    (F, 2, TP, 128),
    (F, 2, TP, 128),
    (len(TIMED), E, TP, 128),
    (len(TIMED), 2, TP, 128),
    (F, TP, 128),
)


def shards(right_side, base_flow, relax):
    rs = right_side.reshape(F * T * R, 128)
    flow = base_flow.reshape(2 * T * R, 128)
    message, pack, mats = call(
        pack_kernel,
        (rs, flow, relax, jnp.asarray(time_matrices())),
        ((8 * T * R + 8, 128), (2 * TP, 128), (2, 2 * TP, 2 * TP)),
        first=True,
    )
    message, pack, older, flows, side_flows = call(
        first_kernel,
        (*exchange(message, pack), mats),
        ((F * T * R, 128), (2 * TP, 128), (5, F * R, TP, 128), (2, E, TP, 128), (2, 2, TP, 128)),
        WORK,
    )
    newer, gram = call(
        second_kernel,
        (*exchange(message, pack), flows, side_flows, older, mats),
        ((4, F * R, TP, 128), (PEERS, 128)),
        WORK + ((48, 128),),
    )
    parts = lax.all_to_all(gram.reshape(PEERS, 1, 128), ("gx", "gy"), 0, 0, tiled=True)
    solution_field, residual = call(
        last_kernel,
        (parts.reshape(PEERS, 128), older, newer),
        ((F * T * R, 128), (F * T * R, 128)),
        final=True,
    )
    return solution_field.reshape(right_side.shape), residual.reshape(right_side.shape)


def solution(mesh):
    placed = (P(None, None, "gy", "gx"), P(None, None, "gy", "gx"), P("gy", "gx"))
    return jax.shard_map(
        shards,
        mesh=mesh,
        in_specs=placed,
        out_specs=(P(None, None, "gy", "gx"), P(None, None, "gy", "gx")),
        check_vma=False,
    )
```

```python
import jax
import jax.numpy as jnp
import numpy as np
from jax import lax
from jax.experimental import pallas as pl
from jax.experimental.pallas import tpu as pltpu
from jax.sharding import PartitionSpec as P

F = 6
T = 33
TP = 40
R = 4
H = 4
E = R + 2 * H
NV = 9
SHIFT = 0.5
SCALE = 0.46
STEP = SCALE / 3.0
MOVE = SCALE * SHIFT
TIMED = (0, 1, 3, 4, 5)
PAIRS = [(i, j) for i in range(NV) for j in range(i, NV)]
PEERS = 256
VM = pl.BlockSpec(memory_space=pltpu.VMEM)


def time_matrices():
    index = np.arange(T, dtype=np.float64)
    diff = index[:, None] - index[None, :]
    sines = np.where(diff == 0.0, 1.0, np.sin(np.pi * diff / T))
    dmat = np.where(diff == 0.0, 0.0, 0.5 * np.where(diff % 2 == 0, 1.0, -1.0) / sines)
    mats = []
    for diagonal in (0.4 * STEP - MOVE, -MOVE):
        full = np.zeros((TP, TP), np.float32)
        full[:T, :T] = 0.8 * STEP * dmat + diagonal * np.eye(T)
        high = full.astype(jnp.bfloat16)
        low = (full - high.astype(np.float32)).astype(jnp.bfloat16)
        top = np.concatenate([high, high], 1)
        bottom = np.concatenate([low, np.zeros_like(low)], 1)
        mats.append(np.concatenate([top, bottom], 0))
    return np.stack(mats)


def lanes(shape=(1, 128)):
    return lax.broadcasted_iota(jnp.int32, shape, len(shape) - 1)


def window(x, place):
    lane = lanes()
    return jnp.where((lane >= place) & (lane < place + 8), pltpu.roll(x, (place + 4) % 128, 1), 0.0)


def raw(ref, f, r):
    return ref[pl.ds(f * T * R + r, T, stride=R), :]


def pack_kernel(rs, flow, relax, mats_in, message, pack, mats, sems):
    rows = F * T * R
    copies = [
        pltpu.make_async_copy(rs, message.at[pl.ds(0, rows)], sems.at[0]),
        pltpu.make_async_copy(flow, message.at[pl.ds(rows, 2 * T * R)], sems.at[1]),
        pltpu.make_async_copy(relax, message.at[pl.ds(8 * T * R, R)], sems.at[2]),
        pltpu.make_async_copy(mats_in, mats, sems.at[3]),
    ]
    for copy in copies:
        copy.start()
    for copy in copies:
        copy.wait()
    for g in range(2):
        total = jnp.zeros((T, 128), jnp.float32)
        for j in range(4):
            for r in range(R):
                total = total + window(raw(message, g * 4 + j, r), j * 32 + r * 8)
        pack[g * TP : g * TP + 32, :] = total[0:32]
        last = jnp.zeros((8, 128), jnp.float32)
        sub = lax.broadcasted_iota(jnp.int32, (8, 128), 0)
        last = jnp.where(sub == 0, jnp.broadcast_to(total[32:33], (8, 128)), last)
        if g == 1:
            extra = jnp.zeros((1, 128), jnp.float32)
            for r in range(R):
                extra = extra + window(message[pl.ds(8 * T * R + r, 1), :], 2 * 32 + r * 8)
            last = jnp.where(sub == 1, jnp.broadcast_to(extra, (8, 128)), last)
        pack[g * TP + 32 : g * TP + 40, :] = last


def put(dst, index, x, scale=None):
    dst[index + (pl.ds(32, 8), slice(None))] = jnp.zeros((8, 128), jnp.float32)
    dst[index + (pl.ds(0, T), slice(None))] = x if scale is None else x * scale


def slabs_of(ref):
    return [ref.at[pl.ds(g * TP, TP)] for g in range(2)]


def sides_of(dst, f, own, sides, g, j, ok):
    lane = lanes()
    north, here, south = (
        pltpu.roll(ref[g][...], (base - 32 * j) % 128, 1) for base, ref in zip((0, 32, 64), sides)
    )
    halo = jnp.where(lane < 32, north, jnp.where(lane < 64, here, south))
    slot = lane % 8
    dst[f, 0] = jnp.where(slot < 4, halo, own) * ok[0]
    dst[f, 1] = jnp.where(slot < 4, own, halo) * ok[1]


def own_windows(slab):
    total = jnp.zeros((TP, 128), jnp.float32)
    for e in range(E):
        total = total + window(slab(e), e * 8)
    return total


def fill(own, north, south, sides, ext, side):
    ok_north, ok_south, _, _ = masks()
    ok = side_masks((1, 128))
    for f in range(F):
        for r in range(R):
            put(ext, (f, r), raw(north, f, r), ok_north)
            put(ext, (f, H + r), raw(own, f, r))
            put(ext, (f, H + R + r), raw(south, f, r), ok_south)
    for f in range(F):
        sides_of(side, f, own_windows(lambda e: ext[f, e]), sides, f // 4, f % 4, ok)


def masks():
    gx, gy = lax.axis_index("gx"), lax.axis_index("gy")
    north = jnp.where(gy > 0, 1.0, 0.0).astype(jnp.float32)
    south = jnp.where(gy < lax.axis_size("gy") - 1, 1.0, 0.0).astype(jnp.float32)
    west = jnp.where(gx > 0, 1.0, 0.0).astype(jnp.float32)
    east = jnp.where(gx < lax.axis_size("gx") - 1, 1.0, 0.0).astype(jnp.float32)
    return north, south, west, east


def side_masks(shape):
    north, south, west, east = masks()
    lane = lanes(shape)
    row, slot = lane // 8, lane % 8
    rows_ok = jnp.where(row < H, north, jnp.where(row < H + R, 1.0, jnp.where(row < E, south, 0.0)))
    return [rows_ok * jnp.where(slot < 4, west, 1.0), rows_ok * jnp.where(slot < 4, 1.0, east)]


def combine(core, xm, xp, ym, yp, fu, fv, rl, td):
    ex = [a - b for a, b in zip(xp, xm)]
    ey = [a - b for a, b in zip(yp, ym)]
    half = 0.5 * STEP
    carried = {f: td[f] + fu * ex[f] + fv * ey[f] for f in TIMED}
    around = [xp[f] + xm[f] + (yp[f] + ym[f]) for f in range(3)]
    return [
        carried[0] - (0.1 * STEP) * around[0] + half * (ex[2] - ex[3] - ey[4]),
        carried[1] - (0.1 * STEP) * around[1] + half * (ey[2] - ex[4] - ey[5]),
        half * (ex[0] + ey[1]) - (0.2 * STEP) * around[2] + (0.8 * STEP - MOVE) * core[2],
        carried[3] + rl * core[3] - half * ex[0],
        carried[4] + rl * core[4] - (0.5 * half) * (ey[0] + ex[1]),
        carried[5] + rl * core[5] - half * ey[1],
    ]


def steps(mats, exts, slabs, flow, sflow, td, std, merged, basis, first):
    north, south, _, _ = masks()
    side_ok = side_masks((8, 128))
    lane = lanes((8, 128))

    def timed(f, a, b):
        x = jnp.concatenate([a, b], 1)
        high = x.astype(jnp.bfloat16).astype(jnp.float32)
        both = jnp.concatenate([high, x - high], 0).astype(jnp.bfloat16)
        out = jnp.dot(mats[0 if f < 2 else 1], both, preferred_element_type=jnp.float32)
        out = out[:TP] + out[TP:]
        return out[:, :128], out[:, 128:]

    for k in range(H):
        src, dst = exts[k % 2], exts[1 - k % 2]
        side, side_new = slabs[k % 2], slabs[1 - k % 2]
        low, count = k + 1, E - 2 * (k + 1)
        last = k == H - 1

        def time_pair(r, src=src):
            for n, f in enumerate(TIMED):
                td[n, r], td[n, r + 1] = timed(f, src[f, r], src[f, r + 1])

        def main_row(r, src=src, dst=dst):
            keep = jnp.where(r < H, north, jnp.where(r < H + R, jnp.float32(1.0), south))
            turn = 125 - 8 * r
            for c in range(TP // 8):
                s = pl.ds(8 * c, 8)
                core = [src[f, r, s] for f in range(F)]
                xm = [src[f, r - 1, s] for f in range(F)]
                xp = [src[f, r + 1, s] for f in range(F)]
                edge = [pltpu.roll(merged[f, s], turn, 1) for f in range(F)]
                ym = [jnp.where(lane == 0, edge[f], pltpu.roll(core[f], 1, 1)) for f in range(F)]
                yp = [jnp.where(lane == 127, edge[f], pltpu.roll(core[f], 127, 1)) for f in range(F)]
                rl = jnp.broadcast_to(flow[0, r, pl.ds(T, 1)], (8, 128))
                times = {f: td[n, r, s] for n, f in enumerate(TIMED)}
                out = combine(core, xm, xp, ym, yp, flow[0, r, s], flow[1, r, s], rl, times)
                for f in range(F):
                    dst[f, r, s] = out[f] * keep

        def pair(i, carry, low=low, time_pair=time_pair, main_row=main_row):
            r = low + 2 * i
            time_pair(jnp.minimum(r + 2, E - 2))
            main_row(r)
            main_row(r + 1)
            return carry

        for f in range(F):
            merged[f] = jnp.where(lanes() % 8 == 3, side[f, 0], pltpu.roll(side[f, 1], 126, 1))
        if not last:
            for n, f in enumerate(TIMED):
                std[n, 0], std[n, 1] = timed(f, side[f, 0], side[f, 1])
        time_pair(low)
        lax.fori_loop(0, count // 2, pair, 0)
        for p in range(0 if last else 2):
            for c in range(TP // 8):
                s = pl.ds(8 * c, 8)
                core = [side[f, p, s] for f in range(F)]
                xm, xp, ym, yp = ([pltpu.roll(a, by, 1) for a in core] for by in (8, 120, 1, 127))
                rl = jnp.broadcast_to(sflow[0, p, pl.ds(T, 1)], (8, 128))
                times = {f: std[n, p, s] for n, f in enumerate(TIMED)}
                out = combine(core, xm, xp, ym, yp, sflow[0, p, s], sflow[1, p, s], rl, times)
                for f in range(F):
                    side_new[f, p, s] = out[f] * side_ok[p]
        for f in range(F):
            for r in range(R):
                basis[first + k, f * R + r] = dst[f, H + r]


def by_parity(load, rows, corners):
    odd = lax.rem(lax.axis_index("gy"), 2) == 1

    @pl.when(odd)
    def _():
        load(*rows, *corners)

    @pl.when(jnp.logical_not(odd))
    def _():
        load(*rows[::-1], *corners[::-1])


def first_kernel(own, even, odd, here, corner_even, corner_odd, mats, main, pack, basis, flow, sflow, ext0, ext1, side0, side1, td, std, merged):
    half = 0.5 * STEP

    def load(north, south, above, below):
        sides = [slabs_of(ref) for ref in (above, here, below)]
        fill(own, north, south, sides, ext0, side0)
        for j in range(2):
            for r in range(R):
                put(flow, (j, r), raw(north, F + j, r), half)
                put(flow, (j, H + r), raw(own, F + j, r), half)
                put(flow, (j, H + R + r), raw(south, F + j, r), half)
        for r in range(R):
            for base, ref in zip((0, H, H + R), (north, own, south)):
                flow[0, base + r, pl.ds(T, 1), :] = ref[pl.ds(8 * T * R + r, 1), :] * STEP
        sub = lax.broadcasted_iota(jnp.int32, (TP, 128), 0)
        scale = jnp.where(sub == T, STEP, half).astype(jnp.float32)
        slot = lanes() % 8
        for j in range(2):
            sides_of(sflow, j, own_windows(lambda e: flow[j, e]), sides, 1, 2 + j, (1.0, 1.0))
            for p in range(2):
                halo = (slot < 4) if p == 0 else (slot >= 4)
                sflow[j, p] = sflow[j, p] * jnp.where(halo, scale, 1.0)

    by_parity(load, (even, odd), (corner_even, corner_odd))
    for f in range(F):
        for r in range(R):
            basis[0, f * R + r] = ext0[f, H + r]
    steps(mats, (ext0, ext1), (side0, side1), flow, sflow, td, std, merged, basis, 1)
    for f in range(F):
        for r in range(R):
            main[pl.ds(f * T * R + r, T, stride=R), :] = basis[H, f * R + r, 0:T]
    for g in range(2):
        total = jnp.zeros((TP, 128), jnp.float32)
        for j in range(4 if g == 0 else 2):
            for r in range(R):
                total = total + window(basis[H, (g * 4 + j) * R + r], j * 32 + r * 8)
        pack[g * TP : (g + 1) * TP, :] = total


def second_kernel(own, even, odd, here, corner_even, corner_odd, flow, sflow, older, mats, basis, gram, ext0, ext1, side0, side1, td, std, merged, rows):

    def load(north, south, above, below):
        fill(own, north, south, [slabs_of(ref) for ref in (above, here, below)], ext0, side0)

    by_parity(load, (even, odd), (corner_even, corner_odd))
    steps(mats, (ext0, ext1), (side0, side1), flow, sflow, td, std, merged, basis, 0)

    def slab(i, sums):
        sums = list(sums)
        for c in range(TP // 8):
            s = pl.ds(8 * c, 8)
            vec = [older[k, i, s] for k in range(5)] + [basis[k, i, s] for k in range(4)]
            for e, (a, b) in enumerate(PAIRS):
                sums[e] = sums[e] + vec[a] * vec[b]
        return tuple(sums)

    zero = jnp.zeros((8, 128), jnp.float32)
    sums = lax.fori_loop(0, F * R, slab, (zero,) * len(PAIRS))
    rows[...] = jnp.zeros((48, 128), jnp.float32)
    for e, value in enumerate(sums):
        rows[pl.ds(e, 1), :] = jnp.sum(value, axis=0, keepdims=True)
    total = jnp.sum(rows[...], axis=1, keepdims=True)
    pick = lanes((48, 128)) == lax.broadcasted_iota(jnp.int32, (48, 128), 0)
    line = jnp.sum(jnp.where(pick, total, 0.0), axis=0, keepdims=True)
    gram[...] = jnp.broadcast_to(line, (PEERS, 128))


def plus(a, b):
    return b if a is None else a if b is None else a + b


def minus(a, b):
    return a if b is None else -b if a is None else a - b


def times(a, b):
    return None if a is None or b is None else a * b


def cycle(gram, c):
    q = [c]
    for _ in range(4):
        q.append([None] + q[-1][:-1])
    w = [
        [plus(times(2.0 + 3.0 * SHIFT, a), times(3.0 / SCALE, b)) for a, b in zip(q[k], q[k + 1])]
        for k in range(4)
    ]

    def dot(a, b):
        total = None
        for x, y in zip(a, b):
            total = plus(total, times(x, y))
        return total

    gw = [[dot(gram[i], v) for i in range(NV)] for v in w]
    n = 4
    target = [dot(c, gw[i]) for i in range(n)]
    factor = [[None] * n for _ in range(n)]
    for j in range(n):
        diag = dot(w[j], gw[j])
        for m in range(j):
            diag = diag - factor[j][m] * factor[j][m]
        root = jnp.sqrt(diag)
        factor[j][j] = root
        for i in range(j + 1, n):
            value = dot(w[i], gw[j])
            for m in range(j):
                value = value - factor[i][m] * factor[j][m]
            factor[i][j] = value / root
    y = []
    for i in range(n):
        value = target[i]
        for m in range(i):
            value = value - factor[i][m] * y[m]
        y.append(value / factor[i][i])
    for i in reversed(range(n)):
        value = y[i]
        for m in range(i + 1, n):
            value = value - factor[m][i] * y[m]
        y[i] = value / factor[i][i]
    step, rest = [None] * NV, list(c)
    for i in range(n):
        step = [plus(a, times(y[i], b)) for a, b in zip(step, q[i])]
        rest = [minus(a, times(y[i], b)) for a, b in zip(rest, w[i])]
    return step, rest


def last_kernel(parts, older, newer, solution, residual):
    total = jnp.sum(parts[...].reshape(PEERS // 8, 8, 128), axis=0)
    total = jnp.sum(total, axis=0, keepdims=True)
    gram = [[None] * NV for _ in range(NV)]
    for e, (i, j) in enumerate(PAIRS):
        gram[i][j] = gram[j][i] = jnp.broadcast_to(total[:, e : e + 1], (8, 128))
    step1, rest = cycle(gram, [1.0] + [None] * (NV - 1))
    zero = jnp.zeros((8, 128), jnp.float32)
    rest = [zero if a is None else a for a in rest]
    step2, rest = cycle(gram, rest)
    step = [plus(a, b) for a, b in zip(step1, step2)]
    step = [None if a is None else a[0:1] for a in step]
    rest = [a[0:1] for a in rest]

    def slab(i, carry):
        f, r = i // R, i % R
        sol = res = None
        for k in range(NV):
            x = older[k, i, 0:T] if k < 5 else newer[k - 5, i, 0:T]
            if step[k] is not None:
                sol = plus(sol, step[k] * x)
            res = plus(res, rest[k] * x)
        solution[pl.ds(f * T * R + r, T, stride=R), :] = sol
        residual[pl.ds(f * T * R + r, T, stride=R), :] = res
        return carry

    lax.fori_loop(0, F * R, slab, 0)


def call(kernel, args, outs, scratch=(), first=False, final=False):
    space = pltpu.HBM if first else pltpu.VMEM
    args = [pltpu.with_memory_space_constraint(a, space) for a in args]
    make = jax.ShapeDtypeStruct if final else pltpu.VMEM
    kinds = [jnp.bfloat16 if shape[-1] == 2 * TP else jnp.float32 for shape in outs]
    scratch = [pltpu.VMEM(shape, jnp.float32) for shape in scratch]
    return pl.pallas_call(
        kernel,
        out_shape=[make(shape, kind) for shape, kind in zip(outs, kinds)],
        in_specs=[pl.BlockSpec(memory_space=space)] * len(args),
        out_specs=[VM] * len(outs),
        scratch_shapes=scratch + [pltpu.SemaphoreType.DMA((4,))] * first,
        compiler_params=pltpu.CompilerParams(vmem_limit_bytes=24 << 20),
    )(*args)


def exchange(message, pack):
    across, down = lax.axis_size("gx"), lax.axis_size("gy")
    even = [(g * down + j, g * down + (j ^ 1)) for g in range(across) for j in range(down)]
    odd = []
    for g in range(across):
        for j in range(down):
            edge = j in (0, down - 1)
            other = j if edge else j + 1 if j % 2 else j - 1
            odd.append((g * down + j, (g ^ 1 if edge else g) * down + other))
    axes = ("gx", "gy")
    rows = [lax.ppermute(message, axes, pairs) for pairs in (even, odd)]
    left = lax.ppermute(pack, "gx", [(g, (g + 1) % across) for g in range(across)])
    right = lax.ppermute(pack, "gx", [((g + 1) % across, g) for g in range(across)])
    slot = lax.broadcasted_iota(jnp.int32, pack.shape, 1) % 8
    here = jnp.where(slot < 4, left, right)
    corners = [lax.ppermute(here, axes, pairs) for pairs in (even, odd)]
    return message, *rows, here, *corners


WORK = (
    (F, E, TP, 128),
    (F, E, TP, 128),
    (F, 2, TP, 128),
    (F, 2, TP, 128),
    (len(TIMED), E, TP, 128),
    (len(TIMED), 2, TP, 128),
    (F, TP, 128),
)


def shards(right_side, base_flow, relax):
    rs = right_side.reshape(F * T * R, 128)
    flow = base_flow.reshape(2 * T * R, 128)
    message, pack, mats = call(
        pack_kernel,
        (rs, flow, relax, jnp.asarray(time_matrices())),
        ((8 * T * R + 8, 128), (2 * TP, 128), (2, 2 * TP, 2 * TP)),
        first=True,
    )
    message, pack, older, flows, side_flows = call(
        first_kernel,
        (*exchange(message, pack), mats),
        ((F * T * R, 128), (2 * TP, 128), (5, F * R, TP, 128), (2, E, TP, 128), (2, 2, TP, 128)),
        WORK,
    )
    newer, gram = call(
        second_kernel,
        (*exchange(message, pack), flows, side_flows, older, mats),
        ((4, F * R, TP, 128), (PEERS, 128)),
        WORK + ((48, 128),),
    )
    parts = lax.all_to_all(gram.reshape(PEERS, 1, 128), ("gx", "gy"), 0, 0, tiled=True)
    solution_field, residual = call(
        last_kernel,
        (parts.reshape(PEERS, 128), older, newer),
        ((F * T * R, 128), (F * T * R, 128)),
        final=True,
    )
    return solution_field.reshape(right_side.shape), residual.reshape(right_side.shape)


def solution(mesh):
    placed = (P(None, None, "gy", "gx"), P(None, None, "gy", "gx"), P("gy", "gx"))
    return jax.shard_map(
        shards,
        mesh=mesh,
        in_specs=placed,
        out_specs=(P(None, None, "gy", "gx"), P(None, None, "gy", "gx")),
        check_vma=False,
    )
```

```python
import jax
import jax.numpy as jnp
import numpy as np
from jax import lax
from jax.experimental import pallas as pl
from jax.experimental.pallas import tpu as pltpu
from jax.sharding import PartitionSpec as P

F = 6
T = 33
TP = 40
R = 4
H = 4
E = R + 2 * H
NV = 9
SHIFT = 0.5
SCALE = 0.46
STEP = SCALE / 3.0
MOVE = SCALE * SHIFT
TIMED = (0, 1, 3, 4, 5)
PAIRS = [(i, j) for i in range(NV) for j in range(i, NV)]
EARLY = [(i, j) for i, j in PAIRS if j < 5]
PEERS = 256
FLOW = 208
VM = pl.BlockSpec(memory_space=pltpu.VMEM)


def time_matrices():
    index = np.arange(T, dtype=np.float64)
    diff = index[:, None] - index[None, :]
    sines = np.where(diff == 0.0, 1.0, np.sin(np.pi * diff / T))
    dmat = np.where(diff == 0.0, 0.0, 0.5 * np.where(diff % 2 == 0, 1.0, -1.0) / sines)
    mats = []
    for diagonal in (0.4 * STEP - MOVE, -MOVE):
        full = np.zeros((TP, TP), np.float32)
        full[:T, :T] = 0.8 * STEP * dmat + diagonal * np.eye(T)
        high = full.astype(jnp.bfloat16)
        low = (full - high.astype(np.float32)).astype(jnp.bfloat16)
        top = np.concatenate([high, high], 1)
        bottom = np.concatenate([low, np.zeros_like(low)], 1)
        mats.append(np.concatenate([top, bottom], 0))
    return np.stack(mats)


def lanes(shape=(1, 128)):
    return lax.broadcasted_iota(jnp.int32, shape, len(shape) - 1)


def window(x, place):
    lane = lanes()
    return jnp.where((lane >= place) & (lane < place + 8), pltpu.roll(x, (place + 4) % 128, 1), 0.0)


def raw(ref, f, r):
    return ref[pl.ds(f * T * R + r, T, stride=R), :]


def is_odd():
    return lax.rem(lax.axis_index("gy"), 2) == 1


def pack_kernel(rs, flow, relax, mats_in, message, even, odd, pack, mats, sems):
    rows = F * T * R
    copies = [
        pltpu.make_async_copy(rs, message.at[pl.ds(0, rows)], sems.at[0]),
        pltpu.make_async_copy(flow, message.at[pl.ds(rows, 2 * T * R)], sems.at[1]),
        pltpu.make_async_copy(relax, message.at[pl.ds(8 * T * R, R)], sems.at[2]),
        pltpu.make_async_copy(mats_in, mats, sems.at[3]),
    ]
    for copy in copies:
        copy.start()
    for copy in copies:
        copy.wait()
    for to in (even, odd):
        to[pl.ds(FLOW - 8, 8), :] = jnp.zeros((8, 128), jnp.float32)
    for g in range(2):
        total = jnp.zeros((T, 128), jnp.float32)
        for j in range(4):
            for r in range(R):
                total = total + window(raw(message, g * 4 + j, r), j * 32 + r * 8)
        pack[g * TP : g * TP + 32, :] = total[0:32]
        last = jnp.zeros((8, 128), jnp.float32)
        sub = lax.broadcasted_iota(jnp.int32, (8, 128), 0)
        last = jnp.where(sub == 0, jnp.broadcast_to(total[32:33], (8, 128)), last)
        if g == 1:
            extra = jnp.zeros((1, 128), jnp.float32)
            for r in range(R):
                extra = extra + window(message[pl.ds(8 * T * R + r, 1), :], 2 * 32 + r * 8)
            last = jnp.where(sub == 1, jnp.broadcast_to(extra, (8, 128)), last)
        pack[g * TP + 32 : g * TP + 40, :] = last

    def rows_for(to, first):
        for j in range(2):
            for q in range(H - 1):
                to[pl.ds((j * (H - 1) + q) * T, T), :] = raw(message, F + j, first + q)
        for q in range(H - 1):
            to[pl.ds(2 * (H - 1) * T + q, 1), :] = message[pl.ds(8 * T * R + first + q, 1), :]

    @pl.when(is_odd())
    def _():
        rows_for(even, 0)
        rows_for(odd, 1)

    @pl.when(jnp.logical_not(is_odd()))
    def _():
        rows_for(even, 1)
        rows_for(odd, 0)


def put(dst, index, x, scale=None):
    dst[index + (pl.ds(32, 8), slice(None))] = jnp.zeros((8, 128), jnp.float32)
    dst[index + (pl.ds(0, T), slice(None))] = x if scale is None else x * scale


def slabs_of(ref):
    return [ref.at[pl.ds(g * TP, TP)] for g in range(2)]


def sides_of(dst, f, own, sides, g, j, ok):
    lane = lanes()
    north, here, south = (
        pltpu.roll(ref[g][...], (base - 32 * j) % 128, 1) for base, ref in zip((0, 32, 64), sides)
    )
    halo = jnp.where(lane < 32, north, jnp.where(lane < 64, here, south))
    slot = lane % 8
    dst[f, 0] = jnp.where(slot < 4, halo, own) * ok[0]
    dst[f, 1] = jnp.where(slot < 4, own, halo) * ok[1]


def own_windows(slab, rows=range(E)):
    total = jnp.zeros((TP, 128), jnp.float32)
    for e in rows:
        total = total + window(slab(e), e * 8)
    return total


def fill(own, north, south, sides, ext, side):
    ok_north, ok_south, _, _ = masks()
    ok = side_masks((1, 128))
    for f in range(F):
        for r in range(R):
            put(ext, (f, r), raw(north, f, r), ok_north)
            put(ext, (f, H + r), raw(own, f, r))
            put(ext, (f, H + R + r), raw(south, f, r), ok_south)
    for f in range(F):
        sides_of(side, f, own_windows(lambda e: ext[f, e]), sides, f // 4, f % 4, ok)


def masks():
    gx, gy = lax.axis_index("gx"), lax.axis_index("gy")
    north = jnp.where(gy > 0, 1.0, 0.0).astype(jnp.float32)
    south = jnp.where(gy < lax.axis_size("gy") - 1, 1.0, 0.0).astype(jnp.float32)
    west = jnp.where(gx > 0, 1.0, 0.0).astype(jnp.float32)
    east = jnp.where(gx < lax.axis_size("gx") - 1, 1.0, 0.0).astype(jnp.float32)
    return north, south, west, east


def side_masks(shape):
    north, south, west, east = masks()
    lane = lanes(shape)
    row, slot = lane // 8, lane % 8
    rows_ok = jnp.where(row < H, north, jnp.where(row < H + R, 1.0, jnp.where(row < E, south, 0.0)))
    return [rows_ok * jnp.where(slot < 4, west, 1.0), rows_ok * jnp.where(slot < 4, 1.0, east)]


def combine(core, xm, xp, ym, yp, fu, fv, rl, td):
    ex = [a - b for a, b in zip(xp, xm)]
    ey = [a - b for a, b in zip(yp, ym)]
    half = 0.5 * STEP
    carried = {f: td[f] + fu * ex[f] + fv * ey[f] for f in TIMED}
    around = [xp[f] + xm[f] + (yp[f] + ym[f]) for f in range(3)]
    return [
        carried[0] - (0.1 * STEP) * around[0] + half * (ex[2] - ex[3] - ey[4]),
        carried[1] - (0.1 * STEP) * around[1] + half * (ey[2] - ex[4] - ey[5]),
        half * (ex[0] + ey[1]) - (0.2 * STEP) * around[2] + (0.8 * STEP - MOVE) * core[2],
        carried[3] + rl * core[3] - half * ex[0],
        carried[4] + rl * core[4] - (0.5 * half) * (ey[0] + ex[1]),
        carried[5] + rl * core[5] - half * ey[1],
    ]


def steps(mats, exts, slabs, flow, sflow, td, std, merged, basis, first):
    north, south, _, _ = masks()
    side_ok = side_masks((8, 128))
    lane = lanes((8, 128))

    def timed(f, a, b):
        x = jnp.concatenate([a, b], 1)
        high = x.astype(jnp.bfloat16).astype(jnp.float32)
        both = jnp.concatenate([high, x - high], 0).astype(jnp.bfloat16)
        out = jnp.dot(mats[0 if f < 2 else 1], both, preferred_element_type=jnp.float32)
        out = out[:TP] + out[TP:]
        return out[:, :128], out[:, 128:]

    for k in range(H):
        src, dst = exts[k % 2], exts[1 - k % 2]
        side, side_new = slabs[k % 2], slabs[1 - k % 2]
        low, count = k + 1, E - 2 * (k + 1)
        last = k == H - 1

        def time_pair(r, src=src):
            for n, f in enumerate(TIMED):
                td[n, r], td[n, r + 1] = timed(f, src[f, r], src[f, r + 1])

        def main_pair(r, src=src, dst=dst):
            keep = [jnp.where(e < H, north, jnp.where(e < H + R, jnp.float32(1.0), south)) for e in (r, r + 1)]
            for c in range(TP // 8):
                s = pl.ds(8 * c, 8)
                rows = [[src[f, r + e, s] for f in range(F)] for e in (-1, 0, 1, 2)]
                beside = [merged[f, s] for f in range(F)]
                for e in range(2):
                    xm, core, xp = rows[e : e + 3]
                    edge = [pltpu.roll(a, 125 - 8 * (r + e), 1) for a in beside]
                    ym = [jnp.where(lane == 0, b, pltpu.roll(a, 1, 1)) for a, b in zip(core, edge)]
                    yp = [jnp.where(lane == 127, b, pltpu.roll(a, 127, 1)) for a, b in zip(core, edge)]
                    rl = jnp.broadcast_to(flow[0, r + e, pl.ds(T, 1)], (8, 128))
                    times = {f: td[n, r + e, s] for n, f in enumerate(TIMED)}
                    out = combine(core, xm, xp, ym, yp, flow[0, r + e, s], flow[1, r + e, s], rl, times)
                    for f in range(F):
                        dst[f, r + e, s] = out[f] * keep[e]

        def pair(i, carry, low=low, time_pair=time_pair, main_pair=main_pair):
            r = low + 2 * i
            time_pair(jnp.minimum(r + 2, E - 2))
            main_pair(r)
            return carry

        for f in range(F):
            merged[f] = jnp.where(lanes() % 8 == 3, side[f, 0], pltpu.roll(side[f, 1], 126, 1))
        if not last:
            for n, f in enumerate(TIMED):
                std[n, 0], std[n, 1] = timed(f, side[f, 0], side[f, 1])
        time_pair(low)
        lax.fori_loop(0, count // 2, pair, 0, unroll=True)
        for p in range(0 if last else 2):
            for c in range(TP // 8):
                s = pl.ds(8 * c, 8)
                core = [side[f, p, s] for f in range(F)]
                xm, xp, ym, yp = ([pltpu.roll(a, by, 1) for a in core] for by in (8, 120, 1, 127))
                rl = jnp.broadcast_to(sflow[0, p, pl.ds(T, 1)], (8, 128))
                times = {f: std[n, p, s] for n, f in enumerate(TIMED)}
                out = combine(core, xm, xp, ym, yp, sflow[0, p, s], sflow[1, p, s], rl, times)
                for f in range(F):
                    side_new[f, p, s] = out[f] * side_ok[p]
        for f in range(F):
            for r in range(R):
                basis[first + k, f * R + r] = dst[f, H + r]


def by_parity(load, *pairs):
    @pl.when(is_odd())
    def _():
        load(*[pair[0] for pair in pairs], *[pair[1] for pair in pairs])

    @pl.when(jnp.logical_not(is_odd()))
    def _():
        load(*[pair[1] for pair in pairs], *[pair[0] for pair in pairs])


def first_kernel(own, even, odd, here, corner_even, corner_odd, flow_even, flow_odd, mats, main, pack, basis, flow, sflow, ext0, ext1, side0, side1, td, std, merged):
    half = 0.5 * STEP

    def load(north, above, flow_north, south, below, flow_south):
        sides = [slabs_of(ref) for ref in (above, here, below)]
        fill(own, north, south, sides, ext0, side0)
        for j in range(2):
            for r in range(R):
                put(flow, (j, H + r), raw(own, F + j, r), half)
            for q in range(H - 1):
                place = pl.ds((j * (H - 1) + q) * T, T)
                put(flow, (j, 1 + q), flow_north[place, :], half)
                put(flow, (j, H + R + q), flow_south[place, :], half)
        for r in range(R):
            flow[0, H + r, pl.ds(T, 1), :] = own[pl.ds(8 * T * R + r, 1), :] * STEP
        for q in range(H - 1):
            place = pl.ds(2 * (H - 1) * T + q, 1)
            flow[0, 1 + q, pl.ds(T, 1), :] = flow_north[place, :] * STEP
            flow[0, H + R + q, pl.ds(T, 1), :] = flow_south[place, :] * STEP
        sub = lax.broadcasted_iota(jnp.int32, (TP, 128), 0)
        scale = jnp.where(sub == T, STEP, half).astype(jnp.float32)
        slot = lanes() % 8
        for j in range(2):
            sides_of(sflow, j, own_windows(lambda e: flow[j, e], range(1, E - 1)), sides, 1, 2 + j, (1.0, 1.0))
            for p in range(2):
                halo = (slot < 4) if p == 0 else (slot >= 4)
                sflow[j, p] = sflow[j, p] * jnp.where(halo, scale, 1.0)

    by_parity(load, (even, odd), (corner_even, corner_odd), (flow_even, flow_odd))
    for f in range(F):
        for r in range(R):
            basis[0, f * R + r] = ext0[f, H + r]
    steps(mats, (ext0, ext1), (side0, side1), flow, sflow, td, std, merged, basis, 1)
    for f in range(F):
        for r in range(R):
            main[pl.ds(f * T * R + r, T, stride=R), :] = basis[H, f * R + r, 0:T]
    for g in range(2):
        total = jnp.zeros((TP, 128), jnp.float32)
        for j in range(4 if g == 0 else 2):
            for r in range(R):
                total = total + window(basis[H, (g * 4 + j) * R + r], j * 32 + r * 8)
        pack[g * TP : (g + 1) * TP, :] = total


def products(slabs, pairs):
    def slab(i, sums):
        sums = list(sums)
        for c in range(TP // 8):
            s = pl.ds(8 * c, 8)
            vec = [get(i, s) for get in slabs]
            for e, (a, b) in enumerate(pairs):
                sums[e] = sums[e] + vec[a] * vec[b]
        return tuple(sums)

    zero = jnp.zeros((8, 128), jnp.float32)
    return lax.fori_loop(0, F * R, slab, (zero,) * len(pairs), unroll=2)


def gram_kernel(older, early):
    slabs = [lambda i, s, k=k: older[k, i, s] for k in range(5)]
    for e, value in enumerate(products(slabs, EARLY)):
        early[e] = value


def second_kernel(own, even, odd, here, corner_even, corner_odd, flow, sflow, older, early, mats, basis, gram, ext0, ext1, side0, side1, td, std, merged, rows):

    def load(north, above, south, below):
        fill(own, north, south, [slabs_of(ref) for ref in (above, here, below)], ext0, side0)

    by_parity(load, (even, odd), (corner_even, corner_odd))
    steps(mats, (ext0, ext1), (side0, side1), flow, sflow, td, std, merged, basis, 0)

    late = [pair for pair in PAIRS if pair not in EARLY]
    slabs = [lambda i, s, k=k: older[k, i, s] for k in range(5)] + [lambda i, s, k=k: basis[k, i, s] for k in range(4)]
    sums = dict(zip(late, products(slabs, late)))
    for e, pair in enumerate(EARLY):
        sums[pair] = early[e]
    rows[...] = jnp.zeros((48, 128), jnp.float32)
    for e, pair in enumerate(PAIRS):
        rows[pl.ds(e, 1), :] = jnp.sum(sums[pair], axis=0, keepdims=True)
    total = jnp.sum(rows[...], axis=1, keepdims=True)
    pick = lanes((48, 128)) == lax.broadcasted_iota(jnp.int32, (48, 128), 0)
    line = jnp.sum(jnp.where(pick, total, 0.0), axis=0, keepdims=True)
    gram[...] = jnp.broadcast_to(line, (PEERS, 128))


def plus(a, b):
    return b if a is None else a if b is None else a + b


def minus(a, b):
    return a if b is None else -b if a is None else a - b


def times(a, b):
    return None if a is None or b is None else a * b


def cycle(gram, c):
    q = [c]
    for _ in range(4):
        q.append([None] + q[-1][:-1])
    w = [
        [plus(times(2.0 + 3.0 * SHIFT, a), times(3.0 / SCALE, b)) for a, b in zip(q[k], q[k + 1])]
        for k in range(4)
    ]

    def dot(a, b):
        total = None
        for x, y in zip(a, b):
            total = plus(total, times(x, y))
        return total

    gw = [[dot(gram[i], v) for i in range(NV)] for v in w]
    n = 4
    y = [dot(c, gw[i]) for i in range(n)]
    low, inverse = [[None] * n for _ in range(n)], []
    for j in range(n):
        held = [dot(w[i], gw[j]) for i in range(j, n)]
        for m in range(j):
            scaled = low[j][m] * diag[m]
            held = [v - low[i][m] * scaled for i, v in zip(range(j, n), held)]
        diag = (diag if j else []) + [held[0]]
        inverse.append(1.0 / held[0])
        low[j][j] = 1.0
        for i in range(j + 1, n):
            low[i][j] = held[i - j] * inverse[j]
    for i in range(n):
        for m in range(i):
            y[i] = y[i] - low[i][m] * y[m]
    y = [a * b for a, b in zip(y, inverse)]
    for i in reversed(range(n)):
        for m in range(i + 1, n):
            y[i] = y[i] - low[m][i] * y[m]
    step, rest = [None] * NV, list(c)
    for i in range(n):
        step = [plus(a, times(y[i], b)) for a, b in zip(step, q[i])]
        rest = [minus(a, times(y[i], b)) for a, b in zip(rest, w[i])]
    return step, rest


def last_kernel(parts, older, newer, solution, residual):
    total = jnp.sum(parts[...].reshape(PEERS // 8, 8, 128), axis=0)
    total = jnp.sum(total, axis=0, keepdims=True)
    gram = [[None] * NV for _ in range(NV)]
    for e, (i, j) in enumerate(PAIRS):
        gram[i][j] = gram[j][i] = jnp.broadcast_to(total[:, e : e + 1], (8, 128))
    step1, rest = cycle(gram, [1.0] + [None] * (NV - 1))
    zero = jnp.zeros((8, 128), jnp.float32)
    rest = [zero if a is None else a for a in rest]
    step2, rest = cycle(gram, rest)
    step = [plus(a, b) for a, b in zip(step1, step2)]
    step = [None if a is None else a[0:1] for a in step]
    rest = [a[0:1] for a in rest]

    def slab(i, carry):
        f, r = i // R, i % R
        sol = res = None
        for k in range(NV):
            x = older[k, i, 0:T] if k < 5 else newer[k - 5, i, 0:T]
            if step[k] is not None:
                sol = plus(sol, step[k] * x)
            res = plus(res, rest[k] * x)
        solution[pl.ds(f * T * R + r, T, stride=R), :] = sol
        residual[pl.ds(f * T * R + r, T, stride=R), :] = res
        return carry

    lax.fori_loop(0, F * R, slab, 0)


def call(kernel, args, outs, scratch=(), first=False, final=False):
    space = pltpu.HBM if first else pltpu.VMEM
    args = [pltpu.with_memory_space_constraint(a, space) for a in args]
    make = jax.ShapeDtypeStruct if final else pltpu.VMEM
    kinds = [jnp.bfloat16 if shape[-1] == 2 * TP else jnp.float32 for shape in outs]
    scratch = [pltpu.VMEM(shape, jnp.float32) for shape in scratch]
    return pl.pallas_call(
        kernel,
        out_shape=[make(shape, kind) for shape, kind in zip(outs, kinds)],
        in_specs=[pl.BlockSpec(memory_space=space)] * len(args),
        out_specs=[VM] * len(outs),
        scratch_shapes=scratch + [pltpu.SemaphoreType.DMA((4,))] * first,
        compiler_params=pltpu.CompilerParams(vmem_limit_bytes=24 << 20),
    )(*args)


def trades(across, down):
    even = [(g * down + j, g * down + (j ^ 1)) for g in range(across) for j in range(down)]
    odd = []
    for g in range(across):
        for j in range(down):
            edge = j in (0, down - 1)
            other = j if edge else j + 1 if j % 2 else j - 1
            odd.append((g * down + j, (g ^ 1 if edge else g) * down + other))
    return even, odd


def exchange(rows, pack):
    across = lax.axis_size("gx")
    pairs = trades(across, lax.axis_size("gy"))
    axes = ("gx", "gy")
    rows = [lax.ppermute(rows, axes, p) for p in pairs]
    left = lax.ppermute(pack, "gx", [(g, (g + 1) % across) for g in range(across)])
    right = lax.ppermute(pack, "gx", [((g + 1) % across, g) for g in range(across)])
    slot = lax.broadcasted_iota(jnp.int32, pack.shape, 1) % 8
    here = jnp.where(slot < 4, left, right)
    corners = [lax.ppermute(here, axes, p) for p in pairs]
    return *rows, here, *corners


WORK = (
    (F, E, TP, 128),
    (F, E, TP, 128),
    (F, 2, TP, 128),
    (F, 2, TP, 128),
    (len(TIMED), E, TP, 128),
    (len(TIMED), 2, TP, 128),
    (F, TP, 128),
)


def shards(right_side, base_flow, relax):
    rs = right_side.reshape(F * T * R, 128)
    flow = base_flow.reshape(2 * T * R, 128)
    own, to_even, to_odd, pack, mats = call(
        pack_kernel,
        (rs, flow, relax, jnp.asarray(time_matrices())),
        ((8 * T * R + 8, 128), (FLOW, 128), (FLOW, 128), (2 * TP, 128), (2, 2 * TP, 2 * TP)),
        first=True,
    )
    flows = [
        lax.ppermute(x, ("gx", "gy"), pairs)
        for x, pairs in zip((to_even, to_odd), trades(lax.axis_size("gx"), lax.axis_size("gy")))
    ]
    own, pack, older, flows, side_flows = call(
        first_kernel,
        (own, *exchange(rs, pack), *flows, mats),
        ((F * T * R, 128), (2 * TP, 128), (5, F * R, TP, 128), (2, E, TP, 128), (2, 2, TP, 128)),
        WORK,
    )
    (early,) = call(gram_kernel, (older,), ((len(EARLY), 8, 128),))
    newer, gram = call(
        second_kernel,
        (own, *exchange(own, pack), flows, side_flows, older, early, mats),
        ((4, F * R, TP, 128), (PEERS, 128)),
        WORK + ((48, 128),),
    )
    parts = lax.all_to_all(gram.reshape(PEERS, 1, 128), ("gx", "gy"), 0, 0, tiled=True)
    solution_field, residual = call(
        last_kernel,
        (parts.reshape(PEERS, 128), older, newer),
        ((F * T * R, 128), (F * T * R, 128)),
        final=True,
    )
    return solution_field.reshape(right_side.shape), residual.reshape(right_side.shape)


def solution(mesh):
    placed = (P(None, None, "gy", "gx"), P(None, None, "gy", "gx"), P("gy", "gx"))
    return jax.shard_map(
        shards,
        mesh=mesh,
        in_specs=placed,
        out_specs=(P(None, None, "gy", "gx"), P(None, None, "gy", "gx")),
        check_vma=False,
    )
```

```python
import jax
import jax.numpy as jnp
import numpy as np
from jax import lax
from jax.experimental import pallas as pl
from jax.experimental.pallas import tpu as pltpu
from jax.sharding import PartitionSpec as P

F = 6
T = 33
TP = 40
R = 4
H = 4
E = R + 2 * H
NV = 9
SHIFT = 0.5
SCALE = 0.46
STEP = SCALE / 3.0
MOVE = SCALE * SHIFT
TIMED = (0, 1, 3, 4, 5)
PAIRS = [(i, j) for i in range(NV) for j in range(i, NV)]
EARLY = [(i, j) for i, j in PAIRS if j < 5]
PEERS = 256
SIDE = 2 * TP
FLOW = 208
VM = pl.BlockSpec(memory_space=pltpu.VMEM)


def time_matrices():
    index = np.arange(T, dtype=np.float64)
    diff = index[:, None] - index[None, :]
    sines = np.where(diff == 0.0, 1.0, np.sin(np.pi * diff / T))
    dmat = np.where(diff == 0.0, 0.0, 0.5 * np.where(diff % 2 == 0, 1.0, -1.0) / sines)
    mats = []
    for diagonal in (0.4 * STEP - MOVE, -MOVE):
        full = np.zeros((TP, TP), np.float32)
        full[:T, :T] = 0.8 * STEP * dmat + diagonal * np.eye(T)
        high = full.astype(jnp.bfloat16)
        low = (full - high.astype(np.float32)).astype(jnp.bfloat16)
        top = np.concatenate([high, high], 1)
        bottom = np.concatenate([low, np.zeros_like(low)], 1)
        mats.append(np.concatenate([top, bottom], 0))
    return np.stack(mats)


def lanes(shape=(1, 128)):
    return lax.broadcasted_iota(jnp.int32, shape, len(shape) - 1)


def window(x, place):
    lane = lanes()
    return jnp.where((lane >= place) & (lane < place + 8), pltpu.roll(x, (place + 4) % 128, 1), 0.0)


def raw(ref, f, r):
    return ref[pl.ds(f * T * R + r, T, stride=R), :]


def is_odd():
    return lax.rem(lax.axis_index("gy"), 2) == 1


def pack_kernel(rs, flow, relax, mats_in, message, even, odd, pack, mats, sems):
    rows = F * T * R
    copies = [
        pltpu.make_async_copy(rs, message.at[pl.ds(0, rows)], sems.at[0]),
        pltpu.make_async_copy(flow, message.at[pl.ds(rows, 2 * T * R)], sems.at[1]),
        pltpu.make_async_copy(relax, message.at[pl.ds(8 * T * R, R)], sems.at[2]),
        pltpu.make_async_copy(mats_in, mats, sems.at[3]),
    ]
    for copy in copies:
        copy.start()
    for copy in copies:
        copy.wait()
    for to in (even, odd):
        to[pl.ds(SIDE + FLOW - 8, 8), :] = jnp.zeros((8, 128), jnp.float32)
    for g in range(2):
        total = jnp.zeros((T, 128), jnp.float32)
        for j in range(4):
            for r in range(R):
                total = total + window(raw(message, g * 4 + j, r), j * 32 + r * 8)
        pack[g * TP : g * TP + 32, :] = total[0:32]
        last = jnp.zeros((8, 128), jnp.float32)
        sub = lax.broadcasted_iota(jnp.int32, (8, 128), 0)
        last = jnp.where(sub == 0, jnp.broadcast_to(total[32:33], (8, 128)), last)
        if g == 1:
            extra = jnp.zeros((1, 128), jnp.float32)
            for r in range(R):
                extra = extra + window(message[pl.ds(8 * T * R + r, 1), :], 2 * 32 + r * 8)
            last = jnp.where(sub == 1, jnp.broadcast_to(extra, (8, 128)), last)
        pack[g * TP + 32 : g * TP + 40, :] = last

    def rows_for(to, first):
        for j in range(2):
            for q in range(H - 1):
                to[pl.ds(SIDE + (j * (H - 1) + q) * T, T), :] = raw(message, F + j, first + q)
        for q in range(H - 1):
            to[pl.ds(SIDE + 2 * (H - 1) * T + q, 1), :] = message[pl.ds(8 * T * R + first + q, 1), :]

    @pl.when(is_odd())
    def _():
        rows_for(even, 0)
        rows_for(odd, 1)

    @pl.when(jnp.logical_not(is_odd()))
    def _():
        rows_for(even, 1)
        rows_for(odd, 0)


def put(dst, index, x, scale=None):
    dst[index + (pl.ds(32, 8), slice(None))] = jnp.zeros((8, 128), jnp.float32)
    dst[index + (pl.ds(0, T), slice(None))] = x if scale is None else x * scale


def slabs_of(ref):
    return [ref.at[pl.ds(g * TP, TP)] for g in range(2)]


def sides_of(dst, f, own, sides, g, j, ok):
    lane = lanes()
    north, here, south = (
        pltpu.roll(ref[g][...], (base - 32 * j) % 128, 1) for base, ref in zip((0, 32, 64), sides)
    )
    halo = jnp.where(lane < 32, north, jnp.where(lane < 64, here, south))
    slot = lane % 8
    dst[f, 0] = jnp.where(slot < 4, halo, own) * ok[0]
    dst[f, 1] = jnp.where(slot < 4, own, halo) * ok[1]


def own_windows(slab, rows=range(E)):
    total = jnp.zeros((TP, 128), jnp.float32)
    for e in rows:
        total = total + window(slab(e), e * 8)
    return total


def fill(own, north, south, sides, ext, side):
    ok_north, ok_south, _, _ = masks()
    ok = side_masks((1, 128))
    for f in range(F):
        for r in range(R):
            put(ext, (f, r), raw(north, f, r), ok_north)
            put(ext, (f, H + r), raw(own, f, r))
            put(ext, (f, H + R + r), raw(south, f, r), ok_south)
    for f in range(F):
        sides_of(side, f, own_windows(lambda e: ext[f, e]), sides, f // 4, f % 4, ok)


def masks():
    gx, gy = lax.axis_index("gx"), lax.axis_index("gy")
    north = jnp.where(gy > 0, 1.0, 0.0).astype(jnp.float32)
    south = jnp.where(gy < lax.axis_size("gy") - 1, 1.0, 0.0).astype(jnp.float32)
    west = jnp.where(gx > 0, 1.0, 0.0).astype(jnp.float32)
    east = jnp.where(gx < lax.axis_size("gx") - 1, 1.0, 0.0).astype(jnp.float32)
    return north, south, west, east


def side_masks(shape):
    north, south, west, east = masks()
    lane = lanes(shape)
    row, slot = lane // 8, lane % 8
    rows_ok = jnp.where(row < H, north, jnp.where(row < H + R, 1.0, jnp.where(row < E, south, 0.0)))
    return [rows_ok * jnp.where(slot < 4, west, 1.0), rows_ok * jnp.where(slot < 4, 1.0, east)]


def combine(core, xm, xp, ym, yp, fu, fv, rl, td):
    ex = [a - b for a, b in zip(xp, xm)]
    ey = [a - b for a, b in zip(yp, ym)]
    half = 0.5 * STEP
    carried = {f: td[f] + fu * ex[f] + fv * ey[f] for f in TIMED}
    around = [xp[f] + xm[f] + (yp[f] + ym[f]) for f in range(3)]
    return [
        carried[0] - (0.1 * STEP) * around[0] + half * (ex[2] - ex[3] - ey[4]),
        carried[1] - (0.1 * STEP) * around[1] + half * (ey[2] - ex[4] - ey[5]),
        half * (ex[0] + ey[1]) - (0.2 * STEP) * around[2] + (0.8 * STEP - MOVE) * core[2],
        carried[3] + rl * core[3] - half * ex[0],
        carried[4] + rl * core[4] - (0.5 * half) * (ey[0] + ex[1]),
        carried[5] + rl * core[5] - half * ey[1],
    ]


def steps(mats, exts, slabs, flow, sflow, td, std, merged, basis, first):
    north, south, _, _ = masks()
    side_ok = side_masks((8, 128))
    lane = lanes((8, 128))

    def timed(f, a, b):
        x = jnp.concatenate([a, b], 1)
        high = x.astype(jnp.bfloat16).astype(jnp.float32)
        both = jnp.concatenate([high, x - high], 0).astype(jnp.bfloat16)
        out = jnp.dot(mats[0 if f < 2 else 1], both, preferred_element_type=jnp.float32)
        out = out[:TP] + out[TP:]
        return out[:, :128], out[:, 128:]

    for k in range(H):
        src, dst = exts[k % 2], exts[1 - k % 2]
        side, side_new = slabs[k % 2], slabs[1 - k % 2]
        low, count = k + 1, E - 2 * (k + 1)
        last = k == H - 1

        def time_pair(r, src=src):
            for n, f in enumerate(TIMED):
                td[n, r], td[n, r + 1] = timed(f, src[f, r], src[f, r + 1])

        def main_pair(r, src=src, dst=dst):
            keep = [jnp.where(e < H, north, jnp.where(e < H + R, jnp.float32(1.0), south)) for e in (r, r + 1)]
            for c in range(TP // 8):
                s = pl.ds(8 * c, 8)
                rows = [[src[f, r + e, s] for f in range(F)] for e in (-1, 0, 1, 2)]
                beside = [merged[f, s] for f in range(F)]
                for e in range(2):
                    xm, core, xp = rows[e : e + 3]
                    edge = [pltpu.roll(a, 125 - 8 * (r + e), 1) for a in beside]
                    ym = [jnp.where(lane == 0, b, pltpu.roll(a, 1, 1)) for a, b in zip(core, edge)]
                    yp = [jnp.where(lane == 127, b, pltpu.roll(a, 127, 1)) for a, b in zip(core, edge)]
                    rl = jnp.broadcast_to(flow[0, r + e, pl.ds(T, 1)], (8, 128))
                    times = {f: td[n, r + e, s] for n, f in enumerate(TIMED)}
                    out = combine(core, xm, xp, ym, yp, flow[0, r + e, s], flow[1, r + e, s], rl, times)
                    for f in range(F):
                        dst[f, r + e, s] = out[f] * keep[e]

        def pair(i, carry, low=low, time_pair=time_pair, main_pair=main_pair):
            r = low + 2 * i
            time_pair(jnp.minimum(r + 2, E - 2))
            main_pair(r)
            return carry

        for f in range(F):
            merged[f] = jnp.where(lanes() % 8 == 3, side[f, 0], pltpu.roll(side[f, 1], 126, 1))
        if not last:
            for n, f in enumerate(TIMED):
                std[n, 0], std[n, 1] = timed(f, side[f, 0], side[f, 1])
        time_pair(low)
        lax.fori_loop(0, count // 2, pair, 0, unroll=True)
        for p in range(0 if last else 2):
            for c in range(TP // 8):
                s = pl.ds(8 * c, 8)
                core = [side[f, p, s] for f in range(F)]
                xm, xp, ym, yp = ([pltpu.roll(a, by, 1) for a in core] for by in (8, 120, 1, 127))
                rl = jnp.broadcast_to(sflow[0, p, pl.ds(T, 1)], (8, 128))
                times = {f: std[n, p, s] for n, f in enumerate(TIMED)}
                out = combine(core, xm, xp, ym, yp, sflow[0, p, s], sflow[1, p, s], rl, times)
                for f in range(F):
                    side_new[f, p, s] = out[f] * side_ok[p]
        for f in range(F):
            for r in range(R):
                basis[first + k, f * R + r] = dst[f, H + r]


def by_parity(load, *pairs):
    @pl.when(is_odd())
    def _():
        load(*[pair[0] for pair in pairs], *[pair[1] for pair in pairs])

    @pl.when(jnp.logical_not(is_odd()))
    def _():
        load(*[pair[1] for pair in pairs], *[pair[0] for pair in pairs])


def first_kernel(own, even, odd, here, near_even, near_odd, mats, main, pack, basis, flow, sflow, ext0, ext1, side0, side1, td, std, merged):
    half = 0.5 * STEP

    def load(north, flow_north, south, flow_south):
        sides = [slabs_of(ref) for ref in (flow_north, here, flow_south)]
        fill(own, north, south, sides, ext0, side0)
        for j in range(2):
            for r in range(R):
                put(flow, (j, H + r), raw(own, F + j, r), half)
            for q in range(H - 1):
                place = pl.ds(SIDE + (j * (H - 1) + q) * T, T)
                put(flow, (j, 1 + q), flow_north[place, :], half)
                put(flow, (j, H + R + q), flow_south[place, :], half)
        for r in range(R):
            flow[0, H + r, pl.ds(T, 1), :] = own[pl.ds(8 * T * R + r, 1), :] * STEP
        for q in range(H - 1):
            place = pl.ds(SIDE + 2 * (H - 1) * T + q, 1)
            flow[0, 1 + q, pl.ds(T, 1), :] = flow_north[place, :] * STEP
            flow[0, H + R + q, pl.ds(T, 1), :] = flow_south[place, :] * STEP
        sub = lax.broadcasted_iota(jnp.int32, (TP, 128), 0)
        scale = jnp.where(sub == T, STEP, half).astype(jnp.float32)
        slot = lanes() % 8
        for j in range(2):
            sides_of(sflow, j, own_windows(lambda e: flow[j, e], range(1, E - 1)), sides, 1, 2 + j, (1.0, 1.0))
            for p in range(2):
                halo = (slot < 4) if p == 0 else (slot >= 4)
                sflow[j, p] = sflow[j, p] * jnp.where(halo, scale, 1.0)

    by_parity(load, (even, odd), (near_even, near_odd))
    for f in range(F):
        for r in range(R):
            basis[0, f * R + r] = ext0[f, H + r]
    steps(mats, (ext0, ext1), (side0, side1), flow, sflow, td, std, merged, basis, 1)
    for f in range(F):
        for r in range(R):
            main[pl.ds(f * T * R + r, T, stride=R), :] = basis[H, f * R + r, 0:T]
    for g in range(2):
        total = jnp.zeros((TP, 128), jnp.float32)
        for j in range(4 if g == 0 else 2):
            for r in range(R):
                total = total + window(basis[H, (g * 4 + j) * R + r], j * 32 + r * 8)
        pack[g * TP : (g + 1) * TP, :] = total


def products(slabs, pairs):
    def slab(i, sums):
        sums = list(sums)
        for c in range(TP // 8):
            s = pl.ds(8 * c, 8)
            vec = [get(i, s) for get in slabs]
            for e, (a, b) in enumerate(pairs):
                sums[e] = sums[e] + vec[a] * vec[b]
        return tuple(sums)

    zero = jnp.zeros((8, 128), jnp.float32)
    return lax.fori_loop(0, F * R, slab, (zero,) * len(pairs), unroll=2)


def gram_kernel(older, early):
    slabs = [lambda i, s, k=k: older[k, i, s] for k in range(5)]
    for e, value in enumerate(products(slabs, EARLY)):
        early[e] = value


def second_kernel(own, even, odd, here, corner_even, corner_odd, flow, sflow, older, early, mats, basis, gram, ext0, ext1, side0, side1, td, std, merged, rows):

    def load(north, above, south, below):
        fill(own, north, south, [slabs_of(ref) for ref in (above, here, below)], ext0, side0)

    by_parity(load, (even, odd), (corner_even, corner_odd))
    steps(mats, (ext0, ext1), (side0, side1), flow, sflow, td, std, merged, basis, 0)

    late = [pair for pair in PAIRS if pair not in EARLY]
    slabs = [lambda i, s, k=k: older[k, i, s] for k in range(5)] + [lambda i, s, k=k: basis[k, i, s] for k in range(4)]
    sums = dict(zip(late, products(slabs, late)))
    for e, pair in enumerate(EARLY):
        sums[pair] = early[e]
    rows[...] = jnp.zeros((48, 128), jnp.float32)
    for e, pair in enumerate(PAIRS):
        rows[pl.ds(e, 1), :] = jnp.sum(sums[pair], axis=0, keepdims=True)
    total = jnp.sum(rows[...], axis=1, keepdims=True)
    pick = lanes((48, 128)) == lax.broadcasted_iota(jnp.int32, (48, 128), 0)
    line = jnp.sum(jnp.where(pick, total, 0.0), axis=0, keepdims=True)
    gram[...] = jnp.broadcast_to(line, (PEERS, 128))


def plus(a, b):
    return b if a is None else a if b is None else a + b


def minus(a, b):
    return a if b is None else -b if a is None else a - b


def times(a, b):
    return None if a is None or b is None else a * b


def cycle(gram, c):
    q = [c]
    for _ in range(4):
        q.append([None] + q[-1][:-1])
    w = [
        [plus(times(2.0 + 3.0 * SHIFT, a), times(3.0 / SCALE, b)) for a, b in zip(q[k], q[k + 1])]
        for k in range(4)
    ]

    def dot(a, b):
        total = None
        for x, y in zip(a, b):
            total = plus(total, times(x, y))
        return total

    gw = [[dot(gram[i], v) for i in range(NV)] for v in w]
    n = 4
    y = [dot(c, gw[i]) for i in range(n)]
    low, inverse = [[None] * n for _ in range(n)], []
    for j in range(n):
        held = [dot(w[i], gw[j]) for i in range(j, n)]
        for m in range(j):
            scaled = low[j][m] * diag[m]
            held = [v - low[i][m] * scaled for i, v in zip(range(j, n), held)]
        diag = (diag if j else []) + [held[0]]
        inverse.append(1.0 / held[0])
        low[j][j] = 1.0
        for i in range(j + 1, n):
            low[i][j] = held[i - j] * inverse[j]
    for i in range(n):
        for m in range(i):
            y[i] = y[i] - low[i][m] * y[m]
    y = [a * b for a, b in zip(y, inverse)]
    for i in reversed(range(n)):
        for m in range(i + 1, n):
            y[i] = y[i] - low[m][i] * y[m]
    step, rest = [None] * NV, list(c)
    for i in range(n):
        step = [plus(a, times(y[i], b)) for a, b in zip(step, q[i])]
        rest = [minus(a, times(y[i], b)) for a, b in zip(rest, w[i])]
    return step, rest


def last_kernel(parts, older, newer, solution, residual):
    total = jnp.sum(parts[...].reshape(PEERS // 8, 8, 128), axis=0)
    total = jnp.sum(total, axis=0, keepdims=True)
    gram = [[None] * NV for _ in range(NV)]
    for e, (i, j) in enumerate(PAIRS):
        gram[i][j] = gram[j][i] = jnp.broadcast_to(total[:, e : e + 1], (8, 128))
    step1, rest = cycle(gram, [1.0] + [None] * (NV - 1))
    zero = jnp.zeros((8, 128), jnp.float32)
    rest = [zero if a is None else a for a in rest]
    step2, rest = cycle(gram, rest)
    step = [plus(a, b) for a, b in zip(step1, step2)]
    step = [None if a is None else a[0:1] for a in step]
    rest = [a[0:1] for a in rest]

    def slab(i, carry):
        f, r = i // R, i % R
        sol = res = None
        for k in range(NV):
            x = older[k, i, 0:T] if k < 5 else newer[k - 5, i, 0:T]
            if step[k] is not None:
                sol = plus(sol, step[k] * x)
            res = plus(res, rest[k] * x)
        solution[pl.ds(f * T * R + r, T, stride=R), :] = sol
        residual[pl.ds(f * T * R + r, T, stride=R), :] = res
        return carry

    lax.fori_loop(0, F * R, slab, 0)


def call(kernel, args, outs, scratch=(), first=False, final=False):
    space = pltpu.HBM if first else pltpu.VMEM
    args = [pltpu.with_memory_space_constraint(a, space) for a in args]
    make = jax.ShapeDtypeStruct if final else pltpu.VMEM
    kinds = [jnp.bfloat16 if shape[-1] == 2 * TP else jnp.float32 for shape in outs]
    scratch = [pltpu.VMEM(shape, jnp.float32) for shape in scratch]
    return pl.pallas_call(
        kernel,
        out_shape=[make(shape, kind) for shape, kind in zip(outs, kinds)],
        in_specs=[pl.BlockSpec(memory_space=space)] * len(args),
        out_specs=[VM] * len(outs),
        scratch_shapes=scratch + [pltpu.SemaphoreType.DMA((4,))] * first,
        compiler_params=pltpu.CompilerParams(vmem_limit_bytes=24 << 20),
    )(*args)


def trades(across, down):
    even = [(g * down + j, g * down + (j ^ 1)) for g in range(across) for j in range(down)]
    odd = []
    for g in range(across):
        for j in range(down):
            edge = j in (0, down - 1)
            other = j if edge else j + 1 if j % 2 else j - 1
            odd.append((g * down + j, (g ^ 1 if edge else g) * down + other))
    return even, odd


def exchange(rows, pack, behind=()):
    across = lax.axis_size("gx")
    pairs = trades(across, lax.axis_size("gy"))
    axes = ("gx", "gy")
    rows = [lax.ppermute(rows, axes, p) for p in pairs]
    left = lax.ppermute(pack, "gx", [(g, (g + 1) % across) for g in range(across)])
    right = lax.ppermute(pack, "gx", [((g + 1) % across, g) for g in range(across)])
    slot = lax.broadcasted_iota(jnp.int32, pack.shape, 1) % 8
    here = jnp.where(slot < 4, left, right)
    near = [x.at[:SIDE].set(here) for x in behind] or [here, here]
    corners = [lax.ppermute(x, axes, p) for x, p in zip(near, pairs)]
    return *rows, here, *corners


WORK = (
    (F, E, TP, 128),
    (F, E, TP, 128),
    (F, 2, TP, 128),
    (F, 2, TP, 128),
    (len(TIMED), E, TP, 128),
    (len(TIMED), 2, TP, 128),
    (F, TP, 128),
)


def shards(right_side, base_flow, relax):
    rs = right_side.reshape(F * T * R, 128)
    flow = base_flow.reshape(2 * T * R, 128)
    own, to_even, to_odd, pack, mats = call(
        pack_kernel,
        (rs, flow, relax, jnp.asarray(time_matrices())),
        ((8 * T * R + 8, 128), (SIDE + FLOW, 128), (SIDE + FLOW, 128), (SIDE, 128), (2, 2 * TP, 2 * TP)),
        first=True,
    )
    own, pack, older, flows, side_flows = call(
        first_kernel,
        (own, *exchange(rs, pack, (to_even, to_odd)), mats),
        ((F * T * R, 128), (2 * TP, 128), (5, F * R, TP, 128), (2, E, TP, 128), (2, 2, TP, 128)),
        WORK,
    )
    (early,) = call(gram_kernel, (older,), ((len(EARLY), 8, 128),))
    newer, gram = call(
        second_kernel,
        (own, *exchange(own, pack), flows, side_flows, older, early, mats),
        ((4, F * R, TP, 128), (PEERS, 128)),
        WORK + ((48, 128),),
    )
    parts = lax.all_to_all(gram.reshape(PEERS, 1, 128), ("gx", "gy"), 0, 0, tiled=True)
    solution_field, residual = call(
        last_kernel,
        (parts.reshape(PEERS, 128), older, newer),
        ((F * T * R, 128), (F * T * R, 128)),
        final=True,
    )
    return solution_field.reshape(right_side.shape), residual.reshape(right_side.shape)


def solution(mesh):
    placed = (P(None, None, "gy", "gx"), P(None, None, "gy", "gx"), P("gy", "gx"))
    return jax.shard_map(
        shards,
        mesh=mesh,
        in_specs=placed,
        out_specs=(P(None, None, "gy", "gx"), P(None, None, "gy", "gx")),
        check_vma=False,
    )
```

```python
import jax
import jax.numpy as jnp
import numpy as np
from jax import lax
from jax.experimental import pallas as pl
from jax.experimental.pallas import tpu as pltpu
from jax.sharding import PartitionSpec as P

F = 6
T = 33
TP = 40
R = 4
H = 4
E = R + 2 * H
NV = 9
SHIFT = 0.5
SCALE = 0.46
STEP = SCALE / 3.0
MOVE = SCALE * SHIFT
TIMED = (0, 1, 3, 4, 5)
PAIRS = [(i, j) for i in range(NV) for j in range(i, NV)]
EARLY = [(i, j) for i, j in PAIRS if j < 5]
PEERS = 256
ROWS = F * T * R
SIDE = 2 * TP
FLOW = 208


def time_matrices():
    index = np.arange(T, dtype=np.float64)
    diff = index[:, None] - index[None, :]
    sines = np.where(diff == 0.0, 1.0, np.sin(np.pi * diff / T))
    dmat = np.where(diff == 0.0, 0.0, 0.5 * np.where(diff % 2 == 0, 1.0, -1.0) / sines)
    mats = []
    for diagonal in (0.4 * STEP - MOVE, -MOVE):
        full = np.zeros((TP, TP), np.float32)
        full[:T, :T] = 0.8 * STEP * dmat + diagonal * np.eye(T)
        high = full.astype(jnp.bfloat16)
        low = (full - high.astype(np.float32)).astype(jnp.bfloat16)
        top = np.concatenate([high, high], 1)
        bottom = np.concatenate([low, np.zeros_like(low)], 1)
        mats.append(np.concatenate([top, bottom], 0))
    return np.stack(mats)


def lanes(shape=(1, 128)):
    return lax.broadcasted_iota(jnp.int32, shape, len(shape) - 1)


def window(x, place):
    lane = lanes()
    return jnp.where((lane >= place) & (lane < place + 8), pltpu.roll(x, (place + 4) % 128, 1), 0.0)


def raw(ref, f, r):
    return ref[pl.ds(f * T * R + r, T, stride=R), :]


def is_odd():
    return lax.rem(lax.axis_index("gy"), 2) == 1


def pack_kernel(rs, flow, relax, mats_in, message, even, odd, pack, mats, sems):
    rows = F * T * R
    copies = [
        pltpu.make_async_copy(rs, message.at[pl.ds(0, rows)], sems.at[0]),
        pltpu.make_async_copy(flow, message.at[pl.ds(rows, 2 * T * R)], sems.at[1]),
        pltpu.make_async_copy(relax, message.at[pl.ds(8 * T * R, R)], sems.at[2]),
        pltpu.make_async_copy(mats_in, mats, sems.at[3]),
    ]
    for copy in copies:
        copy.start()
    for copy in copies:
        copy.wait()
    for to in (even, odd):
        to[pl.ds(SIDE + FLOW - 8, 8), :] = jnp.zeros((8, 128), jnp.float32)
    for g in range(2):
        total = jnp.zeros((T, 128), jnp.float32)
        for j in range(4):
            for r in range(R):
                total = total + window(raw(message, g * 4 + j, r), j * 32 + r * 8)
        pack[g * TP : g * TP + 32, :] = total[0:32]
        last = jnp.zeros((8, 128), jnp.float32)
        sub = lax.broadcasted_iota(jnp.int32, (8, 128), 0)
        last = jnp.where(sub == 0, jnp.broadcast_to(total[32:33], (8, 128)), last)
        if g == 1:
            extra = jnp.zeros((1, 128), jnp.float32)
            for r in range(R):
                extra = extra + window(message[pl.ds(8 * T * R + r, 1), :], 2 * 32 + r * 8)
            last = jnp.where(sub == 1, jnp.broadcast_to(extra, (8, 128)), last)
        pack[g * TP + 32 : g * TP + 40, :] = last

    def rows_for(to, first):
        for j in range(2):
            for q in range(H - 1):
                to[pl.ds(SIDE + (j * (H - 1) + q) * T, T), :] = raw(message, F + j, first + q)
        for q in range(H - 1):
            to[pl.ds(SIDE + 2 * (H - 1) * T + q, 1), :] = message[pl.ds(8 * T * R + first + q, 1), :]

    @pl.when(is_odd())
    def _():
        rows_for(even, 0)
        rows_for(odd, 1)

    @pl.when(jnp.logical_not(is_odd()))
    def _():
        rows_for(even, 1)
        rows_for(odd, 0)


def put(dst, index, x, scale=None):
    dst[index + (pl.ds(32, 8), slice(None))] = jnp.zeros((8, 128), jnp.float32)
    dst[index + (pl.ds(0, T), slice(None))] = x if scale is None else x * scale


def slabs_of(ref):
    return [ref.at[pl.ds(g * TP, TP)] for g in range(2)]


def sides_of(dst, f, own, sides, g, j, ok):
    lane = lanes()
    north, here, south = (
        pltpu.roll(ref[g][...], (base - 32 * j) % 128, 1) for base, ref in zip((0, 32, 64), sides)
    )
    halo = jnp.where(lane < 32, north, jnp.where(lane < 64, here, south))
    slot = lane % 8
    dst[f, 0] = jnp.where(slot < 4, halo, own) * ok[0]
    dst[f, 1] = jnp.where(slot < 4, own, halo) * ok[1]


def own_windows(slab, rows=range(E)):
    total = jnp.zeros((TP, 128), jnp.float32)
    for e in rows:
        total = total + window(slab(e), e * 8)
    return total


def fill(own, north, south, sides, ext, side):
    ok_north, ok_south, _, _ = masks()
    ok = side_masks((1, 128))
    for f in range(F):
        for r in range(R):
            put(ext, (f, r), raw(north, f, r), ok_north)
            put(ext, (f, H + r), raw(own, f, r))
            put(ext, (f, H + R + r), raw(south, f, r), ok_south)
    for f in range(F):
        sides_of(side, f, own_windows(lambda e: ext[f, e]), sides, f // 4, f % 4, ok)


def masks():
    gx, gy = lax.axis_index("gx"), lax.axis_index("gy")
    north = jnp.where(gy > 0, 1.0, 0.0).astype(jnp.float32)
    south = jnp.where(gy < lax.axis_size("gy") - 1, 1.0, 0.0).astype(jnp.float32)
    west = jnp.where(gx > 0, 1.0, 0.0).astype(jnp.float32)
    east = jnp.where(gx < lax.axis_size("gx") - 1, 1.0, 0.0).astype(jnp.float32)
    return north, south, west, east


def side_masks(shape):
    north, south, west, east = masks()
    lane = lanes(shape)
    row, slot = lane // 8, lane % 8
    rows_ok = jnp.where(row < H, north, jnp.where(row < H + R, 1.0, jnp.where(row < E, south, 0.0)))
    return [rows_ok * jnp.where(slot < 4, west, 1.0), rows_ok * jnp.where(slot < 4, 1.0, east)]


def combine(core, xm, xp, ym, yp, fu, fv, rl, td):
    ex = [a - b for a, b in zip(xp, xm)]
    ey = [a - b for a, b in zip(yp, ym)]
    half = 0.5 * STEP
    carried = {f: td[f] + fu * ex[f] + fv * ey[f] for f in TIMED}
    around = [xp[f] + xm[f] + (yp[f] + ym[f]) for f in range(3)]
    return [
        carried[0] - (0.1 * STEP) * around[0] + half * (ex[2] - ex[3] - ey[4]),
        carried[1] - (0.1 * STEP) * around[1] + half * (ey[2] - ex[4] - ey[5]),
        half * (ex[0] + ey[1]) - (0.2 * STEP) * around[2] + (0.8 * STEP - MOVE) * core[2],
        carried[3] + rl * core[3] - half * ex[0],
        carried[4] + rl * core[4] - (0.5 * half) * (ey[0] + ex[1]),
        carried[5] + rl * core[5] - half * ey[1],
    ]


def steps(mats, exts, slabs, flow, sflow, td, std, merged, outs):
    north, south, _, _ = masks()
    side_ok = side_masks((8, 128))
    lane = lanes((8, 128))

    def timed(f, a, b):
        x = jnp.concatenate([a, b], 1)
        high = x.astype(jnp.bfloat16).astype(jnp.float32)
        both = jnp.concatenate([high, x - high], 0).astype(jnp.bfloat16)
        out = jnp.dot(mats[0 if f < 2 else 1], both, preferred_element_type=jnp.float32)
        out = out[:TP] + out[TP:]
        return out[:, :128], out[:, 128:]

    for k in range(H):
        src, dst = exts[k % 2], exts[1 - k % 2]
        side, side_new = slabs[k % 2], slabs[1 - k % 2]
        low, count = k + 1, E - 2 * (k + 1)
        last = k == H - 1

        def time_pair(r, src=src):
            for n, f in enumerate(TIMED):
                td[n, r], td[n, r + 1] = timed(f, src[f, r], src[f, r + 1])

        def main_pair(r, src=src, dst=dst):
            keep = [jnp.where(e < H, north, jnp.where(e < H + R, jnp.float32(1.0), south)) for e in (r, r + 1)]
            for c in range(TP // 8):
                s = pl.ds(8 * c, 8)
                rows = [[src[f, r + e, s] for f in range(F)] for e in (-1, 0, 1, 2)]
                beside = [merged[f, s] for f in range(F)]
                for e in range(2):
                    xm, core, xp = rows[e : e + 3]
                    edge = [pltpu.roll(a, 125 - 8 * (r + e), 1) for a in beside]
                    ym = [jnp.where(lane == 0, b, pltpu.roll(a, 1, 1)) for a, b in zip(core, edge)]
                    yp = [jnp.where(lane == 127, b, pltpu.roll(a, 127, 1)) for a, b in zip(core, edge)]
                    rl = jnp.broadcast_to(flow[0, r + e, pl.ds(T, 1)], (8, 128))
                    times = {f: td[n, r + e, s] for n, f in enumerate(TIMED)}
                    out = combine(core, xm, xp, ym, yp, flow[0, r + e, s], flow[1, r + e, s], rl, times)
                    for f in range(F):
                        dst[f, r + e, s] = out[f] * keep[e]

        def pair(i, carry, low=low, time_pair=time_pair, main_pair=main_pair):
            r = low + 2 * i
            time_pair(jnp.minimum(r + 2, E - 2))
            main_pair(r)
            return carry

        for f in range(F):
            merged[f] = jnp.where(lanes() % 8 == 3, side[f, 0], pltpu.roll(side[f, 1], 126, 1))
        if not last:
            for n, f in enumerate(TIMED):
                std[n, 0], std[n, 1] = timed(f, side[f, 0], side[f, 1])
        time_pair(low)
        lax.fori_loop(0, count // 2, pair, 0, unroll=True)
        for p in range(0 if last else 2):
            for c in range(TP // 8):
                s = pl.ds(8 * c, 8)
                core = [side[f, p, s] for f in range(F)]
                xm, xp, ym, yp = ([pltpu.roll(a, by, 1) for a in core] for by in (8, 120, 1, 127))
                rl = jnp.broadcast_to(sflow[0, p, pl.ds(T, 1)], (8, 128))
                times = {f: std[n, p, s] for n, f in enumerate(TIMED)}
                out = combine(core, xm, xp, ym, yp, sflow[0, p, s], sflow[1, p, s], rl, times)
                for f in range(F):
                    side_new[f, p, s] = out[f] * side_ok[p]
        for f in range(F):
            for r in range(R):
                outs[k][pl.ds(f * T * R + r, T, stride=R), :] = dst[f, H + r, 0:T]


def by_parity(load, *pairs):
    @pl.when(is_odd())
    def _():
        load(*[pair[0] for pair in pairs], *[pair[1] for pair in pairs])

    @pl.when(jnp.logical_not(is_odd()))
    def _():
        load(*[pair[1] for pair in pairs], *[pair[0] for pair in pairs])


def first_kernel(own, even, odd, here, near_even, near_odd, mats, main, pack, older, flow, sflow, ext0, ext1, side0, side1, td, std, merged):
    half = 0.5 * STEP

    def load(north, flow_north, south, flow_south):
        sides = [slabs_of(ref) for ref in (flow_north, here, flow_south)]
        fill(own, north, south, sides, ext0, side0)
        for j in range(2):
            for r in range(R):
                put(flow, (j, H + r), raw(own, F + j, r), half)
            for q in range(H - 1):
                place = pl.ds(SIDE + (j * (H - 1) + q) * T, T)
                put(flow, (j, 1 + q), flow_north[place, :], half)
                put(flow, (j, H + R + q), flow_south[place, :], half)
        for r in range(R):
            flow[0, H + r, pl.ds(T, 1), :] = own[pl.ds(8 * T * R + r, 1), :] * STEP
        for q in range(H - 1):
            place = pl.ds(SIDE + 2 * (H - 1) * T + q, 1)
            flow[0, 1 + q, pl.ds(T, 1), :] = flow_north[place, :] * STEP
            flow[0, H + R + q, pl.ds(T, 1), :] = flow_south[place, :] * STEP
        sub = lax.broadcasted_iota(jnp.int32, (TP, 128), 0)
        scale = jnp.where(sub == T, STEP, half).astype(jnp.float32)
        slot = lanes() % 8
        for j in range(2):
            sides_of(sflow, j, own_windows(lambda e: flow[j, e], range(1, E - 1)), sides, 1, 2 + j, (1.0, 1.0))
            for p in range(2):
                halo = (slot < 4) if p == 0 else (slot >= 4)
                sflow[j, p] = sflow[j, p] * jnp.where(halo, scale, 1.0)

    by_parity(load, (even, odd), (near_even, near_odd))
    older[0] = own[0:ROWS, :]
    outs = [older.at[k] for k in (1, 2, 3)] + [main]
    steps(mats, (ext0, ext1), (side0, side1), flow, sflow, td, std, merged, outs)
    for g in range(2):
        total = jnp.zeros((TP, 128), jnp.float32)
        for j in range(4 if g == 0 else 2):
            for r in range(R):
                total = total + window(ext0[g * 4 + j, H + r], j * 32 + r * 8)
        pack[g * TP : (g + 1) * TP, :] = total


def products(vectors, pairs):
    def part(i, sums):
        sums = list(sums)
        for c in range(9):
            s = pl.ds(pl.multiple_of(72 * i, 8) + 8 * c, 8)
            vec = {k: get(s) for k, get in vectors.items()}
            for e, (a, b) in enumerate(pairs):
                sums[e] = sums[e] + vec[a] * vec[b]
        return tuple(sums)

    zero = jnp.zeros((8, 128), jnp.float32)
    return lax.fori_loop(0, ROWS // 72, part, (zero,) * len(pairs))


def early_vectors(older, main):
    vectors = {k: lambda s, k=k: older[k, s] for k in range(H)}
    vectors[H] = lambda s: main[s]
    return vectors


def gram_kernel(older, main, early):
    for e, value in enumerate(products(early_vectors(older, main), EARLY)):
        early[e] = value


def second_kernel(own, even, odd, here, corner_even, corner_odd, flow, sflow, older, early, mats, newer, gram, ext0, ext1, side0, side1, td, std, merged, rows):

    def load(north, above, south, below):
        fill(own, north, south, [slabs_of(ref) for ref in (above, here, below)], ext0, side0)

    by_parity(load, (even, odd), (corner_even, corner_odd))
    outs = [newer.at[k] for k in range(4)]
    steps(mats, (ext0, ext1), (side0, side1), flow, sflow, td, std, merged, outs)

    late = [pair for pair in PAIRS if pair not in EARLY]
    vectors = early_vectors(older, own)
    for k in range(4):
        vectors[5 + k] = lambda s, k=k: newer[k, s]
    sums = dict(zip(late, products(vectors, late)))
    for e, pair in enumerate(EARLY):
        sums[pair] = early[e]
    rows[...] = jnp.zeros((48, 128), jnp.float32)
    for e, pair in enumerate(PAIRS):
        rows[pl.ds(e, 1), :] = jnp.sum(sums[pair], axis=0, keepdims=True)
    total = jnp.sum(rows[...], axis=1, keepdims=True)
    pick = lanes((48, 128)) == lax.broadcasted_iota(jnp.int32, (48, 128), 0)
    line = jnp.sum(jnp.where(pick, total, 0.0), axis=0, keepdims=True)
    gram[...] = jnp.broadcast_to(line, (PEERS, 128))


def plus(a, b):
    return b if a is None else a if b is None else a + b


def minus(a, b):
    return a if b is None else -b if a is None else a - b


def times(a, b):
    return None if a is None or b is None else a * b


def cycle(gram, c):
    q = [c]
    for _ in range(4):
        q.append([None] + q[-1][:-1])
    w = [
        [plus(times(2.0 + 3.0 * SHIFT, a), times(3.0 / SCALE, b)) for a, b in zip(q[k], q[k + 1])]
        for k in range(4)
    ]

    def dot(a, b):
        total = None
        for x, y in zip(a, b):
            total = plus(total, times(x, y))
        return total

    gw = [[dot(gram[i], v) for i in range(NV)] for v in w]
    n = 4
    y = [dot(c, gw[i]) for i in range(n)]
    low, inverse = [[None] * n for _ in range(n)], []
    for j in range(n):
        held = [dot(w[i], gw[j]) for i in range(j, n)]
        for m in range(j):
            scaled = low[j][m] * diag[m]
            held = [v - low[i][m] * scaled for i, v in zip(range(j, n), held)]
        diag = (diag if j else []) + [held[0]]
        inverse.append(1.0 / held[0])
        low[j][j] = 1.0
        for i in range(j + 1, n):
            low[i][j] = held[i - j] * inverse[j]
    for i in range(n):
        for m in range(i):
            y[i] = y[i] - low[i][m] * y[m]
    y = [a * b for a, b in zip(y, inverse)]
    for i in reversed(range(n)):
        for m in range(i + 1, n):
            y[i] = y[i] - low[m][i] * y[m]
    step, rest = [None] * NV, list(c)
    for i in range(n):
        step = [plus(a, times(y[i], b)) for a, b in zip(step, q[i])]
        rest = [minus(a, times(y[i], b)) for a, b in zip(rest, w[i])]
    return step, rest


def last_kernel(parts, older, main, newer, solution, residual, sol, res, sems):
    total = jnp.sum(parts[...].reshape(PEERS // 8, 8, 128), axis=0)
    total = jnp.sum(total, axis=0, keepdims=True)
    gram = [[None] * NV for _ in range(NV)]
    for e, (i, j) in enumerate(PAIRS):
        gram[i][j] = gram[j][i] = jnp.broadcast_to(total[:, e : e + 1], (8, 128))
    step1, rest = cycle(gram, [1.0] + [None] * (NV - 1))
    zero = jnp.zeros((8, 128), jnp.float32)
    rest = [zero if a is None else a for a in rest]
    step2, rest = cycle(gram, rest)
    step = [plus(a, b) for a, b in zip(step1, step2)]
    vectors = early_vectors(older, main)
    for k in range(4):
        vectors[5 + k] = lambda s, k=k: newer[k, s]
    copies = []
    third = ROWS // 3
    for p in range(3):

        def part(i, carry, p=p):
            for c in range(11):
                s = pl.ds(pl.multiple_of(p * third + 88 * i, 8) + 8 * c, 8)
                one = two = None
                for k in range(NV):
                    x = vectors[k](s)
                    one = plus(one, times(step[k], x))
                    two = plus(two, rest[k] * x)
                sol[s, :] = one
                res[s, :] = two
            return carry

        lax.fori_loop(0, third // 88, part, 0)
        for n, (src, dst) in enumerate(((sol, solution), (res, residual))):
            s = pl.ds(p * third, third)
            copies.append(pltpu.make_async_copy(src.at[s], dst.at[s], sems.at[2 * p + n]))
            copies[-1].start()
    for copy in copies:
        copy.wait()


def call(kernel, args, outs, scratch=(), first=False, final=False):
    space = pltpu.HBM if first else pltpu.VMEM
    args = [pltpu.with_memory_space_constraint(a, space) for a in args]
    make = pltpu.HBM if final else pltpu.VMEM
    kinds = [jnp.bfloat16 if shape[-1] == 2 * TP else jnp.float32 for shape in outs]
    scratch = [pltpu.VMEM(shape, jnp.float32) for shape in scratch]
    return pl.pallas_call(
        kernel,
        out_shape=[make(shape, kind) for shape, kind in zip(outs, kinds)],
        in_specs=[pl.BlockSpec(memory_space=space)] * len(args),
        out_specs=[pl.BlockSpec(memory_space=make)] * len(outs),
        scratch_shapes=scratch + [pltpu.SemaphoreType.DMA((6,))] * (first or final),
        compiler_params=pltpu.CompilerParams(vmem_limit_bytes=24 << 20),
    )(*args)


def trades(across, down):
    even = [(g * down + j, g * down + (j ^ 1)) for g in range(across) for j in range(down)]
    odd = []
    for g in range(across):
        for j in range(down):
            edge = j in (0, down - 1)
            other = j if edge else j + 1 if j % 2 else j - 1
            odd.append((g * down + j, (g ^ 1 if edge else g) * down + other))
    return even, odd


def exchange(rows, pack, behind=()):
    across = lax.axis_size("gx")
    pairs = trades(across, lax.axis_size("gy"))
    axes = ("gx", "gy")
    rows = [lax.ppermute(rows, axes, p) for p in pairs]
    left = lax.ppermute(pack, "gx", [(g, (g + 1) % across) for g in range(across)])
    right = lax.ppermute(pack, "gx", [((g + 1) % across, g) for g in range(across)])
    slot = lax.broadcasted_iota(jnp.int32, pack.shape, 1) % 8
    here = jnp.where(slot < 4, left, right)
    near = [x.at[:SIDE].set(here) for x in behind] or [here, here]
    corners = [lax.ppermute(x, axes, p) for x, p in zip(near, pairs)]
    return *rows, here, *corners


WORK = (
    (F, E, TP, 128),
    (F, E, TP, 128),
    (F, 2, TP, 128),
    (F, 2, TP, 128),
    (len(TIMED), E, TP, 128),
    (len(TIMED), 2, TP, 128),
    (F, TP, 128),
)


def shards(right_side, base_flow, relax):
    rs = right_side.reshape(F * T * R, 128)
    flow = base_flow.reshape(2 * T * R, 128)
    own, to_even, to_odd, pack, mats = call(
        pack_kernel,
        (rs, flow, relax, jnp.asarray(time_matrices())),
        ((8 * T * R + 8, 128), (SIDE + FLOW, 128), (SIDE + FLOW, 128), (SIDE, 128), (2, 2 * TP, 2 * TP)),
        first=True,
    )
    main, pack, older, flows, side_flows = call(
        first_kernel,
        (own, *exchange(rs, pack, (to_even, to_odd)), mats),
        ((ROWS, 128), (SIDE, 128), (H, ROWS, 128), (2, E, TP, 128), (2, 2, TP, 128)),
        WORK,
    )
    (early,) = call(gram_kernel, (older, main), ((len(EARLY), 8, 128),))
    newer, gram = call(
        second_kernel,
        (main, *exchange(main, pack), flows, side_flows, older, early, mats),
        ((4, ROWS, 128), (PEERS, 128)),
        WORK + ((48, 128),),
    )
    parts = lax.all_to_all(gram.reshape(PEERS, 1, 128), ("gx", "gy"), 0, 0, tiled=True)
    solution_field, residual = call(
        last_kernel,
        (parts.reshape(PEERS, 128), older, main, newer),
        ((ROWS, 128), (ROWS, 128)),
        ((ROWS, 128), (ROWS, 128)),
        final=True,
    )
    return solution_field.reshape(right_side.shape), residual.reshape(right_side.shape)


def solution(mesh):
    placed = (P(None, None, "gy", "gx"), P(None, None, "gy", "gx"), P("gy", "gx"))
    return jax.shard_map(
        shards,
        mesh=mesh,
        in_specs=placed,
        out_specs=(P(None, None, "gy", "gx"), P(None, None, "gy", "gx")),
        check_vma=False,
    )
```

```python
import jax
import jax.numpy as jnp
import numpy as np
from jax import lax
from jax.experimental import pallas as pl
from jax.experimental.pallas import tpu as pltpu
from jax.sharding import PartitionSpec as P

F = 6
T = 33
TP = 40
R = 4
H = 4
E = R + 2 * H
NV = 9
SHIFT = 0.5
SCALE = 0.46
STEP = SCALE / 3.0
MOVE = SCALE * SHIFT
TIMED = (0, 1, 3, 4, 5)
PAIRS = [(i, j) for i in range(NV) for j in range(i, NV)]
EARLY = [(i, j) for i, j in PAIRS if j < 5]
PEERS = 256
ROWS = F * T * R
SIDE = 2 * TP
FLOW = 208


def time_matrices():
    index = np.arange(T, dtype=np.float64)
    diff = index[:, None] - index[None, :]
    sines = np.where(diff == 0.0, 1.0, np.sin(np.pi * diff / T))
    dmat = np.where(diff == 0.0, 0.0, 0.5 * np.where(diff % 2 == 0, 1.0, -1.0) / sines)
    mats = []
    for diagonal in (0.4 * STEP - MOVE, -MOVE):
        full = np.zeros((TP, TP), np.float32)
        full[:T, :T] = 0.8 * STEP * dmat + diagonal * np.eye(T)
        high = full.astype(jnp.bfloat16)
        low = (full - high.astype(np.float32)).astype(jnp.bfloat16)
        top = np.concatenate([high, high], 1)
        bottom = np.concatenate([low, np.zeros_like(low)], 1)
        mats.append(np.concatenate([top, bottom], 0))
    return np.stack(mats)


def lanes(shape=(1, 128)):
    return lax.broadcasted_iota(jnp.int32, shape, len(shape) - 1)


def window(x, place):
    lane = lanes()
    return jnp.where((lane >= place) & (lane < place + 8), pltpu.roll(x, (place + 4) % 128, 1), 0.0)


def raw(ref, f, r):
    return ref[pl.ds(f * T * R + r, T, stride=R), :]


def is_odd():
    return lax.rem(lax.axis_index("gy"), 2) == 1


def pack_kernel(rs, flow, relax, mats_in, message, even, odd, pack, mats, sems):
    rows = F * T * R
    copies = [
        pltpu.make_async_copy(rs, message.at[pl.ds(0, rows)], sems.at[0]),
        pltpu.make_async_copy(flow, message.at[pl.ds(rows, 2 * T * R)], sems.at[1]),
        pltpu.make_async_copy(relax, message.at[pl.ds(8 * T * R, R)], sems.at[2]),
        pltpu.make_async_copy(mats_in, mats, sems.at[3]),
    ]
    for copy in copies:
        copy.start()
    for copy in copies:
        copy.wait()
    for to in (even, odd):
        to[pl.ds(SIDE + FLOW - 8, 8), :] = jnp.zeros((8, 128), jnp.float32)
    for g in range(2):
        total = jnp.zeros((T, 128), jnp.float32)
        for j in range(4):
            for r in range(R):
                total = total + window(raw(message, g * 4 + j, r), j * 32 + r * 8)
        pack[g * TP : g * TP + 32, :] = total[0:32]
        last = jnp.zeros((8, 128), jnp.float32)
        sub = lax.broadcasted_iota(jnp.int32, (8, 128), 0)
        last = jnp.where(sub == 0, jnp.broadcast_to(total[32:33], (8, 128)), last)
        if g == 1:
            extra = jnp.zeros((1, 128), jnp.float32)
            for r in range(R):
                extra = extra + window(message[pl.ds(8 * T * R + r, 1), :], 2 * 32 + r * 8)
            last = jnp.where(sub == 1, jnp.broadcast_to(extra, (8, 128)), last)
        pack[g * TP + 32 : g * TP + 40, :] = last

    def rows_for(to, first):
        for j in range(2):
            for q in range(H - 1):
                to[pl.ds(SIDE + (j * (H - 1) + q) * T, T), :] = raw(message, F + j, first + q)
        for q in range(H - 1):
            to[pl.ds(SIDE + 2 * (H - 1) * T + q, 1), :] = message[pl.ds(8 * T * R + first + q, 1), :]

    @pl.when(is_odd())
    def _():
        rows_for(even, 0)
        rows_for(odd, 1)

    @pl.when(jnp.logical_not(is_odd()))
    def _():
        rows_for(even, 1)
        rows_for(odd, 0)


def put(dst, index, x, scale=None):
    dst[index + (pl.ds(32, 8), slice(None))] = jnp.zeros((8, 128), jnp.float32)
    dst[index + (pl.ds(0, T), slice(None))] = x if scale is None else x * scale


def slabs_of(ref):
    return [ref.at[pl.ds(g * TP, TP)] for g in range(2)]


def sides_of(dst, f, own, sides, g, j, ok):
    lane = lanes()
    north, here, south = (
        pltpu.roll(ref[g][...], (base - 32 * j) % 128, 1) for base, ref in zip((0, 32, 64), sides)
    )
    halo = jnp.where(lane < 32, north, jnp.where(lane < 64, here, south))
    slot = lane % 8
    dst[f, 0] = jnp.where(slot < 4, halo, own) * ok[0]
    dst[f, 1] = jnp.where(slot < 4, own, halo) * ok[1]


def own_windows(slab, pack, f, scale=None):
    lane = lanes()
    here = pltpu.roll(pack[pl.ds(f // 4 * TP, TP)], (8 * H - 32 * (f % 4)) % 128, 1)
    total = jnp.where((lane >= 8 * H) & (lane < 8 * (H + R)), here if scale is None else here * scale, 0.0)
    for e in range(1, E - 1):
        if not H <= e < H + R:
            total = total + window(slab(e), e * 8)
    return total


def fill(own, pack, north, south, sides, ext, side):
    ok_north, ok_south, _, _ = masks()
    ok = side_masks((1, 128))
    for f in range(F):
        for r in range(R):
            put(ext, (f, r), raw(north, f, r), ok_north)
            put(ext, (f, H + r), raw(own, f, r))
            put(ext, (f, H + R + r), raw(south, f, r), ok_south)
    for f in range(F):
        sides_of(side, f, own_windows(lambda e: ext[f, e], pack, f), sides, f // 4, f % 4, ok)


def masks():
    gx, gy = lax.axis_index("gx"), lax.axis_index("gy")
    north = jnp.where(gy > 0, 1.0, 0.0).astype(jnp.float32)
    south = jnp.where(gy < lax.axis_size("gy") - 1, 1.0, 0.0).astype(jnp.float32)
    west = jnp.where(gx > 0, 1.0, 0.0).astype(jnp.float32)
    east = jnp.where(gx < lax.axis_size("gx") - 1, 1.0, 0.0).astype(jnp.float32)
    return north, south, west, east


def side_masks(shape):
    north, south, west, east = masks()
    lane = lanes(shape)
    row, slot = lane // 8, lane % 8
    rows_ok = jnp.where(row < H, north, jnp.where(row < H + R, 1.0, jnp.where(row < E, south, 0.0)))
    return [rows_ok * jnp.where(slot < 4, west, 1.0), rows_ok * jnp.where(slot < 4, 1.0, east)]


def combine(core, xm, xp, ym, yp, fu, fv, rl, td):
    ex = [a - b for a, b in zip(xp, xm)]
    ey = [a - b for a, b in zip(yp, ym)]
    half = 0.5 * STEP
    carried = {f: td[f] + fu * ex[f] + fv * ey[f] for f in TIMED}
    around = [xp[f] + xm[f] + (yp[f] + ym[f]) for f in range(3)]
    return [
        carried[0] - (0.1 * STEP) * around[0] + half * (ex[2] - ex[3] - ey[4]),
        carried[1] - (0.1 * STEP) * around[1] + half * (ey[2] - ex[4] - ey[5]),
        half * (ex[0] + ey[1]) - (0.2 * STEP) * around[2] + (0.8 * STEP - MOVE) * core[2],
        carried[3] + rl * core[3] - half * ex[0],
        carried[4] + rl * core[4] - (0.5 * half) * (ey[0] + ex[1]),
        carried[5] + rl * core[5] - half * ey[1],
    ]


def steps(mats, exts, slabs, flow, sflow, td, std, merged, outs):
    north, south, _, _ = masks()
    side_ok = side_masks((8, 128))
    lane = lanes((8, 128))

    def timed(f, a, b):
        x = jnp.concatenate([a, b], 1)
        high = x.astype(jnp.bfloat16).astype(jnp.float32)
        both = jnp.concatenate([high, x - high], 0).astype(jnp.bfloat16)
        out = jnp.dot(mats[0 if f < 2 else 1], both, preferred_element_type=jnp.float32)
        out = out[:TP] + out[TP:]
        return out[:, :128], out[:, 128:]

    for k in range(H):
        src, dst = exts[k % 2], exts[1 - k % 2]
        side, side_new = slabs[k % 2], slabs[1 - k % 2]
        low, count = k + 1, E - 2 * (k + 1)
        last = k == H - 1

        def time_pair(r, src=src):
            for n, f in enumerate(TIMED):
                td[n, r], td[n, r + 1] = timed(f, src[f, r], src[f, r + 1])

        def main_pair(r, src=src, dst=dst):
            for c in range(TP // 8):
                s = pl.ds(8 * c, 8)
                rows = [[src[f, r + e, s] for f in range(F)] for e in (-1, 0, 1, 2)]
                beside = [merged[f, s] for f in range(F)]
                for e in range(2):
                    xm, core, xp = rows[e : e + 3]
                    edge = [pltpu.roll(a, 125 - 8 * (r + e), 1) for a in beside]
                    ym = [jnp.where(lane == 0, b, pltpu.roll(a, 1, 1)) for a, b in zip(core, edge)]
                    yp = [jnp.where(lane == 127, b, pltpu.roll(a, 127, 1)) for a, b in zip(core, edge)]
                    rl = jnp.broadcast_to(flow[0, r + e, pl.ds(T, 1)], (8, 128))
                    times = {f: td[n, r + e, s] for n, f in enumerate(TIMED)}
                    out = combine(core, xm, xp, ym, yp, flow[0, r + e, s], flow[1, r + e, s], rl, times)
                    for f in range(F):
                        inside = H <= r + e < H + R
                        dst[f, r + e, s] = out[f] if inside else out[f] * (north if r + e < H else south)

        for f in range(F):
            merged[f] = jnp.where(lanes() % 8 == 3, side[f, 0], pltpu.roll(side[f, 1], 126, 1))
        if not last:
            for n, f in enumerate(TIMED):
                std[n, 0], std[n, 1] = timed(f, side[f, 0], side[f, 1])
        time_pair(low)
        for i in range(count // 2):
            if i + 1 < count // 2:
                time_pair(low + 2 * i + 2)
            main_pair(low + 2 * i)
        for p in range(0 if last else 2):
            for c in range(TP // 8):
                s = pl.ds(8 * c, 8)
                core = [side[f, p, s] for f in range(F)]
                xm, xp, ym, yp = ([pltpu.roll(a, by, 1) for a in core] for by in (8, 120, 1, 127))
                rl = jnp.broadcast_to(sflow[0, p, pl.ds(T, 1)], (8, 128))
                times = {f: std[n, p, s] for n, f in enumerate(TIMED)}
                out = combine(core, xm, xp, ym, yp, sflow[0, p, s], sflow[1, p, s], rl, times)
                for f in range(F):
                    side_new[f, p, s] = out[f] * side_ok[p]
        for f in range(F):
            for r in range(R):
                outs[k][pl.ds(f * T * R + r, T, stride=R), :] = dst[f, H + r, 0:T]


def by_parity(load, *pairs):
    @pl.when(is_odd())
    def _():
        load(*[pair[0] for pair in pairs], *[pair[1] for pair in pairs])

    @pl.when(jnp.logical_not(is_odd()))
    def _():
        load(*[pair[1] for pair in pairs], *[pair[0] for pair in pairs])


def first_kernel(own, own_pack, even, odd, here, near_even, near_odd, mats, main, pack, older, flow, sflow, ext0, ext1, side0, side1, td, std, merged):
    half = 0.5 * STEP

    def load(north, flow_north, south, flow_south):
        sides = [slabs_of(ref) for ref in (flow_north, here, flow_south)]
        fill(own, own_pack, north, south, sides, ext0, side0)
        for j in range(2):
            for r in range(R):
                put(flow, (j, H + r), raw(own, F + j, r), half)
            for q in range(H - 1):
                place = pl.ds(SIDE + (j * (H - 1) + q) * T, T)
                put(flow, (j, 1 + q), flow_north[place, :], half)
                put(flow, (j, H + R + q), flow_south[place, :], half)
        for r in range(R):
            flow[0, H + r, pl.ds(T, 1), :] = own[pl.ds(8 * T * R + r, 1), :] * STEP
        for q in range(H - 1):
            place = pl.ds(SIDE + 2 * (H - 1) * T + q, 1)
            flow[0, 1 + q, pl.ds(T, 1), :] = flow_north[place, :] * STEP
            flow[0, H + R + q, pl.ds(T, 1), :] = flow_south[place, :] * STEP
        sub = lax.broadcasted_iota(jnp.int32, (TP, 128), 0)
        scale = jnp.where(sub == T, STEP, half).astype(jnp.float32)
        slot = lanes() % 8
        for j in range(2):
            sides_of(sflow, j, own_windows(lambda e: flow[j, e], own_pack, F + j, scale), sides, 1, 2 + j, (1.0, 1.0))
            for p in range(2):
                halo = (slot < 4) if p == 0 else (slot >= 4)
                sflow[j, p] = sflow[j, p] * jnp.where(halo, scale, 1.0)

    by_parity(load, (even, odd), (near_even, near_odd))
    older[0] = own[0:ROWS, :]
    outs = [older.at[k] for k in (1, 2, 3)] + [main]
    steps(mats, (ext0, ext1), (side0, side1), flow, sflow, td, std, merged, outs)
    for g in range(2):
        total = jnp.zeros((TP, 128), jnp.float32)
        for j in range(4 if g == 0 else 2):
            for r in range(R):
                total = total + window(ext0[g * 4 + j, H + r], j * 32 + r * 8)
        pack[g * TP : (g + 1) * TP, :] = total


def products(vectors, pairs):
    def part(i, sums):
        sums = list(sums)
        for c in range(9):
            s = pl.ds(pl.multiple_of(72 * i, 8) + 8 * c, 8)
            vec = {k: get(s) for k, get in vectors.items()}
            for e, (a, b) in enumerate(pairs):
                sums[e] = sums[e] + vec[a] * vec[b]
        return tuple(sums)

    zero = jnp.zeros((8, 128), jnp.float32)
    return lax.fori_loop(0, ROWS // 72, part, (zero,) * len(pairs))


def early_vectors(older, main):
    vectors = {k: lambda s, k=k: older[k, s] for k in range(H)}
    vectors[H] = lambda s: main[s]
    return vectors


def gram_kernel(older, main, early):
    for e, value in enumerate(products(early_vectors(older, main), EARLY)):
        early[e] = value


def second_kernel(own, own_pack, even, odd, here, corner_even, corner_odd, flow, sflow, older, early, mats, newer, gram, ext0, ext1, side0, side1, td, std, merged, rows):

    def load(north, above, south, below):
        fill(own, own_pack, north, south, [slabs_of(ref) for ref in (above, here, below)], ext0, side0)

    by_parity(load, (even, odd), (corner_even, corner_odd))
    outs = [newer.at[k] for k in range(4)]
    steps(mats, (ext0, ext1), (side0, side1), flow, sflow, td, std, merged, outs)

    late = [pair for pair in PAIRS if pair not in EARLY]
    vectors = early_vectors(older, own)
    for k in range(4):
        vectors[5 + k] = lambda s, k=k: newer[k, s]
    sums = dict(zip(late, products(vectors, late)))
    for e, pair in enumerate(EARLY):
        sums[pair] = early[e]
    rows[...] = jnp.zeros((48, 128), jnp.float32)
    for e, pair in enumerate(PAIRS):
        rows[pl.ds(e, 1), :] = jnp.sum(sums[pair], axis=0, keepdims=True)
    total = jnp.sum(rows[...], axis=1, keepdims=True)
    pick = lanes((48, 128)) == lax.broadcasted_iota(jnp.int32, (48, 128), 0)
    line = jnp.sum(jnp.where(pick, total, 0.0), axis=0, keepdims=True)
    gram[...] = jnp.broadcast_to(line, (PEERS, 128))


def plus(a, b):
    return b if a is None else a if b is None else a + b


def minus(a, b):
    return a if b is None else -b if a is None else a - b


def times(a, b):
    return None if a is None or b is None else a * b


def cycle(gram, c):
    q = [c]
    for _ in range(4):
        q.append([None] + q[-1][:-1])
    w = [
        [plus(times(2.0 + 3.0 * SHIFT, a), times(3.0 / SCALE, b)) for a, b in zip(q[k], q[k + 1])]
        for k in range(4)
    ]

    def dot(a, b):
        total = None
        for x, y in zip(a, b):
            total = plus(total, times(x, y))
        return total

    gw = [[dot(gram[i], v) for i in range(NV)] for v in w]
    n = 4
    y = [dot(c, gw[i]) for i in range(n)]
    low, inverse = [[None] * n for _ in range(n)], []
    for j in range(n):
        held = [dot(w[i], gw[j]) for i in range(j, n)]
        for m in range(j):
            scaled = low[j][m] * diag[m]
            held = [v - low[i][m] * scaled for i, v in zip(range(j, n), held)]
        diag = (diag if j else []) + [held[0]]
        inverse.append(1.0 / held[0])
        low[j][j] = 1.0
        for i in range(j + 1, n):
            low[i][j] = held[i - j] * inverse[j]
    for i in range(n):
        for m in range(i):
            y[i] = y[i] - low[i][m] * y[m]
    y = [a * b for a, b in zip(y, inverse)]
    for i in reversed(range(n)):
        for m in range(i + 1, n):
            y[i] = y[i] - low[m][i] * y[m]
    step, rest = [None] * NV, list(c)
    for i in range(n):
        step = [plus(a, times(y[i], b)) for a, b in zip(step, q[i])]
        rest = [minus(a, times(y[i], b)) for a, b in zip(rest, w[i])]
    return step, rest


def last_kernel(parts, older, main, newer, solution, residual, sol, res, sems):
    total = jnp.sum(parts[...].reshape(PEERS // 8, 8, 128), axis=0)
    total = jnp.sum(total, axis=0, keepdims=True)
    gram = [[None] * NV for _ in range(NV)]
    for e, (i, j) in enumerate(PAIRS):
        gram[i][j] = gram[j][i] = jnp.broadcast_to(total[:, e : e + 1], (8, 128))
    step1, rest = cycle(gram, [1.0] + [None] * (NV - 1))
    zero = jnp.zeros((8, 128), jnp.float32)
    rest = [zero if a is None else a for a in rest]
    step2, rest = cycle(gram, rest)
    step = [plus(a, b) for a, b in zip(step1, step2)]
    vectors = early_vectors(older, main)
    for k in range(4):
        vectors[5 + k] = lambda s, k=k: newer[k, s]
    copies = []
    third = ROWS // 3
    for p in range(3):

        def part(i, carry, p=p):
            for c in range(11):
                s = pl.ds(pl.multiple_of(p * third + 88 * i, 8) + 8 * c, 8)
                one = two = None
                for k in range(NV):
                    x = vectors[k](s)
                    one = plus(one, times(step[k], x))
                    two = plus(two, rest[k] * x)
                sol[s, :] = one
                res[s, :] = two
            return carry

        lax.fori_loop(0, third // 88, part, 0)
        for n, (src, dst) in enumerate(((sol, solution), (res, residual))):
            s = pl.ds(p * third, third)
            copies.append(pltpu.make_async_copy(src.at[s], dst.at[s], sems.at[2 * p + n]))
            copies[-1].start()
    for copy in copies:
        copy.wait()


def call(kernel, args, outs, scratch=(), first=False, final=False):
    space = pltpu.HBM if first else pltpu.VMEM
    args = [pltpu.with_memory_space_constraint(a, space) for a in args]
    make = pltpu.HBM if final else pltpu.VMEM
    kinds = [jnp.bfloat16 if shape[-1] == 2 * TP else jnp.float32 for shape in outs]
    scratch = [pltpu.VMEM(shape, jnp.float32) for shape in scratch]
    return pl.pallas_call(
        kernel,
        out_shape=[make(shape, kind) for shape, kind in zip(outs, kinds)],
        in_specs=[pl.BlockSpec(memory_space=space)] * len(args),
        out_specs=[pl.BlockSpec(memory_space=make)] * len(outs),
        scratch_shapes=scratch + [pltpu.SemaphoreType.DMA((6,))] * (first or final),
        compiler_params=pltpu.CompilerParams(vmem_limit_bytes=24 << 20),
    )(*args)


def trades(across, down):
    even = [(g * down + j, g * down + (j ^ 1)) for g in range(across) for j in range(down)]
    odd = []
    for g in range(across):
        for j in range(down):
            edge = j in (0, down - 1)
            other = j if edge else j + 1 if j % 2 else j - 1
            odd.append((g * down + j, (g ^ 1 if edge else g) * down + other))
    return even, odd


def exchange(rows, pack, behind=()):
    across = lax.axis_size("gx")
    pairs = trades(across, lax.axis_size("gy"))
    axes = ("gx", "gy")
    rows = [lax.ppermute(rows, axes, p) for p in pairs]
    left = lax.ppermute(pack, "gx", [(g, (g + 1) % across) for g in range(across)])
    right = lax.ppermute(pack, "gx", [((g + 1) % across, g) for g in range(across)])
    slot = lax.broadcasted_iota(jnp.int32, pack.shape, 1) % 8
    here = jnp.where(slot < 4, left, right)
    near = [x.at[:SIDE].set(here) for x in behind] or [here, here]
    corners = [lax.ppermute(x, axes, p) for x, p in zip(near, pairs)]
    return *rows, here, *corners


WORK = (
    (F, E, TP, 128),
    (F, E, TP, 128),
    (F, 2, TP, 128),
    (F, 2, TP, 128),
    (len(TIMED), E, TP, 128),
    (len(TIMED), 2, TP, 128),
    (F, TP, 128),
)


def shards(right_side, base_flow, relax):
    rs = right_side.reshape(F * T * R, 128)
    flow = base_flow.reshape(2 * T * R, 128)
    own, to_even, to_odd, pack, mats = call(
        pack_kernel,
        (rs, flow, relax, jnp.asarray(time_matrices())),
        ((8 * T * R + 8, 128), (SIDE + FLOW, 128), (SIDE + FLOW, 128), (SIDE, 128), (2, 2 * TP, 2 * TP)),
        first=True,
    )
    main, pack, older, flows, side_flows = call(
        first_kernel,
        (own, pack, *exchange(rs, pack, (to_even, to_odd)), mats),
        ((ROWS, 128), (SIDE, 128), (H, ROWS, 128), (2, E, TP, 128), (2, 2, TP, 128)),
        WORK,
    )
    (early,) = call(gram_kernel, (older, main), ((len(EARLY), 8, 128),))
    newer, gram = call(
        second_kernel,
        (main, pack, *exchange(main, pack), flows, side_flows, older, early, mats),
        ((4, ROWS, 128), (PEERS, 128)),
        WORK + ((48, 128),),
    )
    parts = lax.all_to_all(gram.reshape(PEERS, 1, 128), ("gx", "gy"), 0, 0, tiled=True)
    solution_field, residual = call(
        last_kernel,
        (parts.reshape(PEERS, 128), older, main, newer),
        ((ROWS, 128), (ROWS, 128)),
        ((ROWS, 128), (ROWS, 128)),
        final=True,
    )
    return solution_field.reshape(right_side.shape), residual.reshape(right_side.shape)


def solution(mesh):
    placed = (P(None, None, "gy", "gx"), P(None, None, "gy", "gx"), P("gy", "gx"))
    return jax.shard_map(
        shards,
        mesh=mesh,
        in_specs=placed,
        out_specs=(P(None, None, "gy", "gx"), P(None, None, "gy", "gx")),
        check_vma=False,
    )
```

```python
import jax
import jax.numpy as jnp
import numpy as np
from jax import lax
from jax.experimental import pallas as pl
from jax.experimental.pallas import tpu as pltpu
from jax.sharding import PartitionSpec as P

F = 6
T = 33
TP = 40
R = 4
H = 4
E = R + 2 * H
NV = 9
SHIFT = 0.5
SCALE = 0.46
STEP = SCALE / 3.0
MOVE = SCALE * SHIFT
TIMED = (0, 1, 3, 4, 5)
PAIRS = [(i, j) for i in range(NV) for j in range(i, NV)]
EARLY = [(i, j) for i, j in PAIRS if j < 5]
PEERS = 256
ROWS = F * T * R
SIDE = 2 * TP
FLOW = 208


def time_matrices():
    index = np.arange(T, dtype=np.float64)
    diff = index[:, None] - index[None, :]
    sines = np.where(diff == 0.0, 1.0, np.sin(np.pi * diff / T))
    dmat = np.where(diff == 0.0, 0.0, 0.5 * np.where(diff % 2 == 0, 1.0, -1.0) / sines)
    mats = []
    for diagonal in (0.4 * STEP - MOVE, -MOVE):
        full = np.zeros((TP, TP), np.float32)
        full[:T, :T] = 0.8 * STEP * dmat + diagonal * np.eye(T)
        high = full.astype(jnp.bfloat16)
        low = (full - high.astype(np.float32)).astype(jnp.bfloat16)
        top = np.concatenate([high, high], 1)
        bottom = np.concatenate([low, np.zeros_like(low)], 1)
        mats.append(np.concatenate([top, bottom], 0))
    return np.stack(mats)


def lanes(shape=(1, 128)):
    return lax.broadcasted_iota(jnp.int32, shape, len(shape) - 1)


def window(x, place):
    lane = lanes()
    return jnp.where((lane >= place) & (lane < place + 8), pltpu.roll(x, (place + 4) % 128, 1), 0.0)


def raw(ref, f, r):
    return ref[pl.ds(f * T * R + r, T, stride=R), :]


def is_odd():
    return lax.rem(lax.axis_index("gy"), 2) == 1


def pack_kernel(rs, flow, relax, mats_in, message, even, odd, pack, mats, sems):
    rows = F * T * R
    copies = [
        pltpu.make_async_copy(rs, message.at[pl.ds(0, rows)], sems.at[0]),
        pltpu.make_async_copy(flow, message.at[pl.ds(rows, 2 * T * R)], sems.at[1]),
        pltpu.make_async_copy(relax, message.at[pl.ds(8 * T * R, R)], sems.at[2]),
        pltpu.make_async_copy(mats_in, mats, sems.at[3]),
    ]
    for copy in copies:
        copy.start()
    for copy in copies:
        copy.wait()
    for to in (even, odd):
        to[pl.ds(SIDE + FLOW - 8, 8), :] = jnp.zeros((8, 128), jnp.float32)
    for g in range(2):
        total = jnp.zeros((T, 128), jnp.float32)
        for j in range(4):
            for r in range(R):
                total = total + window(raw(message, g * 4 + j, r), j * 32 + r * 8)
        pack[g * TP : g * TP + 32, :] = total[0:32]
        last = jnp.zeros((8, 128), jnp.float32)
        sub = lax.broadcasted_iota(jnp.int32, (8, 128), 0)
        last = jnp.where(sub == 0, jnp.broadcast_to(total[32:33], (8, 128)), last)
        if g == 1:
            extra = jnp.zeros((1, 128), jnp.float32)
            for r in range(R):
                extra = extra + window(message[pl.ds(8 * T * R + r, 1), :], 2 * 32 + r * 8)
            last = jnp.where(sub == 1, jnp.broadcast_to(extra, (8, 128)), last)
        pack[g * TP + 32 : g * TP + 40, :] = last

    def rows_for(to, first):
        for j in range(2):
            for q in range(H - 1):
                to[pl.ds(SIDE + (j * (H - 1) + q) * T, T), :] = raw(message, F + j, first + q)
        for q in range(H - 1):
            to[pl.ds(SIDE + 2 * (H - 1) * T + q, 1), :] = message[pl.ds(8 * T * R + first + q, 1), :]

    @pl.when(is_odd())
    def _():
        rows_for(even, 0)
        rows_for(odd, 1)

    @pl.when(jnp.logical_not(is_odd()))
    def _():
        rows_for(even, 1)
        rows_for(odd, 0)


def put(dst, index, x, scale=None):
    dst[index + (pl.ds(32, 8), slice(None))] = jnp.zeros((8, 128), jnp.float32)
    dst[index + (pl.ds(0, T), slice(None))] = x if scale is None else x * scale


def slabs_of(ref):
    return [ref.at[pl.ds(g * TP, TP)] for g in range(2)]


def sides_of(dst, f, own, sides, g, j, ok):
    lane = lanes()
    north, here, south = (
        pltpu.roll(ref[g][...], (base - 32 * j) % 128, 1) for base, ref in zip((0, 32, 64), sides)
    )
    halo = jnp.where(lane < 32, north, jnp.where(lane < 64, here, south))
    slot = lane % 8
    dst[f, 0] = jnp.where(slot < 4, halo, own) * ok[0]
    dst[f, 1] = jnp.where(slot < 4, own, halo) * ok[1]


def own_windows(slab, pack, f, scale=None):
    lane = lanes()
    here = pltpu.roll(pack[pl.ds(f // 4 * TP, TP)], (8 * H - 32 * (f % 4)) % 128, 1)
    total = jnp.where((lane >= 8 * H) & (lane < 8 * (H + R)), here if scale is None else here * scale, 0.0)
    for e in range(1, E - 1):
        if not H <= e < H + R:
            total = total + window(slab(e), e * 8)
    return total


def fill(own, pack, north, south, sides, ext, side):
    ok_north, ok_south, _, _ = masks()
    ok = side_masks((1, 128))
    for f in range(F):
        for r in range(R):
            put(ext, (f, r), raw(north, f, r), ok_north)
            put(ext, (f, H + r), raw(own, f, r))
            put(ext, (f, H + R + r), raw(south, f, r), ok_south)
    for f in range(F):
        sides_of(side, f, own_windows(lambda e: ext[f, e], pack, f), sides, f // 4, f % 4, ok)


def masks():
    gx, gy = lax.axis_index("gx"), lax.axis_index("gy")
    north = jnp.where(gy > 0, 1.0, 0.0).astype(jnp.float32)
    south = jnp.where(gy < lax.axis_size("gy") - 1, 1.0, 0.0).astype(jnp.float32)
    west = jnp.where(gx > 0, 1.0, 0.0).astype(jnp.float32)
    east = jnp.where(gx < lax.axis_size("gx") - 1, 1.0, 0.0).astype(jnp.float32)
    return north, south, west, east


def side_masks(shape):
    north, south, west, east = masks()
    lane = lanes(shape)
    row, slot = lane // 8, lane % 8
    rows_ok = jnp.where(row < H, north, jnp.where(row < H + R, 1.0, jnp.where(row < E, south, 0.0)))
    return [rows_ok * jnp.where(slot < 4, west, 1.0), rows_ok * jnp.where(slot < 4, 1.0, east)]


def combine(core, xm, xp, ym, yp, fu, fv, rl, td):
    ex = [a - b for a, b in zip(xp, xm)]
    ey = [a - b for a, b in zip(yp, ym)]
    half = 0.5 * STEP
    carried = {f: td[f] + fu * ex[f] + fv * ey[f] for f in TIMED}
    around = [xp[f] + xm[f] + (yp[f] + ym[f]) for f in range(3)]
    return [
        carried[0] - (0.1 * STEP) * around[0] + half * (ex[2] - ex[3] - ey[4]),
        carried[1] - (0.1 * STEP) * around[1] + half * (ey[2] - ex[4] - ey[5]),
        half * (ex[0] + ey[1]) - (0.2 * STEP) * around[2] + (0.8 * STEP - MOVE) * core[2],
        carried[3] + rl * core[3] - half * ex[0],
        carried[4] + rl * core[4] - (0.5 * half) * (ey[0] + ex[1]),
        carried[5] + rl * core[5] - half * ey[1],
    ]


def steps(mats, exts, slabs, flow, sflow, td, std, merged, outs):
    north, south, _, _ = masks()
    side_ok = side_masks((8, 128))
    lane = lanes((8, 128))

    def timed(f, a, b):
        x = jnp.concatenate([a, b], 1)
        high = x.astype(jnp.bfloat16).astype(jnp.float32)
        both = jnp.concatenate([high, x - high], 0).astype(jnp.bfloat16)
        out = jnp.dot(mats[0 if f < 2 else 1], both, preferred_element_type=jnp.float32)
        out = out[:TP] + out[TP:]
        return out[:, :128], out[:, 128:]

    for k in range(H):
        src, dst = exts[k % 2], exts[1 - k % 2]
        side, side_new = slabs[k % 2], slabs[1 - k % 2]
        low, count = k + 1, E - 2 * (k + 1)
        last = k == H - 1

        def time_pair(r, src=src):
            for n, f in enumerate(TIMED):
                td[n, r], td[n, r + 1] = timed(f, src[f, r], src[f, r + 1])

        def main_pair(r, src=src, dst=dst):
            for c in range(TP // 8):
                s = pl.ds(8 * c, 8)
                rows = [[src[f, r + e, s] for f in range(F)] for e in (-1, 0, 1, 2)]
                beside = [merged[f, s] for f in range(F)]
                for e in range(2):
                    xm, core, xp = rows[e : e + 3]
                    edge = [pltpu.roll(a, 125 - 8 * (r + e), 1) for a in beside]
                    ym = [jnp.where(lane == 0, b, pltpu.roll(a, 1, 1)) for a, b in zip(core, edge)]
                    yp = [jnp.where(lane == 127, b, pltpu.roll(a, 127, 1)) for a, b in zip(core, edge)]
                    rl = jnp.broadcast_to(flow[0, r + e, pl.ds(T, 1)], (8, 128))
                    times = {f: td[n, r + e, s] for n, f in enumerate(TIMED)}
                    out = combine(core, xm, xp, ym, yp, flow[0, r + e, s], flow[1, r + e, s], rl, times)
                    for f in range(F):
                        inside = H <= r + e < H + R
                        dst[f, r + e, s] = out[f] if inside else out[f] * (north if r + e < H else south)

        for f in range(F):
            merged[f] = jnp.where(lanes() % 8 == 3, side[f, 0], pltpu.roll(side[f, 1], 126, 1))
        if not last:
            for n, f in enumerate(TIMED):
                std[n, 0], std[n, 1] = timed(f, side[f, 0], side[f, 1])
        time_pair(low)
        for i in range(count // 2):
            if i + 1 < count // 2:
                time_pair(low + 2 * i + 2)
            main_pair(low + 2 * i)
        for p in range(0 if last else 2):
            for c in range(TP // 8):
                s = pl.ds(8 * c, 8)
                core = [side[f, p, s] for f in range(F)]
                xm, xp, ym, yp = ([pltpu.roll(a, by, 1) for a in core] for by in (8, 120, 1, 127))
                rl = jnp.broadcast_to(sflow[0, p, pl.ds(T, 1)], (8, 128))
                times = {f: std[n, p, s] for n, f in enumerate(TIMED)}
                out = combine(core, xm, xp, ym, yp, sflow[0, p, s], sflow[1, p, s], rl, times)
                for f in range(F):
                    side_new[f, p, s] = out[f] * side_ok[p]
        for f in range(F):
            for r in range(R):
                outs[k][pl.ds(f * T * R + r, T, stride=R), :] = dst[f, H + r, 0:T]


def by_parity(load, *pairs):
    @pl.when(is_odd())
    def _():
        load(*[pair[0] for pair in pairs], *[pair[1] for pair in pairs])

    @pl.when(jnp.logical_not(is_odd()))
    def _():
        load(*[pair[1] for pair in pairs], *[pair[0] for pair in pairs])


def first_kernel(own, own_pack, even, odd, here, near_even, near_odd, mats, main, pack, older, flow, sflow, ext0, ext1, side0, side1, td, std, merged):
    half = 0.5 * STEP

    def load(north, flow_north, south, flow_south):
        sides = [slabs_of(ref) for ref in (flow_north, here, flow_south)]
        fill(own, own_pack, north, south, sides, ext0, side0)
        for j in range(2):
            for r in range(R):
                put(flow, (j, H + r), raw(own, F + j, r), half)
            for q in range(H - 1):
                place = pl.ds(SIDE + (j * (H - 1) + q) * T, T)
                put(flow, (j, 1 + q), flow_north[place, :], half)
                put(flow, (j, H + R + q), flow_south[place, :], half)
        for r in range(R):
            flow[0, H + r, pl.ds(T, 1), :] = own[pl.ds(8 * T * R + r, 1), :] * STEP
        for q in range(H - 1):
            place = pl.ds(SIDE + 2 * (H - 1) * T + q, 1)
            flow[0, 1 + q, pl.ds(T, 1), :] = flow_north[place, :] * STEP
            flow[0, H + R + q, pl.ds(T, 1), :] = flow_south[place, :] * STEP
        sub = lax.broadcasted_iota(jnp.int32, (TP, 128), 0)
        scale = jnp.where(sub == T, STEP, half).astype(jnp.float32)
        slot = lanes() % 8
        for j in range(2):
            sides_of(sflow, j, own_windows(lambda e: flow[j, e], own_pack, F + j, scale), sides, 1, 2 + j, (1.0, 1.0))
            for p in range(2):
                halo = (slot < 4) if p == 0 else (slot >= 4)
                sflow[j, p] = sflow[j, p] * jnp.where(halo, scale, 1.0)

    by_parity(load, (even, odd), (near_even, near_odd))
    older[0] = own[0:ROWS, :]
    outs = [older.at[k] for k in (1, 2, 3)] + [main]
    steps(mats, (ext0, ext1), (side0, side1), flow, sflow, td, std, merged, outs)
    for g in range(2):
        total = jnp.zeros((TP, 128), jnp.float32)
        for j in range(4 if g == 0 else 2):
            for r in range(R):
                total = total + window(ext0[g * 4 + j, H + r], j * 32 + r * 8)
        pack[g * TP : (g + 1) * TP, :] = total


def products(vectors, pairs):
    def part(i, sums):
        sums = list(sums)
        for c in range(9):
            s = pl.ds(pl.multiple_of(72 * i, 8) + 8 * c, 8)
            vec = {k: get(s) for k, get in vectors.items()}
            for e, (a, b) in enumerate(pairs):
                sums[e] = sums[e] + vec[a] * vec[b]
        return tuple(sums)

    zero = jnp.zeros((8, 128), jnp.float32)
    return lax.fori_loop(0, ROWS // 72, part, (zero,) * len(pairs))


def early_vectors(older, main):
    vectors = {k: lambda s, k=k: older[k, s] for k in range(H)}
    vectors[H] = lambda s: main[s]
    return vectors


def gram_kernel(older, main, early):
    for e, value in enumerate(products(early_vectors(older, main), EARLY)):
        early[e] = value


def second_kernel(own, own_pack, even, odd, here, corner_even, corner_odd, flow, sflow, older, early, mats, newer, gram, ext0, ext1, side0, side1, td, std, merged, rows):

    def load(north, above, south, below):
        fill(own, own_pack, north, south, [slabs_of(ref) for ref in (above, here, below)], ext0, side0)

    by_parity(load, (even, odd), (corner_even, corner_odd))
    outs = [newer.at[k] for k in range(4)]
    steps(mats, (ext0, ext1), (side0, side1), flow, sflow, td, std, merged, outs)

    late = [pair for pair in PAIRS if pair not in EARLY]
    vectors = early_vectors(older, own)
    for k in range(4):
        vectors[5 + k] = lambda s, k=k: newer[k, s]
    sums = dict(zip(late, products(vectors, late)))
    for e, pair in enumerate(EARLY):
        sums[pair] = early[e]
    rows[...] = jnp.zeros((48, 128), jnp.float32)
    for e, pair in enumerate(PAIRS):
        rows[pl.ds(e, 1), :] = jnp.sum(sums[pair], axis=0, keepdims=True)
    total = jnp.sum(rows[...], axis=1, keepdims=True)
    pick = lanes((48, 128)) == lax.broadcasted_iota(jnp.int32, (48, 128), 0)
    line = jnp.sum(jnp.where(pick, total, 0.0), axis=0, keepdims=True)
    gram[...] = jnp.broadcast_to(line, (PEERS, 128))


def plus(a, b):
    return b if a is None else a if b is None else a + b


def minus(a, b):
    return a if b is None else -b if a is None else a - b


def times(a, b):
    return None if a is None or b is None else a * b


def cycle(gram, c):
    q = [c]
    for _ in range(4):
        q.append([None] + q[-1][:-1])
    w = [
        [plus(times(2.0 + 3.0 * SHIFT, a), times(3.0 / SCALE, b)) for a, b in zip(q[k], q[k + 1])]
        for k in range(4)
    ]

    def dot(a, b):
        total = None
        for x, y in zip(a, b):
            total = plus(total, times(x, y))
        return total

    gw = [[dot(gram[i], v) for i in range(NV)] for v in w]
    n = 4
    y = [dot(c, gw[i]) for i in range(n)]
    low, inverse = [[None] * n for _ in range(n)], []
    for j in range(n):
        held = [dot(w[i], gw[j]) for i in range(j, n)]
        for m in range(j):
            scaled = low[j][m] * diag[m]
            held = [v - low[i][m] * scaled for i, v in zip(range(j, n), held)]
        diag = (diag if j else []) + [held[0]]
        inverse.append(1.0 / held[0])
        low[j][j] = 1.0
        for i in range(j + 1, n):
            low[i][j] = held[i - j] * inverse[j]
    for i in range(n):
        for m in range(i):
            y[i] = y[i] - low[i][m] * y[m]
    y = [a * b for a, b in zip(y, inverse)]
    for i in reversed(range(n)):
        for m in range(i + 1, n):
            y[i] = y[i] - low[m][i] * y[m]
    step, rest = [None] * NV, list(c)
    for i in range(n):
        step = [plus(a, times(y[i], b)) for a, b in zip(step, q[i])]
        rest = [minus(a, times(y[i], b)) for a, b in zip(rest, w[i])]
    return step, rest


def last_kernel(parts, older, main, newer, solution, residual, sol, res, sems):
    total = jnp.sum(parts[...].reshape(PEERS // 8, 8, 128), axis=0)
    total = jnp.sum(total, axis=0, keepdims=True)
    gram = [[None] * NV for _ in range(NV)]
    for e, (i, j) in enumerate(PAIRS):
        gram[i][j] = gram[j][i] = jnp.broadcast_to(total[:, e : e + 1], (8, 128))
    step1, rest = cycle(gram, [1.0] + [None] * (NV - 1))
    zero = jnp.zeros((8, 128), jnp.float32)
    rest = [zero if a is None else a for a in rest]
    step2, rest = cycle(gram, rest)
    step = [plus(a, b) for a, b in zip(step1, step2)]
    vectors = early_vectors(older, main)
    for k in range(4):
        vectors[5 + k] = lambda s, k=k: newer[k, s]
    copies = []
    third = ROWS // 3
    for p in range(3):

        def part(i, carry, p=p):
            for c in range(11):
                s = pl.ds(pl.multiple_of(p * third + 88 * i, 8) + 8 * c, 8)
                one = two = None
                for k in range(NV):
                    x = vectors[k](s)
                    one = plus(one, times(step[k], x))
                    two = plus(two, rest[k] * x)
                sol[s, :] = one
                res[s, :] = two
            return carry

        lax.fori_loop(0, third // 88, part, 0)
        for n, (src, dst) in enumerate(((sol, solution), (res, residual))):
            s = pl.ds(p * third, third)
            copies.append(pltpu.make_async_copy(src.at[s], dst.at[s], sems.at[2 * p + n]))
            copies[-1].start()
    for copy in copies:
        copy.wait()


def call(kernel, args, outs, scratch=(), first=False, final=False):
    space = pltpu.HBM if first else pltpu.VMEM
    args = [pltpu.with_memory_space_constraint(a, space) for a in args]
    make = pltpu.HBM if final else pltpu.VMEM
    kinds = [jnp.bfloat16 if shape[-1] == 2 * TP else jnp.float32 for shape in outs]
    scratch = [pltpu.VMEM(shape, jnp.float32) for shape in scratch]
    return pl.pallas_call(
        kernel,
        out_shape=[make(shape, kind) for shape, kind in zip(outs, kinds)],
        in_specs=[pl.BlockSpec(memory_space=space)] * len(args),
        out_specs=[pl.BlockSpec(memory_space=make)] * len(outs),
        scratch_shapes=scratch + [pltpu.SemaphoreType.DMA((6,))] * (first or final),
        compiler_params=pltpu.CompilerParams(vmem_limit_bytes=24 << 20),
    )(*args)


def trades(across, down):
    even = [(g * down + j, g * down + (j ^ 1)) for g in range(across) for j in range(down)]
    odd = []
    for g in range(across):
        for j in range(down):
            edge = j in (0, down - 1)
            other = j if edge else j + 1 if j % 2 else j - 1
            odd.append((g * down + j, (g ^ 1 if edge else g) * down + other))
    return even, odd


def exchange(rows, pack, behind=()):
    across = lax.axis_size("gx")
    pairs = trades(across, lax.axis_size("gy"))
    axes = ("gx", "gy")
    rows = [lax.ppermute(rows, axes, p) for p in pairs]
    ones = lax.ppermute(pack, "gx", [(g, g ^ 1) for g in range(across)])
    others = lax.ppermute(pack, "gx", [(g, (g + (1 if g % 2 else -1)) % across) for g in range(across)])
    slot = lax.broadcasted_iota(jnp.int32, pack.shape, 1) % 8
    here = jnp.where((slot < 4) == (lax.axis_index("gx") % 2 == 1), ones, others)
    near = [x.at[:SIDE].set(here) for x in behind] or [here, here]
    corners = [lax.ppermute(x, axes, p) for x, p in zip(near, pairs)]
    return *rows, here, *corners


WORK = (
    (F, E, TP, 128),
    (F, E, TP, 128),
    (F, 2, TP, 128),
    (F, 2, TP, 128),
    (len(TIMED), E, TP, 128),
    (len(TIMED), 2, TP, 128),
    (F, TP, 128),
)


def shards(right_side, base_flow, relax):
    rs = right_side.reshape(F * T * R, 128)
    flow = base_flow.reshape(2 * T * R, 128)
    own, to_even, to_odd, pack, mats = call(
        pack_kernel,
        (rs, flow, relax, jnp.asarray(time_matrices())),
        ((8 * T * R + 8, 128), (SIDE + FLOW, 128), (SIDE + FLOW, 128), (SIDE, 128), (2, 2 * TP, 2 * TP)),
        first=True,
    )
    main, pack, older, flows, side_flows = call(
        first_kernel,
        (own, pack, *exchange(rs, pack, (to_even, to_odd)), mats),
        ((ROWS, 128), (SIDE, 128), (H, ROWS, 128), (2, E, TP, 128), (2, 2, TP, 128)),
        WORK,
    )
    (early,) = call(gram_kernel, (older, main), ((len(EARLY), 8, 128),))
    newer, gram = call(
        second_kernel,
        (main, pack, *exchange(main, pack), flows, side_flows, older, early, mats),
        ((4, ROWS, 128), (PEERS, 128)),
        WORK + ((48, 128),),
    )
    parts = lax.all_to_all(gram.reshape(PEERS, 1, 128), ("gx", "gy"), 0, 0, tiled=True)
    solution_field, residual = call(
        last_kernel,
        (parts.reshape(PEERS, 128), older, main, newer),
        ((ROWS, 128), (ROWS, 128)),
        ((ROWS, 128), (ROWS, 128)),
        final=True,
    )
    return solution_field.reshape(right_side.shape), residual.reshape(right_side.shape)


def solution(mesh):
    placed = (P(None, None, "gy", "gx"), P(None, None, "gy", "gx"), P("gy", "gx"))
    return jax.shard_map(
        shards,
        mesh=mesh,
        in_specs=placed,
        out_specs=(P(None, None, "gy", "gx"), P(None, None, "gy", "gx")),
        check_vma=False,
    )
```

```python
import jax
import jax.numpy as jnp
import numpy as np
from jax import lax
from jax.experimental import pallas as pl
from jax.experimental.pallas import tpu as pltpu
from jax.sharding import PartitionSpec as P

F = 6
T = 33
TP = 40
R = 4
H = 4
E = R + 2 * H
NV = 9
SHIFT = 0.5
SCALE = 0.46
STEP = SCALE / 3.0
MOVE = SCALE * SHIFT
TIMED = (0, 1, 3, 4, 5)
PAIRS = [(i, j) for i in range(NV) for j in range(i, NV)]
EARLY = [(i, j) for i, j in PAIRS if j < 5]
PEERS = 256
ROWS = F * T * R
SIDE = 2 * TP
FLOW = 208


def time_matrices():
    index = np.arange(T, dtype=np.float64)
    diff = index[:, None] - index[None, :]
    sines = np.where(diff == 0.0, 1.0, np.sin(np.pi * diff / T))
    dmat = np.where(diff == 0.0, 0.0, 0.5 * np.where(diff % 2 == 0, 1.0, -1.0) / sines)
    mats = []
    for diagonal in (0.4 * STEP - MOVE, -MOVE):
        full = np.zeros((TP, TP), np.float32)
        full[:T, :T] = 0.8 * STEP * dmat + diagonal * np.eye(T)
        high = full.astype(jnp.bfloat16)
        low = (full - high.astype(np.float32)).astype(jnp.bfloat16)
        top = np.concatenate([high, high], 1)
        bottom = np.concatenate([low, np.zeros_like(low)], 1)
        mats.append(np.concatenate([top, bottom], 0))
    return np.stack(mats)


def lanes(shape=(1, 128)):
    return lax.broadcasted_iota(jnp.int32, shape, len(shape) - 1)


def turned(x, by):
    return pltpu.roll(x, by % 128, 1) if by % 128 else x


def window(x, place):
    lane = lanes()
    return jnp.where((lane >= place) & (lane < place + 8), pltpu.roll(x, (place + 4) % 128, 1), 0.0)


def raw(ref, f, r):
    return ref[pl.ds(f * T * R + r, T, stride=R), :]


def is_odd():
    return lax.rem(lax.axis_index("gy"), 2) == 1


def pack_kernel(rs, flow, relax, mats_in, message, even, odd, pack, mats, sems):
    rows = F * T * R
    copies = [
        pltpu.make_async_copy(rs, message.at[pl.ds(0, rows)], sems.at[0]),
        pltpu.make_async_copy(flow, message.at[pl.ds(rows, 2 * T * R)], sems.at[1]),
        pltpu.make_async_copy(relax, message.at[pl.ds(8 * T * R, R)], sems.at[2]),
        pltpu.make_async_copy(mats_in, mats, sems.at[3]),
    ]
    for copy in copies:
        copy.start()
    for copy in copies:
        copy.wait()
    for to in (even, odd):
        to[pl.ds(SIDE + FLOW - 8, 8), :] = jnp.zeros((8, 128), jnp.float32)
    for g in range(2):
        total = jnp.zeros((T, 128), jnp.float32)
        for j in range(4):
            for r in range(R):
                total = total + window(raw(message, g * 4 + j, r), j * 32 + r * 8)
        pack[g * TP : g * TP + 32, :] = total[0:32]
        last = jnp.zeros((8, 128), jnp.float32)
        sub = lax.broadcasted_iota(jnp.int32, (8, 128), 0)
        last = jnp.where(sub == 0, jnp.broadcast_to(total[32:33], (8, 128)), last)
        if g == 1:
            extra = jnp.zeros((1, 128), jnp.float32)
            for r in range(R):
                extra = extra + window(message[pl.ds(8 * T * R + r, 1), :], 2 * 32 + r * 8)
            last = jnp.where(sub == 1, jnp.broadcast_to(extra, (8, 128)), last)
        pack[g * TP + 32 : g * TP + 40, :] = last

    def rows_for(to, first):
        for j in range(2):
            for q in range(H - 1):
                to[pl.ds(SIDE + (j * (H - 1) + q) * T, T), :] = raw(message, F + j, first + q)
        for q in range(H - 1):
            to[pl.ds(SIDE + 2 * (H - 1) * T + q, 1), :] = message[pl.ds(8 * T * R + first + q, 1), :]

    @pl.when(is_odd())
    def _():
        rows_for(even, 0)
        rows_for(odd, 1)

    @pl.when(jnp.logical_not(is_odd()))
    def _():
        rows_for(even, 1)
        rows_for(odd, 0)


def put(dst, index, x, scale=None):
    dst[index + (pl.ds(32, 8), slice(None))] = jnp.zeros((8, 128), jnp.float32)
    dst[index + (pl.ds(0, T), slice(None))] = x if scale is None else x * scale


def slabs_of(ref):
    return [ref.at[pl.ds(g * TP, TP)] for g in range(2)]


def sides_of(dst, f, own, sides, g, j, ok):
    lane = lanes()
    north, here, south = (
        turned(ref[g][...], base - 32 * j) for base, ref in zip((0, 32, 64), sides)
    )
    halo = jnp.where(lane < 32, north, jnp.where(lane < 64, here, south))
    slot = lane % 8
    dst[f, 0] = jnp.where(slot < 4, halo, own) * ok[0]
    dst[f, 1] = jnp.where(slot < 4, own, halo) * ok[1]


def own_windows(slab, pack, f, scale=None):
    lane = lanes()
    here = turned(pack[pl.ds(f // 4 * TP, TP)], 8 * H - 32 * (f % 4))
    total = jnp.where((lane >= 8 * H) & (lane < 8 * (H + R)), here if scale is None else here * scale, 0.0)
    for e in range(1, E - 1):
        if not H <= e < H + R:
            total = total + window(slab(e), e * 8)
    return total


def fill(own, pack, north, south, sides, ext, side):
    ok_north, ok_south, _, _ = masks()
    ok = side_masks((1, 128))
    for f in range(F):
        for r in range(R):
            put(ext, (f, r), raw(north, f, r), ok_north)
            put(ext, (f, H + r), raw(own, f, r))
            put(ext, (f, H + R + r), raw(south, f, r), ok_south)
    for f in range(F):
        sides_of(side, f, own_windows(lambda e: ext[f, e], pack, f), sides, f // 4, f % 4, ok)


def masks():
    gx, gy = lax.axis_index("gx"), lax.axis_index("gy")
    north = jnp.where(gy > 0, 1.0, 0.0).astype(jnp.float32)
    south = jnp.where(gy < lax.axis_size("gy") - 1, 1.0, 0.0).astype(jnp.float32)
    west = jnp.where(gx > 0, 1.0, 0.0).astype(jnp.float32)
    east = jnp.where(gx < lax.axis_size("gx") - 1, 1.0, 0.0).astype(jnp.float32)
    return north, south, west, east


def side_masks(shape):
    north, south, west, east = masks()
    lane = lanes(shape)
    row, slot = lane // 8, lane % 8
    rows_ok = jnp.where(row < H, north, jnp.where(row < H + R, 1.0, jnp.where(row < E, south, 0.0)))
    return [rows_ok * jnp.where(slot < 4, west, 1.0), rows_ok * jnp.where(slot < 4, 1.0, east)]


def combine(core, xm, xp, ym, yp, fu, fv, rl, td):
    ex = [a - b for a, b in zip(xp, xm)]
    ey = [a - b for a, b in zip(yp, ym)]
    half = 0.5 * STEP
    carried = {f: td[f] + fu * ex[f] + fv * ey[f] for f in TIMED}
    around = [xp[f] + xm[f] + (yp[f] + ym[f]) for f in range(3)]
    return [
        carried[0] - (0.1 * STEP) * around[0] + half * (ex[2] - ex[3] - ey[4]),
        carried[1] - (0.1 * STEP) * around[1] + half * (ey[2] - ex[4] - ey[5]),
        half * (ex[0] + ey[1]) - (0.2 * STEP) * around[2] + (0.8 * STEP - MOVE) * core[2],
        carried[3] + rl * core[3] - half * ex[0],
        carried[4] + rl * core[4] - (0.5 * half) * (ey[0] + ex[1]),
        carried[5] + rl * core[5] - half * ey[1],
    ]


def steps(mats, exts, slabs, flow, sflow, td, std, merged, outs):
    north, south, _, _ = masks()
    side_ok = side_masks((8, 128))
    lane = lanes((8, 128))

    def timed(f, a, b):
        x = jnp.concatenate([a, b], 1)
        high = x.astype(jnp.bfloat16).astype(jnp.float32)
        both = jnp.concatenate([high, x - high], 0).astype(jnp.bfloat16)
        out = jnp.dot(mats[0 if f < 2 else 1], both, preferred_element_type=jnp.float32)
        out = out[:TP] + out[TP:]
        return out[:, :128], out[:, 128:]

    for k in range(H):
        src, dst = exts[k % 2], exts[1 - k % 2]
        side, side_new = slabs[k % 2], slabs[1 - k % 2]
        low, count = k + 1, E - 2 * (k + 1)
        last = k == H - 1

        def time_pair(r, src=src):
            for n, f in enumerate(TIMED):
                td[n, r], td[n, r + 1] = timed(f, src[f, r], src[f, r + 1])

        def main_pair(r, src=src, dst=dst):
            for c in range(TP // 8):
                s = pl.ds(8 * c, 8)
                rows = [[src[f, r + e, s] for f in range(F)] for e in (-1, 0, 1, 2)]
                beside = [merged[f, s] for f in range(F)]
                for e in range(2):
                    xm, core, xp = rows[e : e + 3]
                    edge = [pltpu.roll(a, 125 - 8 * (r + e), 1) for a in beside]
                    ym = [jnp.where(lane == 0, b, pltpu.roll(a, 1, 1)) for a, b in zip(core, edge)]
                    yp = [jnp.where(lane == 127, b, pltpu.roll(a, 127, 1)) for a, b in zip(core, edge)]
                    rl = jnp.broadcast_to(flow[0, r + e, pl.ds(T, 1)], (8, 128))
                    times = {f: td[n, r + e, s] for n, f in enumerate(TIMED)}
                    out = combine(core, xm, xp, ym, yp, flow[0, r + e, s], flow[1, r + e, s], rl, times)
                    for f in range(F):
                        inside = H <= r + e < H + R
                        dst[f, r + e, s] = out[f] if inside else out[f] * (north if r + e < H else south)

        for f in range(F):
            merged[f] = jnp.where(lanes() % 8 == 3, side[f, 0], pltpu.roll(side[f, 1], 126, 1))
        if not last:
            for n, f in enumerate(TIMED):
                std[n, 0], std[n, 1] = timed(f, side[f, 0], side[f, 1])
        time_pair(low)
        for i in range(count // 2):
            if i + 1 < count // 2:
                time_pair(low + 2 * i + 2)
            main_pair(low + 2 * i)
        for p in range(0 if last else 2):
            for c in range(TP // 8):
                s = pl.ds(8 * c, 8)
                core = [side[f, p, s] for f in range(F)]
                xm, xp, ym, yp = ([pltpu.roll(a, by, 1) for a in core] for by in (8, 120, 1, 127))
                rl = jnp.broadcast_to(sflow[0, p, pl.ds(T, 1)], (8, 128))
                times = {f: std[n, p, s] for n, f in enumerate(TIMED)}
                out = combine(core, xm, xp, ym, yp, sflow[0, p, s], sflow[1, p, s], rl, times)
                for f in range(F):
                    side_new[f, p, s] = out[f] * side_ok[p]
        for f in range(F):
            for r in range(R):
                outs[k][pl.ds(f * T * R + r, T, stride=R), :] = dst[f, H + r, 0:T]


def by_parity(load, *pairs):
    @pl.when(is_odd())
    def _():
        load(*[pair[0] for pair in pairs], *[pair[1] for pair in pairs])

    @pl.when(jnp.logical_not(is_odd()))
    def _():
        load(*[pair[1] for pair in pairs], *[pair[0] for pair in pairs])


def first_kernel(own, own_pack, even, odd, here, near_even, near_odd, mats, main, pack, older, flow, sflow, ext0, ext1, side0, side1, td, std, merged):
    half = 0.5 * STEP

    def load(north, flow_north, south, flow_south):
        sides = [slabs_of(ref) for ref in (flow_north, here, flow_south)]
        fill(own, own_pack, north, south, sides, ext0, side0)
        for j in range(2):
            for r in range(R):
                put(flow, (j, H + r), raw(own, F + j, r), half)
            for q in range(H - 1):
                place = pl.ds(SIDE + (j * (H - 1) + q) * T, T)
                put(flow, (j, 1 + q), flow_north[place, :], half)
                put(flow, (j, H + R + q), flow_south[place, :], half)
        for r in range(R):
            flow[0, H + r, pl.ds(T, 1), :] = own[pl.ds(8 * T * R + r, 1), :] * STEP
        for q in range(H - 1):
            place = pl.ds(SIDE + 2 * (H - 1) * T + q, 1)
            flow[0, 1 + q, pl.ds(T, 1), :] = flow_north[place, :] * STEP
            flow[0, H + R + q, pl.ds(T, 1), :] = flow_south[place, :] * STEP
        sub = lax.broadcasted_iota(jnp.int32, (TP, 128), 0)
        scale = jnp.where(sub == T, STEP, half).astype(jnp.float32)
        slot = lanes() % 8
        for j in range(2):
            sides_of(sflow, j, own_windows(lambda e: flow[j, e], own_pack, F + j, scale), sides, 1, 2 + j, (1.0, 1.0))
            for p in range(2):
                halo = (slot < 4) if p == 0 else (slot >= 4)
                sflow[j, p] = sflow[j, p] * jnp.where(halo, scale, 1.0)

    by_parity(load, (even, odd), (near_even, near_odd))
    older[0] = own[0:ROWS, :]
    outs = [older.at[k] for k in (1, 2, 3)] + [main]
    steps(mats, (ext0, ext1), (side0, side1), flow, sflow, td, std, merged, outs)
    for g in range(2):
        total = jnp.zeros((TP, 128), jnp.float32)
        for j in range(4 if g == 0 else 2):
            for r in range(R):
                total = total + window(ext0[g * 4 + j, H + r], j * 32 + r * 8)
        pack[g * TP : (g + 1) * TP, :] = total


def products(vectors, pairs):
    def part(i, sums):
        sums = list(sums)
        for c in range(9):
            s = pl.ds(pl.multiple_of(72 * i, 8) + 8 * c, 8)
            vec = {k: get(s) for k, get in vectors.items()}
            for e, (a, b) in enumerate(pairs):
                sums[e] = sums[e] + vec[a] * vec[b]
        return tuple(sums)

    zero = jnp.zeros((8, 128), jnp.float32)
    return lax.fori_loop(0, ROWS // 72, part, (zero,) * len(pairs))


def early_vectors(older, main):
    vectors = {k: lambda s, k=k: older[k, s] for k in range(H)}
    vectors[H] = lambda s: main[s]
    return vectors


def gram_kernel(older, main, early):
    for e, value in enumerate(products(early_vectors(older, main), EARLY)):
        early[e] = value


def second_kernel(own, own_pack, even, odd, here, corner_even, corner_odd, flow, sflow, older, early, mats, newer, gram, ext0, ext1, side0, side1, td, std, merged, rows):

    def load(north, above, south, below):
        fill(own, own_pack, north, south, [slabs_of(ref) for ref in (above, here, below)], ext0, side0)

    by_parity(load, (even, odd), (corner_even, corner_odd))
    outs = [newer.at[k] for k in range(4)]
    steps(mats, (ext0, ext1), (side0, side1), flow, sflow, td, std, merged, outs)

    late = [pair for pair in PAIRS if pair not in EARLY]
    vectors = early_vectors(older, own)
    for k in range(4):
        vectors[5 + k] = lambda s, k=k: newer[k, s]
    sums = dict(zip(late, products(vectors, late)))
    for e, pair in enumerate(EARLY):
        sums[pair] = early[e]
    rows[...] = jnp.zeros((48, 128), jnp.float32)
    for e, pair in enumerate(PAIRS):
        rows[pl.ds(e, 1), :] = jnp.sum(sums[pair], axis=0, keepdims=True)
    total = jnp.sum(rows[...], axis=1, keepdims=True)
    pick = lanes((48, 128)) == lax.broadcasted_iota(jnp.int32, (48, 128), 0)
    line = jnp.sum(jnp.where(pick, total, 0.0), axis=0, keepdims=True)
    gram[...] = jnp.broadcast_to(line, (PEERS, 128))


def plus(a, b):
    return b if a is None else a if b is None else a + b


def minus(a, b):
    return a if b is None else -b if a is None else a - b


def times(a, b):
    return None if a is None or b is None else a * b


def cycle(gram, c):
    q = [c]
    for _ in range(4):
        q.append([None] + q[-1][:-1])
    w = [
        [plus(times(2.0 + 3.0 * SHIFT, a), times(3.0 / SCALE, b)) for a, b in zip(q[k], q[k + 1])]
        for k in range(4)
    ]

    def dot(a, b):
        total = None
        for x, y in zip(a, b):
            total = plus(total, times(x, y))
        return total

    gw = [[dot(gram[i], v) for i in range(NV)] for v in w]
    n = 4
    y = [dot(c, gw[i]) for i in range(n)]
    low, inverse = [[None] * n for _ in range(n)], []
    for j in range(n):
        held = [dot(w[i], gw[j]) for i in range(j, n)]
        for m in range(j):
            scaled = low[j][m] * diag[m]
            held = [v - low[i][m] * scaled for i, v in zip(range(j, n), held)]
        diag = (diag if j else []) + [held[0]]
        inverse.append(1.0 / held[0])
        low[j][j] = 1.0
        for i in range(j + 1, n):
            low[i][j] = held[i - j] * inverse[j]
    for i in range(n):
        for m in range(i):
            y[i] = y[i] - low[i][m] * y[m]
    y = [a * b for a, b in zip(y, inverse)]
    for i in reversed(range(n)):
        for m in range(i + 1, n):
            y[i] = y[i] - low[m][i] * y[m]
    step, rest = [None] * NV, list(c)
    for i in range(n):
        step = [plus(a, times(y[i], b)) for a, b in zip(step, q[i])]
        rest = [minus(a, times(y[i], b)) for a, b in zip(rest, w[i])]
    return step, rest


def last_kernel(parts, older, main, newer, solution, residual, sol, res, sems):
    total = jnp.sum(parts[...].reshape(PEERS // 8, 8, 128), axis=0)
    total = jnp.sum(total, axis=0, keepdims=True)
    gram = [[None] * NV for _ in range(NV)]
    for e, (i, j) in enumerate(PAIRS):
        gram[i][j] = gram[j][i] = jnp.broadcast_to(total[:, e : e + 1], (8, 128))
    step1, rest = cycle(gram, [1.0] + [None] * (NV - 1))
    zero = jnp.zeros((8, 128), jnp.float32)
    rest = [zero if a is None else a for a in rest]
    step2, rest = cycle(gram, rest)
    step = [plus(a, b) for a, b in zip(step1, step2)]
    vectors = early_vectors(older, main)
    for k in range(4):
        vectors[5 + k] = lambda s, k=k: newer[k, s]
    copies = []
    third = ROWS // 3
    for p in range(3):

        def part(i, carry, p=p):
            for c in range(11):
                s = pl.ds(pl.multiple_of(p * third + 88 * i, 8) + 8 * c, 8)
                one = two = None
                for k in range(NV):
                    x = vectors[k](s)
                    one = plus(one, times(step[k], x))
                    two = plus(two, rest[k] * x)
                sol[s, :] = one
                res[s, :] = two
            return carry

        lax.fori_loop(0, third // 88, part, 0)
        for n, (src, dst) in enumerate(((sol, solution), (res, residual))):
            s = pl.ds(p * third, third)
            copies.append(pltpu.make_async_copy(src.at[s], dst.at[s], sems.at[2 * p + n]))
            copies[-1].start()
    for copy in copies:
        copy.wait()


def call(kernel, args, outs, scratch=(), first=False, final=False):
    space = pltpu.HBM if first else pltpu.VMEM
    args = [pltpu.with_memory_space_constraint(a, space) for a in args]
    make = pltpu.HBM if final else pltpu.VMEM
    kinds = [jnp.bfloat16 if shape[-1] == 2 * TP else jnp.float32 for shape in outs]
    scratch = [pltpu.VMEM(shape, jnp.float32) for shape in scratch]
    return pl.pallas_call(
        kernel,
        out_shape=[make(shape, kind) for shape, kind in zip(outs, kinds)],
        in_specs=[pl.BlockSpec(memory_space=space)] * len(args),
        out_specs=[pl.BlockSpec(memory_space=make)] * len(outs),
        scratch_shapes=scratch + [pltpu.SemaphoreType.DMA((6,))] * (first or final),
        compiler_params=pltpu.CompilerParams(vmem_limit_bytes=24 << 20),
    )(*args)


def trades(across, down):
    even = [(g * down + j, g * down + (j ^ 1)) for g in range(across) for j in range(down)]
    odd = []
    for g in range(across):
        for j in range(down):
            edge = j in (0, down - 1)
            other = j if edge else j + 1 if j % 2 else j - 1
            odd.append((g * down + j, (g ^ 1 if edge else g) * down + other))
    return even, odd


def exchange(rows, pack, behind=()):
    across = lax.axis_size("gx")
    pairs = trades(across, lax.axis_size("gy"))
    axes = ("gx", "gy")
    rows = [lax.ppermute(rows, axes, p) for p in pairs]
    ones = lax.ppermute(pack, "gx", [(g, g ^ 1) for g in range(across)])
    others = lax.ppermute(pack, "gx", [(g, (g + (1 if g % 2 else -1)) % across) for g in range(across)])
    slot = lax.broadcasted_iota(jnp.int32, pack.shape, 1) % 8
    here = jnp.where((slot < 4) == (lax.axis_index("gx") % 2 == 1), ones, others)
    near = [x.at[:SIDE].set(here) for x in behind] or [here, here]
    corners = [lax.ppermute(x, axes, p) for x, p in zip(near, pairs)]
    return *rows, here, *corners


WORK = (
    (F, E, TP, 128),
    (F, E, TP, 128),
    (F, 2, TP, 128),
    (F, 2, TP, 128),
    (len(TIMED), E, TP, 128),
    (len(TIMED), 2, TP, 128),
    (F, TP, 128),
)


def shards(right_side, base_flow, relax):
    rs = right_side.reshape(F * T * R, 128)
    flow = base_flow.reshape(2 * T * R, 128)
    own, to_even, to_odd, pack, mats = call(
        pack_kernel,
        (rs, flow, relax, jnp.asarray(time_matrices())),
        ((8 * T * R + 8, 128), (SIDE + FLOW, 128), (SIDE + FLOW, 128), (SIDE, 128), (2, 2 * TP, 2 * TP)),
        first=True,
    )
    main, pack, older, flows, side_flows = call(
        first_kernel,
        (own, pack, *exchange(rs, pack, (to_even, to_odd)), mats),
        ((ROWS, 128), (SIDE, 128), (H, ROWS, 128), (2, E, TP, 128), (2, 2, TP, 128)),
        WORK,
    )
    (early,) = call(gram_kernel, (older, main), ((len(EARLY), 8, 128),))
    newer, gram = call(
        second_kernel,
        (main, pack, *exchange(main, pack), flows, side_flows, older, early, mats),
        ((4, ROWS, 128), (PEERS, 128)),
        WORK + ((48, 128),),
    )
    parts = lax.all_to_all(gram.reshape(PEERS, 1, 128), ("gx", "gy"), 0, 0, tiled=True)
    solution_field, residual = call(
        last_kernel,
        (parts.reshape(PEERS, 128), older, main, newer),
        ((ROWS, 128), (ROWS, 128)),
        ((ROWS, 128), (ROWS, 128)),
        final=True,
    )
    return solution_field.reshape(right_side.shape), residual.reshape(right_side.shape)


def solution(mesh):
    placed = (P(None, None, "gy", "gx"), P(None, None, "gy", "gx"), P("gy", "gx"))
    return jax.shard_map(
        shards,
        mesh=mesh,
        in_specs=placed,
        out_specs=(P(None, None, "gy", "gx"), P(None, None, "gy", "gx")),
        check_vma=False,
    )
```
